32 devices in a mesh: section: 2 (over core), dp: 16 (over z, y, x).
Axes of the slice: x: 2, y: 2, z: 4, core: 2. Of those that a mesh axis runs over, the one named last changes fastest.
Arguments:
- block_input: bfloat16 [6, 4096, 1280], P(None, 'dp'), may hold values from -6 to 6
- output_cotangent: bfloat16 [6, 4096, 1280], P(None, 'dp'), may hold values from -6 to 6
- residues_before: int32 [6, 4096], P(None, 'dp'), may hold values from 0 to 1023, as said below
- residues_after: int32 [6, 4096], P(None, 'dp'), may hold values from 0 to 1023, as said below
- residue_types: int32 [6, 4096], P(None, 'dp'), may hold values from 0 to 24
- loss_mask: int32 [6, 4096], P(None, 'dp'), may hold values from 0 to 1, as said below
- first_gain: float32 [2, 1280], P('section'), may hold values from 0.5 to 1.5
- first_shift: float32 [2, 1280], P('section'), may hold values from -3 to 3
- narrow_weight: bfloat16 [2, 1280, 640], P('section'), may hold values from -0.15625 to 0.15625
- narrow_bias: float32 [2, 640], P('section'), may hold values from -3 to 3
- middle_gain: float32 [2, 640], P('section'), may hold values from 0.5 to 1.5
- middle_shift: float32 [2, 640], P('section'), may hold values from -3 to 3
- conv_weight: bfloat16 [2, 5, 640, 640], P('section'), may hold values from -0.109375 to 0.109375
- conv_bias: float32 [2, 640], P('section'), may hold values from -3 to 3
- last_gain: float32 [2, 640], P('section'), may hold values from 0.5 to 1.5
- last_shift: float32 [2, 640], P('section'), may hold values from -3 to 3
- widen_weight: bfloat16 [2, 640, 1280], P('section'), may hold values from -0.3125 to 0.3125
- widen_bias: float32 [2, 1280], P('section'), may hold values from -3 to 3
- head_weight: bfloat16 [1280, 30], replicated, may hold values from -0.3125 to 0.3125
Outputs:
- block_outputs: bfloat16 [2, 6, 4096, 1280], P('section', None, 'dp')
- input_grads: bfloat16 [2, 6, 4096, 1280], P('section', None, 'dp')
- first_gain_grad: float32 [2, 1280], P('section')
- first_shift_grad: float32 [2, 1280], P('section')
- narrow_weight_grad: float32 [2, 1280, 640], P('section')
- narrow_bias_grad: float32 [2, 640], P('section')
- middle_gain_grad: float32 [2, 640], P('section')
- middle_shift_grad: float32 [2, 640], P('section')
- conv_weight_grad: float32 [2, 5, 640, 640], P('section')
- conv_bias_grad: float32 [2, 640], P('section')
- last_gain_grad: float32 [2, 640], P('section')
- last_shift_grad: float32 [2, 640], P('section')
- widen_weight_grad: float32 [2, 640, 1280], P('section')
- widen_bias_grad: float32 [2, 1280], P('section')
- type_counts: int32 [30], replicated
- type_loss: float32 [30], replicated
The draws below stay inside these ranges and needn't reach their ends.
Inputs may be any that keep to these rules, and one draw needn't show every extreme that they name: Each micro-batch's stream is packed with whole proteins laid end to end; residues_before and residues_after count the residues of the same protein before and after each position, so they fall to 0 at the first and last residue of every protein. No protein has more than 1024 residues, and each micro-batch holds one of exactly 1024. `residues_after`: consistent with residues_before: the two add up to the protein's length minus one. `residue_types`: types 30 - 5 to 29 never occur. `loss_mask`: each residue is scored with a chance that rises from 1/20 at the start of the stream to 3/10 at its end.
All inputs are finite; a program needn't handle non-finite values.
Results may differ from the reference program's by a relative error of at most 0.0095.
Values may be sent and summed in bfloat16 or wider, within the bound.
No kernel may reach another device: no remote copies, remote signals or barrier semaphores. Data moves between devices by JAX's collectives and lax.ppermute only.
A program may use at most 320 MiB of HBM per device.

```python
import jax
import jax.numpy as jnp
from jax import lax

D = 1280
H = 640
VOCAB = 30
KERNEL_TAPS = 5
DILATION_BLOCK1 = 2
DILATION_BLOCK2 = 64
MAXLEN = 1024
MICRO = 6
TOKENS = 4096


boundary_rate = 256


def protein_spans(key):
    subkeys = jax.random.split(key, 2)
    places = jnp.arange(TOKENS, dtype=jnp.int32)[None, :]
    longest = jax.random.randint(subkeys[0], (MICRO, 1), 0, TOKENS - MAXLEN + 1)
    random_edges = jax.random.randint(subkeys[1], (MICRO, TOKENS), 0, boundary_rate) == 0
    on_grid = (places - longest) % MAXLEN == 0
    inside = (places > longest) & (places < longest + MAXLEN)
    starts = (random_edges | on_grid | (places == 0)) & jnp.logical_not(inside)
    opening = lax.cummax(jnp.where(starts, places, 0), axis=1)
    following = jnp.concatenate([starts[:, 1:], jnp.ones((MICRO, 1), dtype=jnp.bool_)], axis=1)
    ending = lax.cummin(jnp.where(following, places + 1, TOKENS), axis=1, reverse=True)
    return ((places - opening).astype(jnp.int32), (ending - 1 - places).astype(jnp.int32))


def draw_residues_before(key, part):
    span_pair = protein_spans(key)
    return span_pair[0]


def draw_residues_after(key, part):
    span_pair = protein_spans(key)
    return span_pair[1]


def draw_loss_mask(key, part):
    key = jax.random.fold_in(key, 3)
    places = jnp.arange(TOKENS, dtype=jnp.int32)
    levels = 200 + 1000 * places // TOKENS
    return (jax.random.randint(key, (MICRO, TOKENS), 0, 4000) < levels[None, :]).astype(jnp.int32)


def with_ends(result, stream_key, smallest, largest):
    longest = result.shape.index(max(result.shape))
    spots = []
    for shift in (0, 1):
        where = [jax.random.randint(jax.random.fold_in(stream_key, axis), (), 0, length) for axis, length in enumerate(result.shape)]
        where[longest] = (where[longest] + shift) % result.shape[longest]
        spots.append(tuple(where))
    return result.at[spots[0]].set(smallest).at[spots[1]].set(largest)


def steps_of(stream_key, extent, cuts, least, largest):
    level, own = 1.0, jax.random.fold_in(stream_key, 6)
    for position, parts in cuts:
        draws = jnp.exp(jax.random.uniform(jax.random.fold_in(own, position), (parts,), jnp.float32, least / len(cuts), largest / len(cuts)))
        level = level * jnp.repeat(draws, extent[position] // parts).reshape([-1 if axis == position else 1 for axis in range(len(extent))])
    return level


def noise(key, shape, width, bound, cuts=(), held_as=jnp.bfloat16):
    values = width * jax.random.normal(key, shape, jnp.float32)
    if cuts:
        values = values * steps_of(key, shape, cuts, -0.22, 0.18)
    return jnp.clip(values, -bound, bound).astype(held_as)


def setup_inputs(seed: int = 0) -> dict:
    seeds = jax.random.split(jax.random.key(seed), 20)
    block_input = noise(seeds[0], (MICRO, TOKENS, D), 1.0, 6.0, ((1, 16),))
    output_cotangent = noise(seeds[1], (MICRO, TOKENS, D), 1.0, 6.0, ((1, 16),))
    residues_before = draw_residues_before(jax.random.fold_in(seeds[19], 71), 0)
    residues_after = draw_residues_after(jax.random.fold_in(seeds[19], 71), 0)
    residue_types = with_ends(jax.random.randint(seeds[4], (MICRO, TOKENS), 0, VOCAB - 5), jax.random.fold_in(seeds[4], 1), 0, (VOCAB - 5) - 1).astype(jnp.int32)
    loss_mask = draw_loss_mask(jax.random.fold_in(seeds[19], 71), 0)
    first_gain = jnp.clip(1.0 + 0.1 * jax.random.normal(seeds[6], (2, D), jnp.float32), 0.5, 1.5)
    first_shift = noise(seeds[7], (2, D), 0.5, 3.0, ((0, 2),), jnp.float32)
    narrow_weight = noise(seeds[8], (2, D, H), D ** -0.5, 0.15625, ((0, 2),))
    narrow_bias = noise(seeds[9], (2, H), 0.5, 3.0, ((0, 2),), jnp.float32)
    middle_gain = jnp.clip(1.0 + 0.1 * jax.random.normal(seeds[10], (2, H), jnp.float32), 0.5, 1.5)
    middle_shift = noise(seeds[11], (2, H), 0.5, 3.0, ((0, 2),), jnp.float32)
    conv_weight = noise(seeds[12], (2, KERNEL_TAPS, H, H), (KERNEL_TAPS * H) ** -0.5, 0.109375, ((0, 2),))
    conv_bias = noise(seeds[13], (2, H), 0.5, 3.0, ((0, 2),), jnp.float32)
    last_gain = jnp.clip(1.0 + 0.1 * jax.random.normal(seeds[14], (2, H), jnp.float32), 0.5, 1.5)
    last_shift = noise(seeds[15], (2, H), 0.5, 3.0, ((0, 2),), jnp.float32)
    widen_weight = noise(seeds[16], (2, H, D), (H // 2) ** -0.5, 0.3125, ((0, 2),))
    widen_bias = noise(seeds[17], (2, D), 0.5, 3.0, ((0, 2),), jnp.float32)
    head_weight = noise(seeds[18], (D, VOCAB), (D // 4) ** -0.5, 0.3125)
    return {"block_input": block_input, "output_cotangent": output_cotangent, "residues_before": residues_before, "residues_after": residues_after, "residue_types": residue_types, "loss_mask": loss_mask, "first_gain": first_gain, "first_shift": first_shift, "narrow_weight": narrow_weight, "narrow_bias": narrow_bias, "middle_gain": middle_gain, "middle_shift": middle_shift, "conv_weight": conv_weight, "conv_bias": conv_bias, "last_gain": last_gain, "last_shift": last_shift, "widen_weight": widen_weight, "widen_bias": widen_bias, "head_weight": head_weight}


epsilon = 1e-05
highest = lax.Precision.HIGHEST

@jax.custom_vjp
def low(v):
    return lax.optimization_barrier(v.astype(jnp.bfloat16)).astype(jnp.float32)

@jax.custom_vjp
def low_back(v):
    return v

def low_keep(v):
    return (low(v), None)

def low_pass(kept, grad):
    return (grad,)

def back_keep(v):
    return (v, None)

def back_low(kept, grad):
    return (low(grad),)
low.defvjp(low_keep, low_pass)
low_back.defvjp(back_keep, back_low)

def norm_act(values, gain_row, shift_row):
    center = values - lax.optimization_barrier(jnp.mean(values, axis=-1, keepdims=True))
    spread = lax.optimization_barrier(jnp.mean(center * center, axis=-1, keepdims=True))
    return jax.nn.gelu(center * lax.rsqrt(spread + epsilon) * gain_row + shift_row, approximate=False)

def tap_valid_mask(leading_rows, following_rows, dilation_size):
    offsets = (jnp.arange(KERNEL_TAPS, dtype=jnp.int32) - KERNEL_TAPS // 2) * dilation_size
    return ((offsets[None, :] >= -leading_rows[:, None]) & (offsets[None, :] <= following_rows[:, None])).astype(jnp.float32)

def conv_taps(values, live_taps, dilation_size):
    border_extent = KERNEL_TAPS // 2 * dilation_size
    length = values.shape[0]
    padded = jnp.pad(values, ((border_extent, border_extent), (0, 0)))
    pieces = [padded[column * dilation_size:column * dilation_size + length] * live_taps[:, column:column + 1] for column in range(KERNEL_TAPS)]
    return jnp.concatenate(pieces, axis=1)

def dilated_block(stream, params, live_taps, dilation_size):
    activated = low(norm_act(stream, params[0], params[1]))
    narrow = low_back(jnp.dot(activated, params[2], precision=highest) + params[3])
    middle = low(norm_act(narrow, params[4], params[5]))
    stacked = conv_taps(middle, live_taps, dilation_size)
    conv_matrix = params[6].reshape(KERNEL_TAPS * H, H)
    convolved = low_back(jnp.dot(stacked, conv_matrix, precision=highest) + params[7])
    outer_act = low(norm_act(convolved, params[8], params[9]))
    branch = low_back(jnp.dot(outer_act, params[10], precision=highest) + params[11])
    return stream + branch

def type_terms(logits, type_ids, mask_rows):
    row_max = lax.optimization_barrier(jnp.max(logits, axis=1, keepdims=True))
    log_total = row_max[:, 0] + jnp.log(lax.optimization_barrier(jnp.sum(jnp.exp(logits - row_max), axis=1)))
    onehot = (type_ids[:, None] == jnp.arange(logits.shape[1], dtype=jnp.int32)[None, :]).astype(jnp.float32)
    picked = lax.optimization_barrier(jnp.sum(logits * onehot, axis=1))
    weighting = mask_rows.astype(jnp.float32)
    row_loss = (log_total - picked) * weighting
    return (lax.optimization_barrier(jnp.sum(onehot * weighting[:, None], axis=0)), lax.optimization_barrier(jnp.sum(onehot * row_loss[:, None], axis=0)))

def reference(block_input, output_cotangent, residues_before, residues_after, residue_types, loss_mask, first_gain, first_shift, narrow_weight, narrow_bias, middle_gain, middle_shift, conv_weight, conv_bias, last_gain, last_shift, widen_weight, widen_bias, head_weight):
    weights = tuple((tensor.astype(jnp.float32) for tensor in (first_gain, first_shift, narrow_weight, narrow_bias, middle_gain, middle_shift, conv_weight, conv_bias, last_gain, last_shift, widen_weight, widen_bias)))
    head_matrix = head_weight.astype(jnp.float32)
    lower_block = tuple((tensor[0] for tensor in weights))
    upper_block = tuple((tensor[1] for tensor in weights))

    def one_batch(carried, batch_items):
        sums, counts, losses = carried
        stream, cotangent, leading_rows, following_rows, type_ids, mask_rows = batch_items
        nearby_tap_mask = tap_valid_mask(leading_rows, following_rows, DILATION_BLOCK1)
        distant_tap_mask = tap_valid_mask(leading_rows, following_rows, DILATION_BLOCK2)

        def forward(source_input, bottom_block_params, top_block_params, probe_zero):
            hidden_state = dilated_block(source_input, bottom_block_params, nearby_tap_mask, DILATION_BLOCK1)
            handed_output = low_back(low(hidden_state) + probe_zero)
            final_output = dilated_block(handed_output, top_block_params, distant_tap_mask, DILATION_BLOCK2)
            logits = jnp.dot(low(final_output), head_matrix, precision=highest)
            return (hidden_state, final_output, logits)
        source_input = stream.astype(jnp.float32)
        (hidden_state, final_output, logits), pullback = jax.vjp(forward, source_input, lower_block, upper_block, jnp.zeros_like(source_input))
        source_grad, lower_grad, upper_grad, passed_grad = pullback((jnp.zeros_like(hidden_state), cotangent.astype(jnp.float32), jnp.zeros_like(logits)))
        sums = jax.tree.map(lambda running, first_term, second_term: running + jnp.stack([first_term, second_term]), sums, lower_grad, upper_grad)
        part_counts, part_losses = type_terms(logits, type_ids, mask_rows)
        outputs = (hidden_state.astype(jnp.bfloat16), final_output.astype(jnp.bfloat16), source_grad.astype(jnp.bfloat16), passed_grad.astype(jnp.bfloat16))
        return ((sums, counts + part_counts, losses + part_losses), outputs)
    initial = (tuple((jnp.zeros_like(tensor) for tensor in weights)), jnp.zeros((VOCAB,), jnp.float32), jnp.zeros((VOCAB,), jnp.float32))
    (sums, counts, losses), stacked_out = lax.scan(one_batch, initial, (block_input, output_cotangent, residues_before, residues_after, residue_types, loss_mask))
    hiddens, finals, source_grads, passed_grads = stacked_out
    return (jnp.stack([hiddens, finals]), jnp.stack([source_grads, passed_grads]), sums[0], sums[1], sums[2], sums[3], sums[4], sums[5], sums[6], sums[7], sums[8], sums[9], sums[10], sums[11], counts.astype(jnp.int32), losses / jnp.maximum(counts, 1.0))
```

```python
import functools

import jax
import jax.numpy as jnp
from jax import lax
from jax.experimental import pallas as pl
from jax.experimental.pallas import tpu as pltpu
from jax.sharding import PartitionSpec as P

TAPS = 5
DIL0 = 2
DIL1 = 64
EPS = 1e-05
RIM0 = 8
RIM1 = TAPS // 2 * DIL1
F32 = jnp.float32
BF16 = jnp.bfloat16
FG, FS, NB, MG, MS, CB, LG, LS, WB = range(9)
VROWS = 16
LANES = 128
TYPE_COL, MASK_COL = 16, 17
VMEM_LIMIT = 56 * 1024 * 1024
ANY = pl.BlockSpec(memory_space=pl.ANY)


def dot_nn(a, b):
    return lax.dot_general(a, b, (((1,), (0,)), ((), ())), preferred_element_type=F32)


def dot_nt(a, b):
    return lax.dot_general(a, b, (((1,), (1,)), ((), ())), preferred_element_type=F32)


def dot_tn(a, b):
    return lax.dot_general(a, b, (((0,), (0,)), ((), ())), preferred_element_type=F32)


def gelu_parts(y):
    d = jnp.abs(y) * (0.3275911 * 0.7071067811865476) + 1.0
    t = pl.reciprocal(d, approx=True)
    t = t * (2.0 - d * t)
    e = jnp.exp(y * y * -0.5)
    tail = 0.5 * 1.061405429
    tail = tail * t + 0.5 * -1.453152027
    tail = tail * t + 0.5 * 1.421413741
    tail = tail * t + 0.5 * -0.284496736
    tail = tail * t + 0.5 * 0.254829592
    tail = tail * t * e
    phi_big = jnp.where(y >= 0, 1.0 - tail, tail)
    return y * phi_big, phi_big + y * e * 0.3989422804014327


def normed_of(u):
    mean = jnp.mean(u, axis=-1, keepdims=True)
    center = u - mean
    scale = lax.rsqrt(jnp.mean(center * center, axis=-1, keepdims=True) + EPS)
    return center * scale, mean, scale


def norm_back(err, slope, normed, scale, gain):
    q = err * slope
    p = q * gain
    m1 = jnp.mean(p, axis=-1, keepdims=True)
    m2 = jnp.mean(p * normed, axis=-1, keepdims=True)
    return (p - m1 - normed * m2) * scale, q * normed, q


def fold8(v):
    return sum(v[k : k + 8] for k in range(0, v.shape[0], 8))


def chunks(rows, size, body):
    lax.fori_loop(0, rows // size, lambda i, c: (body(pl.multiple_of(i * size, size)), c)[1], 0)


def pick_copy(cond, one, other, dst, sem):
    @pl.when(cond)
    def _():
        pltpu.make_async_copy(one, dst, sem).start()

    @pl.when(jnp.logical_not(cond))
    def _():
        pltpu.make_async_copy(other, dst, sem).start()

    return pltpu.make_async_copy(one, dst, sem)


def conv_copy(cond, one, other, dst, sem):
    inner = one.shape[1]
    waits = []
    for j in range(TAPS):
        part = dst.at[:, (TAPS - 1 - j) * inner : (TAPS - j) * inner]
        waits.append(pick_copy(cond, one.at[j], other.at[j], part, sem.at[j]))
    return waits


def f0_kernel(c_ref, x_ref, xh_ref, mk_ref, v0_ref, v1_ref, nwo, nwx, cwo, cwx, wwo, wwx,
              act0, slx0, mux0, rsx0, nn0, sln0, rsn0, st0, nc0, slc0, rsc0, oa0, out0,
              act1, slx1, mux1, rsx1, nn1, sln1, rsn1, mid1,
              nw0, cw0, ww0, nw1, act_s, n32, mid32, c32, r32, sems):
    low = c_ref[0] == 0
    first = pl.program_id(0) == 0
    rows = x_ref.shape[1]
    inner = n32.shape[1]

    def copies(start):
        pairs = ((nwo, nwx, nw0, 0), (cwo, cwx, cw0, 1), (wwo, wwx, ww0, 2), (nwx, nwo, nw1, 3))
        for one, other, dst, k in pairs:
            if start:
                pick_copy(low, one, other, dst, sems.at[k])
            else:
                pltpu.make_async_copy(one, dst, sems.at[k]).wait()

    @pl.when(first)
    def _():
        copies(True)

    def first_norm(u, k):
        normed, mean, scale = normed_of(u)
        act, slope = gelu_parts(normed * v0_ref[FG : FG + 1] + v0_ref[FS : FS + 1])
        return act.astype(BF16), slope, mean, scale

    def stage1(r):
        s = pl.ds(r, 16)
        act, slope, mean, scale = first_norm(x_ref[0, s, :].astype(F32), 0)
        act_s[s, :] = act
        act0[0, s, :] = act
        slx0[0, s, :] = slope.astype(BF16)
        mux0[0, s, :] = mean
        rsx0[0, s, :] = scale

    chunks(rows, 16, stage1)
    act, _, _, _ = first_norm(xh_ref[0].astype(F32), 0)
    act_s[rows : rows + 2 * RIM0, :] = act

    @pl.when(first)
    def _():
        copies(False)

    n32[...] = dot_nn(act_s[...], nw0[...])

    def mid_norm(u, v_ref):
        normed, _, scale = normed_of(u + v_ref[NB : NB + 1, :inner])
        act, slope = gelu_parts(normed * v_ref[MG : MG + 1, :inner] + v_ref[MS : MS + 1, :inner])
        return act.astype(BF16), slope, normed, scale

    def stage2(r):
        s = pl.ds(r, 16)
        mid, slope, normed, scale = mid_norm(n32[s, :], v0_ref)
        mid32[pl.ds(r + RIM0, 16), :] = mid.astype(F32)
        nn0[0, s, :] = normed.astype(BF16)
        sln0[0, s, :] = slope.astype(BF16)
        rsn0[0, s, :] = scale

    chunks(rows, 16, stage2)
    rim, _, _, _ = mid_norm(n32[rows : rows + 2 * RIM0, :], v0_ref)
    rim = rim.astype(F32)
    mid32[0:RIM0, :] = rim[:RIM0]
    mid32[rows + RIM0 : rows + 2 * RIM0, :] = rim[RIM0:]

    def stage3(r):
        s = pl.ds(r, 16)
        window = mid32[pl.ds(r, 32), :]
        for j in range(TAPS):
            at = RIM0 + (j - TAPS // 2) * DIL0
            live = mk_ref[0, s, j : j + 1]
            st0[0, s, j * inner : (j + 1) * inner] = (window[at : at + 16] * live).astype(BF16)

    chunks(rows, 16, stage3)
    c32[...] = dot_nn(st0[0], cw0[...].reshape(TAPS * inner, inner))

    def stage4(r):
        s = pl.ds(r, 16)
        normed, _, scale = normed_of(c32[s, :] + v0_ref[CB : CB + 1, :inner])
        act, slope = gelu_parts(normed * v0_ref[LG : LG + 1, :inner] + v0_ref[LS : LS + 1, :inner])
        oa0[0, s, :] = act.astype(BF16)
        nc0[0, s, :] = normed.astype(BF16)
        slc0[0, s, :] = slope.astype(BF16)
        rsc0[0, s, :] = scale

    chunks(rows, 16, stage4)
    r32[...] = dot_nn(oa0[0], ww0[...])

    def stage5(r):
        s = pl.ds(r, 16)
        res = (x_ref[0, s, :].astype(F32) + (r32[s, :] + v0_ref[WB : WB + 1])).astype(BF16)
        out0[0, s, :] = res
        normed, mean, scale = normed_of(res.astype(F32))
        act, slope = gelu_parts(normed * v1_ref[FG : FG + 1] + v1_ref[FS : FS + 1])
        act1[0, s, :] = act.astype(BF16)
        slx1[0, s, :] = slope.astype(BF16)
        mux1[0, s, :] = mean
        rsx1[0, s, :] = scale

    chunks(rows, 16, stage5)
    n32[0:rows, :] = dot_nn(act1[0], nw1[...])

    def stage6(r):
        s = pl.ds(r, 16)
        mid, slope, normed, scale = mid_norm(n32[s, :], v1_ref)
        mid1[0, s, :] = mid
        nn1[0, s, :] = normed.astype(BF16)
        sln1[0, s, :] = slope.astype(BF16)
        rsn1[0, s, :] = scale

    chunks(rows, 16, stage6)


def f1_kernel(c_ref, mid_ref, up_ref, dn_ref, mk_ref, v1_ref, cot_ref, cwo, cwx, wwo, wwx,
              st1, oa1, cg1, vec,
              cw1, ww1, ext, c32, e32, acc, sems):
    low = c_ref[0] == 0
    step = pl.program_id(0)
    rows = mid_ref.shape[1]
    inner = c32.shape[1]

    @pl.when(step == 0)
    def _():
        pick_copy(low, cwx, cwo, cw1, sems.at[0])
        pick_copy(low, wwx, wwo, ww1, sems.at[1])
        acc[...] = jnp.zeros_like(acc)

    ext[0:RIM1, :] = up_ref[0]
    ext[RIM1 : RIM1 + rows, :] = mid_ref[0]
    ext[RIM1 + rows : 2 * RIM1 + rows, :] = dn_ref[0]

    def stack(r):
        s = pl.ds(r, 32)
        for j in range(TAPS):
            at = RIM1 + (j - TAPS // 2) * DIL1
            live = mk_ref[0, s, 8 + j : 9 + j]
            part = ext[pl.ds(r + at, 32), :].astype(F32) * live
            st1[0, s, j * inner : (j + 1) * inner] = part.astype(BF16)

    chunks(rows, 32, stack)

    def cot_sum(r):
        acc[3, :, :] += fold8(cot_ref[0, pl.ds(r, 16), :].astype(F32))

    chunks(rows, 16, cot_sum)

    @pl.when(step == 0)
    def _():
        pltpu.make_async_copy(cwx, cw1, sems.at[0]).wait()
        pltpu.make_async_copy(wwx, ww1, sems.at[1]).wait()

    e32[...] = dot_nt(cot_ref[0], ww1[...])
    c32[...] = dot_nn(st1[0], cw1[...].reshape(TAPS * inner, inner))

    def stage(r):
        s = pl.ds(r, 16)
        gain = v1_ref[LG : LG + 1, :inner]
        normed, _, scale = normed_of(c32[s, :] + v1_ref[CB : CB + 1, :inner])
        act, slope = gelu_parts(normed * gain + v1_ref[LS : LS + 1, :inner])
        oa1[0, s, :] = act.astype(BF16)
        du, dgain, dshift = norm_back(e32[s, :], slope, normed, scale, gain)
        du = du.astype(BF16)
        cg1[0, s, :] = du
        acc[0, :, :inner] += fold8(dgain)
        acc[1, :, :inner] += fold8(dshift)
        acc[2, :, :inner] += fold8(du.astype(F32))

    chunks(rows, 16, stage)

    @pl.when(step == pl.num_programs(0) - 1)
    def _():
        vec[...] = jnp.sum(acc[...], axis=1)


def o1_kernel(c_ref, out0_ref, oa_ref, mk_ref, v1_ref, head_ref, wwo, wwx, out1, tot, ww1, r32, lg, acc, sems, *, vocab):
    low = c_ref[0] == 0
    step = pl.program_id(0)
    rows = oa_ref.shape[1]

    @pl.when(step == 0)
    def _():
        pick_copy(low, wwx, wwo, ww1, sems.at[0])
        acc[...] = jnp.zeros_like(acc)
        pltpu.make_async_copy(wwx, ww1, sems.at[0]).wait()

    r32[...] = dot_nn(oa_ref[0], ww1[...])

    def stage(r):
        s = pl.ds(r, 16)
        out1[0, s, :] = (out0_ref[0, s, :].astype(F32) + (r32[s, :] + v1_ref[WB : WB + 1])).astype(BF16)

    chunks(rows, 16, stage)
    lg[...] = dot_nn(out1[0], head_ref[...])

    def loss(r):
        s = pl.ds(r, 32)
        lane = lax.broadcasted_iota(jnp.int32, (32, LANES), 1)
        logits = jnp.where(lane < vocab, lg[s, :], -1e30)
        top = jnp.max(logits, axis=-1, keepdims=True)
        log_total = top + jnp.log(jnp.sum(jnp.exp(logits - top), axis=-1, keepdims=True))
        kind = mk_ref[0, s, TYPE_COL : TYPE_COL + 1].astype(jnp.int32)
        weight = mk_ref[0, s, MASK_COL : MASK_COL + 1]
        onehot = jnp.where(lane == kind, weight, 0.0)
        acc[0] += fold8(onehot)
        acc[1] += fold8(onehot * (log_total - logits))

    chunks(rows, 32, loss)

    @pl.when(step == pl.num_programs(0) - 1)
    def _():
        tot[...] = jnp.sum(acc[...], axis=1)


def back_conv(dst32, stg, cw2):
    dst32[...] = dot_nt(stg[...], cw2[...])


def back_mid(rows, inner, m32, sln, nn, rsn, v_ref, ng, acc, at):
    def stage(r):
        s = pl.ds(r, 16)
        du, dgain, dshift = norm_back(
            m32[s, :], sln[0, s, :].astype(F32), nn[0, s, :].astype(F32), rsn[0, s, :], v_ref[MG : MG + 1, :inner]
        )
        du = du.astype(BF16)
        ng[0, s, :] = du
        acc[at, :, :inner] += fold8(dgain)
        acc[at + 1, :, :inner] += fold8(dshift)
        acc[at + 2, :, :inner] += fold8(du.astype(F32))

    chunks(rows, 16, stage)


def back_first(rows, a32, slx, src, mux, rsx, v_ref, grad, ig, acc, at):
    def stage(r):
        s = pl.ds(r, 16)
        scale = rsx[0, s, :]
        normed = (src[0, s, :].astype(F32) - mux[0, s, :]) * scale
        du, dgain, dshift = norm_back(a32[s, :], slx[0, s, :].astype(F32), normed, scale, v_ref[FG : FG + 1])
        ig[0, s, :] = (grad[0, s, :].astype(F32) + du).astype(BF16)
        acc[at, :, :] += fold8(dgain)
        acc[at + 1, :, :] += fold8(dshift)

    chunks(rows, 16, stage)


def b10_kernel(c_ref, cg_ref, up_ref, dn_ref, mk_ref, v0_ref, v1_ref, cot_ref, sln1, nn1, rsn1, slx1, out0, mux1, rsx1,
               slc0, nc0, rsc0, cwo, cwx, nwo, nwx, wwo, wwx,
               ng1, ig1, cg0, vec,
               cw2, nw1, ww0, ext, stg, m32, a32, acc, sems):
    low = c_ref[0] == 0
    step = pl.program_id(0)
    rows = cg_ref.shape[1]
    inner = m32.shape[1]

    @pl.when(step == 0)
    def _():
        waits = conv_copy(low, cwx, cwo, cw2, sems)
        waits.append(pick_copy(low, nwx, nwo, nw1, sems.at[TAPS]))
        waits.append(pick_copy(low, wwo, wwx, ww0, sems.at[TAPS + 1]))
        acc[...] = jnp.zeros_like(acc)
        for w in waits:
            w.wait()

    ext[0:RIM1, :] = up_ref[0]
    ext[RIM1 : RIM1 + rows, :] = cg_ref[0]
    ext[RIM1 + rows : 2 * RIM1 + rows, :] = dn_ref[0]

    def stack(r):
        s = pl.ds(r, 32)
        for j in range(TAPS):
            at = RIM1 + (j - TAPS // 2) * DIL1
            live = mk_ref[0, s, 8 + j : 9 + j]
            part = ext[pl.ds(r + at, 32), :].astype(F32) * live
            stg[s, j * inner : (j + 1) * inner] = part.astype(BF16)

    chunks(rows, 32, stack)
    back_conv(m32, stg, cw2)
    back_mid(rows, inner, m32, sln1, nn1, rsn1, v1_ref, ng1, acc, 0)
    a32[...] = dot_nt(ng1[0], nw1[...])
    back_first(rows, a32, slx1, out0, mux1, rsx1, v1_ref, cot_ref, ig1, acc, 3)
    m32[...] = dot_nt(ig1[0], ww0[...])

    def stage(r):
        s = pl.ds(r, 16)
        du, dgain, dshift = norm_back(
            m32[s, :], slc0[0, s, :].astype(F32), nc0[0, s, :].astype(F32), rsc0[0, s, :], v0_ref[LG : LG + 1, :inner]
        )
        du = du.astype(BF16)
        cg0[0, s, :] = du
        acc[5, :, :inner] += fold8(dgain)
        acc[6, :, :inner] += fold8(dshift)
        acc[7, :, :inner] += fold8(du.astype(F32))
        acc[8, :, :] += fold8(ig1[0, s, :].astype(F32))

    chunks(rows, 16, stage)

    @pl.when(step == pl.num_programs(0) - 1)
    def _():
        vec[...] = jnp.sum(acc[...], axis=1)


def b0_kernel(c_ref, cg_ref, rim_ref, mk_ref, v0_ref, ig1_ref, sln0, nn0, rsn0, slx0, x_ref, mux0, rsx0,
              cwo, cwx, nwo, nwx,
              ng0, ig0, vec,
              cw2, nw0, ext, stg, m32, a32, acc, sems):
    low = c_ref[0] == 0
    step = pl.program_id(0)
    rows = cg_ref.shape[1]
    inner = m32.shape[1]

    @pl.when(step == 0)
    def _():
        waits = conv_copy(low, cwo, cwx, cw2, sems)
        waits.append(pick_copy(low, nwo, nwx, nw0, sems.at[TAPS]))
        acc[...] = jnp.zeros_like(acc)
        for w in waits:
            w.wait()

    rim = rim_ref[0].astype(F32)
    ext[0:RIM0, :] = rim[:RIM0]
    ext[rows + RIM0 : rows + 2 * RIM0, :] = rim[RIM0:]

    def widen(r):
        ext[pl.ds(r + RIM0, 16), :] = cg_ref[0, pl.ds(r, 16), :].astype(F32)

    chunks(rows, 16, widen)

    def stack(r):
        s = pl.ds(r, 16)
        window = ext[pl.ds(r, 32), :]
        for j in range(TAPS):
            at = RIM0 + (j - TAPS // 2) * DIL0
            live = mk_ref[0, s, j : j + 1]
            stg[s, j * inner : (j + 1) * inner] = (window[at : at + 16] * live).astype(BF16)

    chunks(rows, 16, stack)
    back_conv(m32, stg, cw2)
    back_mid(rows, inner, m32, sln0, nn0, rsn0, v0_ref, ng0, acc, 0)
    a32[...] = dot_nt(ng0[0], nw0[...])
    back_first(rows, a32, slx0, x_ref, mux0, rsx0, v0_ref, ig1_ref, ig0, acc, 3)

    @pl.when(step == pl.num_programs(0) - 1)
    def _():
        vec[...] = jnp.sum(acc[...], axis=1)


def weight_terms(pairs, tile, out_rows):
    specs, args, spans = [], [], []
    at = 0
    for a, g in pairs:
        rows = a.shape[0]
        na, ng = a.shape[1] // tile, g.shape[1] // tile

        def a_map(s, at=at, na=na, ng=ng):
            return (0, jnp.clip(s - at, 0, na * ng - 1) % na)

        def g_map(s, at=at, na=na, ng=ng):
            return (0, jnp.clip(s - at, 0, na * ng - 1) // na)

        specs += [pl.BlockSpec((rows, tile), a_map), pl.BlockSpec((rows, tile), g_map)]
        args += [a, g]
        spans.append((at, at + na * ng))
        at += na * ng

    def kernel(*refs):
        out = refs[-1]
        s = pl.program_id(0)
        for k, (lo, hi) in enumerate(spans):

            @pl.when((s >= lo) & (s < hi))
            def _(k=k):
                out[...] = dot_tn(refs[2 * k][...], refs[2 * k + 1][...]).astype(BF16)

    flops = at * 2 * tile * tile * args[0].shape[0]
    return pl.pallas_call(
        kernel,
        grid=(at,),
        in_specs=specs,
        out_specs=pl.BlockSpec((tile, tile), lambda s: (s, 0)),
        out_shape=jax.ShapeDtypeStruct((out_rows, tile), BF16),
        compiler_params=pltpu.CompilerParams(vmem_limit_bytes=VMEM_LIMIT),
        cost_estimate=pl.CostEstimate(flops=flops, bytes_accessed=4 * out_rows * tile, transcendentals=0),
    )(*args)


def add_low(one, other):
    return (one.astype(F32) + other.astype(F32)).astype(BF16)


def halves(buf, bit):
    rows = buf.shape[0] // 2
    keep = lax.dynamic_slice_in_dim(buf, bit * rows, rows, 0)
    send = lax.dynamic_slice_in_dim(buf, (1 - bit) * rows, rows, 0)
    return keep, send


def dp_steps(count, sec, at):
    bits = count.bit_length() - 1
    orders = [list(range(bits)), [1, 0] + list(range(2, bits))]
    out = []
    for k in range(bits):
        pairs = [
            (s * count + d, s * count + (d ^ (1 << orders[s][k])))
            for s in range(2)
            for d in range(count)
        ]
        place = jnp.where(sec == 0, orders[0][k], orders[1][k])
        out.append((pairs, (at >> place) & 1))
    return out


def body(block_input, output_cotangent, residues_before, residues_after, residue_types, loss_mask,
         first_gain, first_shift, narrow_weight, narrow_bias, middle_gain, middle_shift,
         conv_weight, conv_bias, last_gain, last_shift, widen_weight, widen_bias, head_weight):
    sec = lax.axis_index("section")
    at = lax.axis_index("dp")
    count = lax.axis_size("dp")
    low = sec == 0
    micro, rows, width = block_input.shape
    own = micro // 2
    inner = narrow_weight.shape[2]
    vocab = head_weight.shape[1]
    swap = [(0, 1), (1, 0)]
    ahead = [(i, (i + 1) % count) for i in range(count)]
    behind = [((i + 1) % count, i) for i in range(count)]
    c_arr = sec.astype(jnp.int32).reshape(1)

    def other(v):
        return lax.ppermute(v, "section", swap)

    nwo, cwo, wwo = narrow_weight[0], conv_weight[0], widen_weight[0]
    nwx, cwx, wwx = other(nwo), other(cwo), other(wwo)
    vectors = (first_gain, first_shift, narrow_bias, middle_gain, middle_shift, conv_bias, last_gain, last_shift, widen_bias)
    packed = jnp.concatenate(
        [jnp.pad(v, ((0, 0), (0, width - v.shape[1]))) for v in vectors] + [jnp.zeros((VROWS - len(vectors), width), F32)]
    )
    packed_x = other(packed)
    v0 = jnp.where(low, packed, packed_x)
    v1 = jnp.where(low, packed_x, packed)

    x_own = lax.dynamic_slice_in_dim(block_input, sec * own, own, 0)
    xh = jnp.concatenate(
        [lax.ppermute(x_own[:, -RIM0:], "dp", ahead), lax.ppermute(x_own[:, :RIM0], "dp", behind)], axis=1
    )

    lane = jnp.arange(LANES, dtype=jnp.int32)[None, None, :]
    offset = jnp.where(lane < 8, (lane - TAPS // 2) * DIL0, (lane - 8 - TAPS // 2) * DIL1)
    masks = ((offset >= -residues_before[..., None]) & (offset <= residues_after[..., None])).astype(F32)
    masks = jnp.where(lane == TYPE_COL, residue_types[..., None].astype(F32), masks)
    masks = jnp.where(lane == MASK_COL, loss_mask[..., None].astype(F32), masks)

    def mine(shape):
        return pl.BlockSpec((1, *shape), lambda i, c: (c[0] * own + i, 0, 0))

    def each(n, w):
        return pl.BlockSpec((1, n, w), lambda i, c: (i, 0, 0))

    def whole(*shape):
        return pl.BlockSpec(shape, lambda i, c: (0,) * len(shape))

    def call(kernel, ins, in_specs, outs, scratch, flops, nbytes, trans=0):
        return pl.pallas_call(
            kernel,
            grid_spec=pltpu.PrefetchScalarGridSpec(
                num_scalar_prefetch=1,
                grid=(own,),
                in_specs=in_specs,
                out_specs=[o[1] for o in outs],
                scratch_shapes=scratch,
            ),
            out_shape=[o[0] for o in outs],
            compiler_params=pltpu.CompilerParams(vmem_limit_bytes=VMEM_LIMIT),
            cost_estimate=pl.CostEstimate(flops=flops, bytes_accessed=nbytes, transcendentals=trans),
        )(c_arr, *ins)

    def o_each(w, dtype=BF16):
        return (jax.ShapeDtypeStruct((own, rows, w), dtype), each(rows, w))

    def o_vec(n, w):
        return (jax.ShapeDtypeStruct((n, w), F32), whole(n, w))

    dma = pltpu.SemaphoreType.DMA
    vspec = whole(VROWS, width)
    mm = 2 * own * rows * width * inner
    wide, thin, one = o_each(width), o_each(inner), o_each(1, F32)
    (act0, slx0, mux0, rsx0, nn0, sln0, rsn0, st0, nc0, slc0, rsc0, oa0, out0,
     act1, slx1, mux1, rsx1, nn1, sln1, rsn1, mid1) = call(
        f0_kernel,
        (block_input, xh, masks, v0, v1, nwo, nwx, cwo, cwx, wwo, wwx),
        [mine((rows, width)), each(2 * RIM0, width), mine((rows, LANES)), vspec, vspec] + [ANY] * 6,
        [wide, wide, one, one, thin, thin, one, o_each(TAPS * inner), thin, thin, one, thin, wide,
         wide, wide, one, one, thin, thin, one, thin],
        [
            pltpu.VMEM((width, inner), BF16),
            pltpu.VMEM((TAPS, inner, inner), BF16),
            pltpu.VMEM((inner, width), BF16),
            pltpu.VMEM((width, inner), BF16),
            pltpu.VMEM((rows + 2 * RIM0, width), BF16),
            pltpu.VMEM((rows + 2 * RIM0, inner), F32),
            pltpu.VMEM((rows + 2 * RIM0, inner), F32),
            pltpu.VMEM((rows, inner), F32),
            pltpu.VMEM((rows, width), F32),
            dma((4,)),
        ],
        int(5.5 * mm), 40_000_000, own * rows * 8 * width,
    )

    up1 = lax.ppermute(mid1[:, -RIM1:], "dp", ahead)
    dn1 = lax.ppermute(mid1[:, :RIM1], "dp", behind)
    st1, oa1, cg1, vec1 = call(
        f1_kernel,
        (mid1, up1, dn1, masks, v1, output_cotangent, cwo, cwx, wwo, wwx),
        [each(rows, inner), each(RIM1, inner), each(RIM1, inner), mine((rows, LANES)), vspec, mine((rows, width))] + [ANY] * 4,
        [o_each(TAPS * inner), thin, thin, o_vec(4, width)],
        [
            pltpu.VMEM((TAPS, inner, inner), BF16),
            pltpu.VMEM((inner, width), BF16),
            pltpu.VMEM((rows + 2 * RIM1, inner), BF16),
            pltpu.VMEM((rows, inner), F32),
            pltpu.VMEM((rows, inner), F32),
            pltpu.VMEM((4, 8, width), F32),
            dma((2,)),
        ],
        int(3.5 * mm), 20_000_000, own * rows * 2 * inner,
    )

    upg = lax.ppermute(cg1[:, -RIM1:], "dp", ahead)
    dng = lax.ppermute(cg1[:, :RIM1], "dp", behind)

    def flat(v):
        return v.reshape(own * rows, v.shape[2])

    cot_own = flat(lax.dynamic_slice_in_dim(output_cotangent, sec * own, own, 0))
    unit = 2 * count * 8

    def padded(n):
        return -(-n // unit) * unit

    rows_a = padded((TAPS + width // inner) * inner)
    rows_b = padded(width)
    pay_a1 = weight_terms([(flat(oa1), cot_own), (flat(st1), flat(cg1))], inner, rows_a)

    ng1, ig1, cg0, vec10 = call(
        b10_kernel,
        (cg1, upg, dng, masks, v0, v1, output_cotangent, sln1, nn1, rsn1, slx1, out0, mux1, rsx1, slc0, nc0, rsc0,
         cwo, cwx, nwo, nwx, wwo, wwx),
        [each(rows, inner), each(RIM1, inner), each(RIM1, inner), mine((rows, LANES)), vspec, vspec, mine((rows, width)),
         each(rows, inner), each(rows, inner), each(rows, 1), each(rows, width), each(rows, width), each(rows, 1), each(rows, 1),
         each(rows, inner), each(rows, inner), each(rows, 1)] + [ANY] * 6,
        [thin, wide, thin, o_vec(9, width)],
        [
            pltpu.VMEM((inner, TAPS * inner), BF16),
            pltpu.VMEM((width, inner), BF16),
            pltpu.VMEM((inner, width), BF16),
            pltpu.VMEM((rows + 2 * RIM1, inner), BF16),
            pltpu.VMEM((rows, TAPS * inner), BF16),
            pltpu.VMEM((rows, inner), F32),
            pltpu.VMEM((rows, width), F32),
            pltpu.VMEM((9, 8, width), F32),
            dma((TAPS + 2,)),
        ],
        int(4.5 * mm), 30_000_000,
    )

    upz = lax.ppermute(cg0[:, -RIM0:], "dp", ahead)
    dnz = lax.ppermute(cg0[:, :RIM0], "dp", behind)
    rim0 = jnp.concatenate([upz, dnz], axis=1)
    pay_b1 = weight_terms([(flat(act1), flat(ng1))], inner, rows_b)
    pay_a0 = weight_terms([(flat(oa0), flat(ig1)), (flat(st0), flat(cg0))], inner, rows_a)

    ng0, ig0, vec0 = call(
        b0_kernel,
        (cg0, rim0, masks, v0, ig1, sln0, nn0, rsn0, slx0, block_input, mux0, rsx0, cwo, cwx, nwo, nwx),
        [each(rows, inner), each(2 * RIM0, inner), mine((rows, LANES)), vspec, each(rows, width),
         each(rows, inner), each(rows, inner), each(rows, 1), each(rows, width), mine((rows, width)), each(rows, 1), each(rows, 1)]
        + [ANY] * 4,
        [thin, wide, o_vec(5, width)],
        [
            pltpu.VMEM((inner, TAPS * inner), BF16),
            pltpu.VMEM((width, inner), BF16),
            pltpu.VMEM((rows + 2 * RIM0, inner), F32),
            pltpu.VMEM((rows, TAPS * inner), BF16),
            pltpu.VMEM((rows, inner), F32),
            pltpu.VMEM((rows, width), F32),
            pltpu.VMEM((5, 8, width), F32),
            dma((TAPS + 1,)),
        ],
        int(3.5 * mm), 25_000_000,
    )
    pay_b0 = weight_terms([(flat(act0), flat(ng0))], inner, rows_b)

    head = jnp.pad(head_weight, ((0, 0), (0, LANES - vocab)))
    out1, tot = call(
        functools.partial(o1_kernel, vocab=vocab),
        (out0, oa1, masks, v1, head, wwo, wwx),
        [each(rows, width), each(rows, inner), mine((rows, LANES)), vspec, whole(width, LANES), ANY, ANY],
        [wide, o_vec(2, LANES)],
        [
            pltpu.VMEM((inner, width), BF16),
            pltpu.VMEM((rows, width), F32),
            pltpu.VMEM((rows, LANES), F32),
            pltpu.VMEM((2, 8, LANES), F32),
            dma((1,)),
        ],
        int(1.2 * mm), 8_000_000,
    )

    steps = dp_steps(count, sec, at)

    def hop(v, pairs):
        return lax.ppermute(v, ("section", "dp"), pairs)

    def summed(pay):
        keep, send = halves(pay, sec)
        buf = add_low(keep, other(send))
        for pairs, bit in steps:
            keep, send = halves(buf, bit)
            buf = add_low(keep, hop(send, pairs))
        for pairs, bit in reversed(steps):
            come = hop(buf, pairs)
            one, two = jnp.where(bit == 0, buf, come), jnp.where(bit == 0, come, buf)
            buf = jnp.concatenate([one, two], axis=0)
        return buf

    half_a1, half_b1, half_a0, half_b0 = summed(pay_a1), summed(pay_b1), summed(pay_a0), summed(pay_b0)

    def joined(half0, half1):
        keep = jnp.where(low, half0, half1)
        come = other(jnp.where(low, half1, half0))
        return jnp.concatenate([jnp.where(low, keep, come), jnp.where(low, come, keep)], axis=0)

    full_a, full_b = joined(half_a0, half_a1), joined(half_b0, half_b1)
    cols = width // inner
    widen_grad = jnp.concatenate([full_a[k * inner : (k + 1) * inner] for k in range(cols)], axis=1).astype(F32)
    conv_grad = full_a[cols * inner : (cols + TAPS) * inner].astype(F32).reshape(TAPS, inner, inner)
    narrow_grad = full_b[:width].astype(F32)

    small = jnp.concatenate([vec1, vec10, vec0, jnp.pad(tot, ((0, 0), (0, width - LANES)))], axis=0)
    small = jnp.pad(small, ((0, -small.shape[0] % 8), (0, 0)))
    for pairs, _ in steps:
        small = small + hop(small, pairs)
    small = small + other(small)
    n1, n10 = vec1.shape[0], vec10.shape[0]
    s1, s10, s0 = small[:n1], small[n1 : n1 + n10], small[n1 + n10 : n1 + n10 + vec0.shape[0]]
    type_total, loss_total = small[n1 + n10 + vec0.shape[0]], small[n1 + n10 + vec0.shape[0] + 1]
    type_total, loss_total = type_total[:vocab], loss_total[:vocab]

    def sel(in0, in1):
        return jnp.where(low, in0, in1)[None]

    first_gain_grad = sel(s0[3], s10[3])
    first_shift_grad = sel(s0[4], s10[4])
    middle_gain_grad = sel(s0[0], s10[0])[:, :inner]
    middle_shift_grad = sel(s0[1], s10[1])[:, :inner]
    narrow_bias_grad = sel(s0[2], s10[2])[:, :inner]
    last_gain_grad = sel(s10[5], s1[0])[:, :inner]
    last_shift_grad = sel(s10[6], s1[1])[:, :inner]
    conv_bias_grad = sel(s10[7], s1[2])[:, :inner]
    widen_bias_grad = sel(s10[8], s1[3])

    def gathered(in0, in1):
        keep = jnp.where(low, in0, in1)
        come = other(jnp.where(low, in1, in0))
        return jnp.concatenate([jnp.where(low, keep, come), jnp.where(low, come, keep)], axis=0)[None]

    return (
        gathered(out0, out1),
        gathered(ig0, ig1),
        first_gain_grad,
        first_shift_grad,
        narrow_grad[None],
        narrow_bias_grad,
        middle_gain_grad,
        middle_shift_grad,
        conv_grad[None],
        conv_bias_grad,
        last_gain_grad,
        last_shift_grad,
        widen_grad[None],
        widen_bias_grad,
        type_total.astype(jnp.int32),
        loss_total / jnp.maximum(type_total, 1.0),
    )


def solution(mesh):
    rows = P(None, "dp", None)
    ids = P(None, "dp")
    vec = P("section", None)
    mat = P("section", None, None)
    conv = P("section", None, None, None)
    weights = (vec, vec, mat, vec, vec, vec, conv, vec, vec, vec, mat, vec)
    grads = P("section", None, "dp", None)
    return jax.shard_map(
        body,
        mesh=mesh,
        in_specs=(rows, rows, ids, ids, ids, ids, *weights, P()),
        out_specs=(grads, grads, *weights, P(), P()),
        check_vma=False,
    )
```

```python
import functools

import jax
import jax.numpy as jnp
from jax import lax
from jax.experimental import pallas as pl
from jax.experimental.pallas import tpu as pltpu
from jax.sharding import PartitionSpec as P

TAPS = 5
MID = TAPS // 2
DIL0 = 2
DIL1 = 64
EPS = 1e-05
SCALE = 2
RIM0 = 8
RIM1 = MID * DIL1
F32 = jnp.float32
BF16 = jnp.bfloat16
LANES = 128
LIVE1 = 8
VMEM_LIMIT = 56 * 1024 * 1024
ANY = pl.BlockSpec(memory_space=pl.ANY)


def dot_nn(a, b):
    return lax.dot_general(a, b, (((1,), (0,)), ((), ())), preferred_element_type=F32)


def dot_nt(a, b):
    return lax.dot_general(a, b, (((1,), (1,)), ((), ())), preferred_element_type=F32)


def dot_tn(a, b):
    return lax.dot_general(a, b, (((0,), (0,)), ((), ())), preferred_element_type=F32)


def gelu_parts(y):
    phi_big = lax.erf(y * 0.7071067811865476) * 0.5 + 0.5
    e = jnp.exp(y * y * -0.5)
    return y * phi_big, phi_big + y * e * 0.3989422804014327


def normed_of(u):
    mean = jnp.mean(u, axis=-1, keepdims=True)
    center = u - mean
    scale = lax.rsqrt(jnp.mean(center * center, axis=-1, keepdims=True) + EPS)
    return center * scale, mean, scale


def norm_back(err, slope, normed, scale, gain):
    q = err * slope
    p = q * gain
    m1 = jnp.mean(p, axis=-1, keepdims=True)
    m2 = jnp.mean(p * normed, axis=-1, keepdims=True)
    return (p - m1 - normed * m2) * scale, q * normed, q


def fold8(v):
    return sum(v[k : k + 8] for k in range(0, v.shape[0], 8))


def chunks(rows, size, body):
    steps = rows // size
    lax.fori_loop(0, steps, lambda i, c: (body(pl.multiple_of(i * size, size)), c)[1], 0, unroll=min(8, steps))


def summed_chunks(rows, size, width, terms, body):
    steps = rows // size

    def one(i, held):
        return tuple(h + fold8(v) for h, v in zip(held, body(pl.multiple_of(i * size, size))))

    return lax.fori_loop(0, steps, one, (jnp.zeros((8, width), F32),) * terms, unroll=min(8, steps))


def pick_copy(cond, one, other, dst, sem):
    @pl.when(cond)
    def _():
        pltpu.make_async_copy(one, dst, sem).start()

    @pl.when(jnp.logical_not(cond))
    def _():
        pltpu.make_async_copy(other, dst, sem).start()


def pick_wait(one, dst, sem):
    pltpu.make_async_copy(one, dst, sem).wait()


def conv_parts(one, dst):
    inner = one.shape[1]
    return [(j, dst.at[:, (TAPS - 1 - j) * inner : (TAPS - j) * inner]) for j in range(TAPS)]


def columns(row):
    return jnp.broadcast_to(row, (LANES, row.shape[1])).T


class Vectors:
    def __init__(self, ref, width, inner):
        at = 0
        for name in ("fg", "fs", "wb"):
            setattr(self, name, ref[:, at : at + width])
            at += width
        for name in ("nb", "mg", "ms", "cb", "lg", "ls"):
            setattr(self, name, ref[:, at : at + inner])
            at += inner


def f0_kernel(c_ref, x_ref, xh_ref, rb_ref, ra_ref, v0_ref, v1_ref, nwo, nwx, cwo, cwx, wwo, wwx,
              mk, act0, slx0, mux0, rsx0, nn0, sln0, rsn0, st0, nc0, slc0, rsc0, oa0, out0,
              act1, slx1, mux1, rsx1, nn1, sln1, rsn1, mid1,
              nw0, cw0, ww0, nw1, act_s, n32, mid32, c32, r32, sems):
    low = c_ref[0] == 0
    first = pl.program_id(0) == 0
    rows, width = x_ref.shape[1:]
    inner = n32.shape[1]
    v0, v1 = Vectors(v0_ref, width, inner), Vectors(v1_ref, width, inner)

    @pl.when(first)
    def _():
        pick_copy(low, nwo, nwx, nw0, sems.at[0])
        pick_copy(low, cwo, cwx, cw0, sems.at[1])
        pick_copy(low, wwo, wwx, ww0, sems.at[2])
        pick_copy(low, nwx, nwo, nw1, sems.at[3])

    lane = lax.broadcasted_iota(jnp.int32, (rows, LANES), 1)
    offset = jnp.where(lane < LIVE1, (lane - MID) * DIL0, (lane - LIVE1 - MID) * DIL1).astype(F32)
    before, after = columns(rb_ref[0].astype(F32)), columns(ra_ref[0].astype(F32))
    mk[0] = jnp.where((offset >= -before) & (offset <= after), 1.0, 0.0)

    def first_norm(u, v):
        normed, mean, scale = normed_of(u)
        act, slope = gelu_parts(normed * v.fg + v.fs)
        return act.astype(BF16), slope.astype(BF16), mean, scale

    def stage1(r):
        s = pl.ds(r, 16)
        act, slope, mean, scale = first_norm(x_ref[0, s, :].astype(F32), v0)
        act_s[s, :] = act
        act0[0, s, :] = act
        slx0[0, s, :] = slope
        mux0[0, s, :] = mean
        rsx0[0, s, :] = scale

    chunks(rows, 16, stage1)
    act, _, _, _ = first_norm(xh_ref[0].astype(F32), v0)
    act_s[rows : rows + 2 * RIM0, :] = act

    @pl.when(first)
    def _():
        pick_wait(nwo, nw0, sems.at[0])

    n32[...] = dot_nn(act_s[...], nw0[...])

    def mid_norm(u, v):
        normed, _, scale = normed_of(u + v.nb)
        act, slope = gelu_parts(normed * v.mg + v.ms)
        return act.astype(BF16), slope.astype(BF16), normed.astype(BF16), scale

    def stage2(r):
        s = pl.ds(r, 32)
        mid, slope, normed, scale = mid_norm(n32[s, :], v0)
        mid32[pl.ds(r + RIM0, 32), :] = mid.astype(F32)
        nn0[0, s, :] = normed
        sln0[0, s, :] = slope
        rsn0[0, s, :] = scale

    chunks(rows, 32, stage2)
    rim = mid_norm(n32[rows : rows + 2 * RIM0, :], v0)[0].astype(F32)
    mid32[0:RIM0, :] = rim[:RIM0]
    mid32[rows + RIM0 : rows + 2 * RIM0, :] = rim[RIM0:]
    near_taps(rows, inner, mid32, mk, st0.at[0])

    @pl.when(first)
    def _():
        pick_wait(cwo, cw0, sems.at[1])

    c32[...] = dot_nn(st0[0], cw0[...].reshape(TAPS * inner, inner))

    def stage4(r):
        s = pl.ds(r, 32)
        normed, _, scale = normed_of(c32[s, :] + v0.cb)
        act, slope = gelu_parts(normed * v0.lg + v0.ls)
        oa0[0, s, :] = act.astype(BF16)
        nc0[0, s, :] = normed.astype(BF16)
        slc0[0, s, :] = slope.astype(BF16)
        rsc0[0, s, :] = scale

    chunks(rows, 32, stage4)

    @pl.when(first)
    def _():
        pick_wait(wwo, ww0, sems.at[2])
        pick_wait(nwx, nw1, sems.at[3])

    r32[...] = dot_nn(oa0[0], ww0[...])

    def stage5(r):
        s = pl.ds(r, 16)
        res = (x_ref[0, s, :].astype(F32) + (r32[s, :] + v0.wb)).astype(BF16)
        out0[0, s, :] = res
        act, slope, mean, scale = first_norm(res.astype(F32), v1)
        act1[0, s, :] = act
        slx1[0, s, :] = slope
        mux1[0, s, :] = mean
        rsx1[0, s, :] = scale

    chunks(rows, 16, stage5)
    n32[0:rows, :] = dot_nn(act1[0], nw1[...])

    def stage6(r):
        s = pl.ds(r, 32)
        mid, slope, normed, scale = mid_norm(n32[s, :], v1)
        mid1[0, s, :] = mid
        nn1[0, s, :] = normed
        sln1[0, s, :] = slope
        rsn1[0, s, :] = scale

    chunks(rows, 32, stage6)


def near_taps(rows, inner, ext32, mk, dst):
    def stack(r):
        s = pl.ds(r, 16)
        window = ext32[pl.ds(r, 32), :]
        for j in range(TAPS):
            at = RIM0 + (j - MID) * DIL0
            live = mk[0, s, j : j + 1]
            dst[s, j * inner : (j + 1) * inner] = (window[at : at + 16] * live).astype(BF16)

    chunks(rows, 16, stack)


def far_taps(rows, inner, own_ref, up_ref, dn_ref, mk, dst):
    pieces = rows // DIL1
    for k in range(pieces):
        for j in range(TAPS):
            at = k + j - MID
            live = mk[0, k * DIL1 : (k + 1) * DIL1, LIVE1 + j : LIVE1 + j + 1]
            if at < 0:
                part = up_ref[0, (at + MID) * DIL1 : (at + MID + 1) * DIL1, :]
            elif at >= pieces:
                part = dn_ref[0, (at - pieces) * DIL1 : (at - pieces + 1) * DIL1, :]
            else:
                part = own_ref[0, at * DIL1 : (at + 1) * DIL1, :]
            dst[k * DIL1 : (k + 1) * DIL1, j * inner : (j + 1) * inner] = (part.astype(F32) * live).astype(BF16)


def f1_kernel(c_ref, mid_ref, up_ref, dn_ref, mk, v1_ref, cot_ref, cwo, cwx, wwo, wwx,
              st1, oa1, cg1, vec, cw1, ww1, c32, e32, acc, sems):
    low = c_ref[0] == 0
    step = pl.program_id(0)
    rows, width = cot_ref.shape[1:]
    inner = c32.shape[1]
    v1 = Vectors(v1_ref, width, inner)

    @pl.when(step == 0)
    def _():
        pick_copy(low, wwx, wwo, ww1, sems.at[1])
        pick_copy(low, cwx, cwo, cw1, sems.at[0])
        acc[...] = jnp.zeros_like(acc)

    far_taps(rows, inner, mid_ref, up_ref, dn_ref, mk, st1.at[0])
    (cot_sum,) = summed_chunks(rows, 16, width, 1, lambda r: (cot_ref[0, pl.ds(r, 16), :].astype(F32),))
    acc[3] += cot_sum

    @pl.when(step == 0)
    def _():
        pick_wait(wwx, ww1, sems.at[1])

    e32[...] = dot_nt(cot_ref[0], ww1[...])

    @pl.when(step == 0)
    def _():
        pick_wait(cwx, cw1, sems.at[0])

    c32[...] = dot_nn(st1[0], cw1[...].reshape(TAPS * inner, inner))

    def stage(r):
        s = pl.ds(r, 16)
        normed, _, scale = normed_of(c32[s, :] + v1.cb)
        act, slope = gelu_parts(normed * v1.lg + v1.ls)
        oa1[0, s, :] = act.astype(BF16)
        du, dgain, dshift = norm_back(e32[s, :], slope, normed, scale, v1.lg)
        du = du.astype(BF16)
        cg1[0, s, :] = du
        return dgain, dshift, du.astype(F32)

    sums = summed_chunks(rows, 16, inner, 3, stage)
    for k in range(3):
        acc[k, :, :inner] += sums[k]

    @pl.when(step == pl.num_programs(0) - 1)
    def _():
        vec[...] = jnp.sum(acc[...], axis=1)


def o1_kernel(c_ref, out0_ref, oa_ref, rt_ref, lm_ref, v1_ref, head_ref, wwo, wwx,
              out1, tot, ww1, r32, lg, acc, sems, *, vocab):
    low = c_ref[0] == 0
    step = pl.program_id(0)
    rows, width = out0_ref.shape[1:]
    v1 = Vectors(v1_ref, width, oa_ref.shape[2])

    @pl.when(step == 0)
    def _():
        pick_copy(low, wwx, wwo, ww1, sems.at[0])
        acc[...] = jnp.zeros_like(acc)
        pick_wait(wwx, ww1, sems.at[0])

    r32[...] = dot_nn(oa_ref[0], ww1[...])

    def stage(r):
        s = pl.ds(r, 16)
        out1[0, s, :] = (out0_ref[0, s, :].astype(F32) + (r32[s, :] + v1.wb)).astype(BF16)

    chunks(rows, 16, stage)
    lg[...] = dot_nn(out1[0], head_ref[...])
    lane = lax.broadcasted_iota(jnp.int32, (rows, LANES), 1)
    logits = jnp.where(lane < vocab, lg[...], -1e30)
    top = jnp.max(logits, axis=-1, keepdims=True)
    log_total = top + jnp.log(jnp.sum(jnp.exp(logits - top), axis=-1, keepdims=True))
    kind, weight = columns(rt_ref[0].astype(F32)), columns(lm_ref[0].astype(F32))
    onehot = jnp.where(lane == kind.astype(jnp.int32), weight, 0.0)
    acc[0] += fold8(onehot)
    acc[1] += fold8(onehot * (log_total - logits))

    @pl.when(step == pl.num_programs(0) - 1)
    def _():
        tot[...] = jnp.sum(acc[...], axis=1)


def middle_back(rows, inner, m32, sln, nn, rsn, gain, ng, acc):
    def stage(r):
        s = pl.ds(r, 16)
        du, dgain, dshift = norm_back(m32[s, :], sln[0, s, :].astype(F32), nn[0, s, :].astype(F32), rsn[0, s, :], gain)
        du = du.astype(BF16)
        ng[0, s, :] = du
        return dgain, dshift, du.astype(F32)

    sums = summed_chunks(rows, 16, inner, 3, stage)
    for k in range(3):
        acc[k] += sums[k]


def mid_kernel(c_ref, cg_ref, *refs, far, block):
    if far:
        up_ref, dn_ref, mk, v_ref, sln, nn, rsn, cwo, cwx, ng, vec, cw2, stg, m32, acc, sems = refs
    else:
        rim_ref, mk, v_ref, sln, nn, rsn, cwo, cwx, ng, vec, cw2, ext, stg, m32, acc, sems = refs
    low = c_ref[0] == block
    step = pl.program_id(0)
    rows, inner = cg_ref.shape[1:]
    parts = conv_parts(cwo, cw2)

    @pl.when(step == 0)
    def _():
        for j, dst in parts:
            pick_copy(low, cwo.at[j], cwx.at[j], dst, sems.at[j])
        acc[...] = jnp.zeros_like(acc)

    if far:
        far_taps(rows, inner, cg_ref, up_ref, dn_ref, mk, stg)
    else:
        rim = rim_ref[0].astype(F32)
        ext[0:RIM0, :] = rim[:RIM0]
        ext[rows + RIM0 : rows + 2 * RIM0, :] = rim[RIM0:]

        def widen(r):
            ext[pl.ds(r + RIM0, 16), :] = cg_ref[0, pl.ds(r, 16), :].astype(F32)

        chunks(rows, 16, widen)
        near_taps(rows, inner, ext, mk, stg)

    @pl.when(step == 0)
    def _():
        for j, dst in parts:
            pick_wait(cwo.at[j], dst, sems.at[j])

    m32[...] = dot_nt(stg[...], cw2[...])
    at = v_ref.shape[1] - 5 * inner
    middle_back(rows, inner, m32, sln, nn, rsn, v_ref[:, at : at + inner], ng, acc)

    @pl.when(step == pl.num_programs(0) - 1)
    def _():
        vec[...] = jnp.sum(acc[...], axis=1)


def first_kernel(c_ref, ng_ref, v_ref, grad, slx, src, mux, rsx, nwo, nwx, ig, vec, nw, a32, acc, sems, *, block):
    low = c_ref[0] == block
    step = pl.program_id(0)
    rows, width = grad.shape[1:]
    gain = v_ref[:, :width]

    @pl.when(step == 0)
    def _():
        pick_copy(low, nwo, nwx, nw, sems.at[0])
        acc[...] = jnp.zeros_like(acc)
        pick_wait(nwo, nw, sems.at[0])

    a32[...] = dot_nt(ng_ref[0], nw[...])

    def stage(r):
        s = pl.ds(r, 16)
        scale = rsx[0, s, :]
        normed = (src[0, s, :].astype(F32) - mux[0, s, :]) * scale
        du, dgain, dshift = norm_back(a32[s, :], slx[0, s, :].astype(F32), normed, scale, gain)
        ig[0, s, :] = (grad[0, s, :].astype(F32) + du).astype(BF16)
        return dgain, dshift

    sums = summed_chunks(rows, 16, width, 2, stage)
    for k in range(2):
        acc[k] += sums[k]

    @pl.when(step == pl.num_programs(0) - 1)
    def _():
        vec[...] = jnp.sum(acc[...], axis=1)


def last_kernel(c_ref, ig_ref, v_ref, slc, nc, rsc, wwo, wwx, cg, vec, ww, e32, acc, sems):
    low = c_ref[0] == 0
    step = pl.program_id(0)
    rows, width = ig_ref.shape[1:]
    inner = e32.shape[1]
    gain = Vectors(v_ref, width, inner).lg

    @pl.when(step == 0)
    def _():
        pick_copy(low, wwo, wwx, ww, sems.at[0])
        acc[...] = jnp.zeros_like(acc)

    (ig_sum,) = summed_chunks(rows, 16, width, 1, lambda r: (ig_ref[0, pl.ds(r, 16), :].astype(F32),))
    acc[3] += ig_sum

    @pl.when(step == 0)
    def _():
        pick_wait(wwo, ww, sems.at[0])

    e32[...] = dot_nt(ig_ref[0], ww[...])

    def stage(r):
        s = pl.ds(r, 16)
        du, dgain, dshift = norm_back(e32[s, :], slc[0, s, :].astype(F32), nc[0, s, :].astype(F32), rsc[0, s, :], gain)
        du = du.astype(BF16)
        cg[0, s, :] = du
        return dgain, dshift, du.astype(F32)

    sums = summed_chunks(rows, 16, inner, 3, stage)
    for k in range(3):
        acc[k, :, :inner] += sums[k]

    @pl.when(step == pl.num_programs(0) - 1)
    def _():
        vec[...] = jnp.sum(acc[...], axis=1)


def weight_terms(c_arr, pairs, own, tile, unit):
    specs, args, spans = [], [], []
    at = 0

    def index(v, pick):
        if v.shape[0] == own:
            return lambda s, c: (0, 0, pick(s))
        return lambda s, c: (c[0], 0, pick(s))

    for a, g in pairs:
        na, ng = a.shape[2] // tile, g.shape[2] // tile
        local = functools.partial(lambda s, lo, n: jnp.clip(s - lo, 0, n - 1), lo=at, n=na * ng)
        block = (own, a.shape[1], tile)
        specs.append(pl.BlockSpec(block, index(a, lambda s, local=local, na=na: local(s) % na)))
        specs.append(pl.BlockSpec(block, index(g, lambda s, local=local, na=na: local(s) // na)))
        args += [a, g]
        spans.append((at, at + na * ng))
        at += na * ng
    half = tile // 2
    depth = own * args[0].shape[1]
    out_rows = -(-at * half // unit) * unit

    def kernel(c_ref, *refs):
        keep, send, whole = refs[-3:]
        s = pl.program_id(0)
        for k, (lo, hi) in enumerate(spans):

            @pl.when((s >= lo) & (s < hi))
            def _(k=k):
                a, g = (refs[2 * k + i][...].reshape(depth, tile) for i in range(2))
                whole[...] = dot_tn(a, g).astype(BF16)

        stay = pl.multiple_of(c_ref[0] * half, half)
        keep[...] = whole[pl.ds(stay, half), :]
        send[...] = whole[pl.ds(half - stay, half), :]

    return pl.pallas_call(
        kernel,
        grid_spec=pltpu.PrefetchScalarGridSpec(
            num_scalar_prefetch=1,
            grid=(at,),
            in_specs=specs,
            out_specs=[pl.BlockSpec((half, tile), lambda s, c: (s, 0))] * 2,
            scratch_shapes=[pltpu.VMEM((tile, tile), BF16)],
        ),
        out_shape=[jax.ShapeDtypeStruct((out_rows, tile), BF16)] * 2,
        compiler_params=pltpu.CompilerParams(vmem_limit_bytes=VMEM_LIMIT),
        cost_estimate=pl.CostEstimate(
            flops=at * 2 * tile * tile * depth // SCALE, bytes_accessed=4 * out_rows * tile // SCALE, transcendentals=0
        ),
    )(c_arr, *args)


def unpack_kernel(c_ref, row_ref, sig_ref, *refs, groups, count, cols):
    n = sum(len(g[2]) for g in groups)
    ins, (conv, widen, narrow), (held, sems) = refs[:n], refs[n : n + 3], refs[n + 3 :]
    s = pl.program_id(0)
    half = conv.shape[1] // 2

    def fetch(k):
        _, base, numbers = groups[k]
        arrays = [ins[i] for i in numbers]
        rows = sum(a.shape[0] for a in arrays) // 2
        shard = rows // count
        first = 0
        for a in arrays:
            mine = 0 if first < count else 1
            for p in range(a.shape[0] // shard):
                h = c_ref[0] if mine == 0 else 1 - c_ref[0]
                to = pl.multiple_of(((first + p) % count ^ sig_ref[mine]) * shard + base, 16)
                pltpu.make_async_copy(a.at[pl.ds(p * shard, shard)], held.at[h, pl.ds(to, shard)], sems.at[k]).start()
            first += a.shape[0] // shard

    def landed(k):
        _, base, numbers = groups[k]
        rows = sum(ins[i].shape[0] for i in numbers) // 2
        part = held.at[:, base : base + rows]
        pltpu.make_async_copy(part, part, sems.at[k]).wait()

    @pl.when(s == 0)
    def _():
        for step in (fetch, landed):
            for k, (core, _, _) in enumerate(groups):
                if core is None:
                    step(k)
                else:
                    pl.when(c_ref[0] == core)(functools.partial(step, k))

    def rows_of(step):
        at = pl.multiple_of(row_ref[step], half)
        return held[0, pl.ds(at, half), :].astype(F32), held[1, pl.ds(at, half), :].astype(F32)

    @pl.when(s < TAPS)
    def _():
        conv[0, :half, :], conv[0, half:, :] = rows_of(s)

    @pl.when((s >= TAPS) & (s < TAPS + cols))
    def _():
        widen[:half, :], widen[half:, :] = rows_of(s)

    @pl.when(s >= TAPS + cols)
    def _():
        narrow[:half, :], narrow[half:, :] = rows_of(s)


def add_low(one, other):
    return (one.astype(F32) + other.astype(F32)).astype(BF16)


def part(v, at, rows):
    return lax.dynamic_slice_in_dim(v, at * rows, rows, 0)


def tie(value, *after):
    return lax.optimization_barrier((value, *after))[0]


def dim_orders(count):
    rest = list(range(2, count.bit_length() - 1))
    return [[0, *rest[:1], 1, *rest[1:]], [1, 0, *rest]]


class Chain:
    def __init__(self, keep, send, steps):
        self.keep, self.send, self.steps = keep, send, steps
        self.at = -1
        self.pieces = None

    def ready(self, *after):
        bits = len(self.steps)
        if after:
            self.come = tie(self.come, *after)
            if self.pieces is not None:
                self.pieces = (self.pieces[0], self.come)
        if 0 <= self.at < bits:
            bit = self.steps[self.at][1]
            rows = self.keep.shape[0] // 2
            self.send = add_low(part(self.keep, 1 - bit, rows), part(self.come, 1 - bit, rows))
            self.keep = add_low(part(self.keep, bit, rows), part(self.come, bit, rows))
        elif self.at == bits:
            self.send = add_low(self.keep, self.come)
        elif self.at > bits:
            self.send = jnp.concatenate(self.pieces, axis=0)
        return self.send

    def go(self, *after):
        send = tie(self.send, *after) if after else self.send
        bits = len(self.steps)
        if self.at < 0:
            self.come = swapped(send)
        elif self.at < bits:
            self.come = hop(send, self.steps[self.at][0])
        else:
            self.come = hop(send, self.steps[2 * bits - 1 - self.at][0])
            self.pieces = (send, self.come)
        self.at += 1
        return self.come

    def step(self, *after):
        self.ready()
        return self.go(*after)

    def done(self):
        return self.at == 2 * len(self.steps)

    def finish(self):
        while not self.done():
            self.step()
        return [*self.pieces, *(swapped(p) for p in self.pieces)]


def swapped(v):
    return lax.ppermute(v, "section", [(0, 1), (1, 0)])


def hop(v, pairs):
    return lax.ppermute(v, ("section", "dp"), pairs)


def body(block_input, output_cotangent, residues_before, residues_after, residue_types, loss_mask,
         first_gain, first_shift, narrow_weight, narrow_bias, middle_gain, middle_shift,
         conv_weight, conv_bias, last_gain, last_shift, widen_weight, widen_bias, head_weight):
    sec = lax.axis_index("section")
    at = lax.axis_index("dp")
    count = lax.axis_size("dp")
    low = sec == 0
    micro, rows, width = block_input.shape
    own = micro // 2
    inner = narrow_weight.shape[2]
    vocab = head_weight.shape[1]
    ahead = [(i, (i + 1) % count) for i in range(count)]
    behind = [((i + 1) % count, i) for i in range(count)]
    c_arr = sec.astype(jnp.int32).reshape(1)

    nwo, cwo, wwo = narrow_weight[0], conv_weight[0], widen_weight[0]
    nwx, cwx, wwx = swapped(nwo), swapped(cwo), swapped(wwo)
    packed = jnp.concatenate(
        (first_gain, first_shift, widen_bias, narrow_bias, middle_gain, middle_shift, conv_bias, last_gain, last_shift), axis=1
    )
    packed_x = swapped(packed)
    v0 = jnp.where(low, packed, packed_x)
    v1 = jnp.where(low, packed_x, packed)

    x_own = lax.dynamic_slice_in_dim(block_input, sec * own, own, 0)
    xh = jnp.concatenate(
        [lax.ppermute(x_own[:, -RIM0:], "dp", ahead), lax.ppermute(x_own[:, :RIM0], "dp", behind)], axis=1
    )
    before, after, kinds, scored = (v[:, None, :] for v in (residues_before, residues_after, residue_types, loss_mask))

    def mine(n, w):
        return pl.BlockSpec((1, n, w), lambda i, c: (c[0] * own + i, 0, 0))

    def each(n, w):
        return pl.BlockSpec((1, n, w), lambda i, c: (i, 0, 0))

    def whole(*shape):
        return pl.BlockSpec(shape, lambda i, c: (0,) * len(shape))

    def call(kernel, c, ins, in_specs, outs, scratch, flops, nbytes, trans=0):
        return pl.pallas_call(
            kernel,
            grid_spec=pltpu.PrefetchScalarGridSpec(
                num_scalar_prefetch=1,
                grid=(own,),
                in_specs=in_specs,
                out_specs=[o[1] for o in outs],
                scratch_shapes=scratch,
            ),
            out_shape=[o[0] for o in outs],
            compiler_params=pltpu.CompilerParams(vmem_limit_bytes=VMEM_LIMIT),
            cost_estimate=pl.CostEstimate(flops=int(flops / SCALE), bytes_accessed=int(nbytes / SCALE), transcendentals=0),
        )(c, *ins)

    def o_each(w, dtype=BF16):
        return (jax.ShapeDtypeStruct((own, rows, w), dtype), each(rows, w))

    def o_vec(n, w):
        return (jax.ShapeDtypeStruct((n, w), F32), whole(n, w))

    dma = pltpu.SemaphoreType.DMA
    vspec = whole(1, packed.shape[1])
    mm = 2 * own * rows * width * inner
    wide, thin, one, masks, taps = o_each(width), o_each(inner), o_each(1, F32), o_each(LANES, F32), o_each(TAPS * inner)
    e_wide, e_thin, e_one, e_masks = wide[1], thin[1], one[1], masks[1]
    id_spec = mine(1, rows)
    (mk, act0, slx0, mux0, rsx0, nn0, sln0, rsn0, st0, nc0, slc0, rsc0, oa0, out0,
     act1, slx1, mux1, rsx1, nn1, sln1, rsn1, mid1) = call(
        f0_kernel,
        c_arr,
        (block_input, xh, before, after, v0, v1, nwo, nwx, cwo, cwx, wwo, wwx),
        [mine(rows, width), each(2 * RIM0, width), id_spec, id_spec, vspec, vspec] + [ANY] * 6,
        [masks, wide, wide, one, one, thin, thin, one, taps, thin, thin, one, thin, wide, wide, wide, one, one, thin, thin, one, thin],
        [
            pltpu.VMEM((width, inner), BF16),
            pltpu.VMEM((TAPS, inner, inner), BF16),
            pltpu.VMEM((inner, width), BF16),
            pltpu.VMEM((width, inner), BF16),
            pltpu.VMEM((rows + 2 * RIM0, width), BF16),
            pltpu.VMEM((rows + 2 * RIM0, inner), F32),
            pltpu.VMEM((rows + 2 * RIM0, inner), F32),
            pltpu.VMEM((rows, inner), F32),
            pltpu.VMEM((rows, width), F32),
            dma((4,)),
        ],
        5.5 * mm, 40_000_000, own * rows * 8 * width,
    )

    up1 = lax.ppermute(mid1[:, -RIM1:], "dp", ahead)
    dn1 = lax.ppermute(mid1[:, :RIM1], "dp", behind)
    st1, oa1, cg1, vec1 = call(
        f1_kernel,
        c_arr,
        (mid1, up1, dn1, mk, v1, output_cotangent, cwo, cwx, wwo, wwx),
        [e_thin, each(RIM1, inner), each(RIM1, inner), e_masks, vspec, mine(rows, width)] + [ANY] * 4,
        [taps, thin, thin, o_vec(4, width)],
        [
            pltpu.VMEM((TAPS, inner, inner), BF16),
            pltpu.VMEM((inner, width), BF16),
            pltpu.VMEM((rows, inner), F32),
            pltpu.VMEM((rows, inner), F32),
            pltpu.VMEM((4, 8, width), F32),
            dma((2,)),
        ],
        3.5 * mm, 20_000_000, own * rows * 2 * inner,
    )

    rim_up, rim_dn = cg1[:, -RIM1:], cg1[:, :RIM1]
    upg = lax.ppermute(rim_up, "dp", ahead)
    dng = lax.ppermute(rim_dn, "dp", behind)

    orders = dim_orders(count)
    steps, signs = [], [0, 0]
    bits = len(orders[0])
    for k in range(bits):
        pairs = [(s * count + d, s * count + (d ^ (1 << orders[s][k]))) for s in range(2) for d in range(count)]
        place = [(at >> orders[s][k]) & 1 for s in range(2)]
        steps.append((pairs, jnp.where(low, place[0], place[1])))
        signs = [g + (p << (bits - 1 - k)) for g, p in zip(signs, place)]
    unit = 16 * count
    terms = functools.partial(weight_terms, own=own, tile=inner, unit=unit)

    g1 = Chain(*terms(tie(c_arr, rim_up, rim_dn), [(oa1, output_cotangent), (st1, cg1)]), steps)
    g1_come = g1.step()
    head = jnp.pad(head_weight, ((0, 0), (0, LANES - vocab)))
    out1, tot = call(
        functools.partial(o1_kernel, vocab=vocab),
        tie(c_arr, g1.keep),
        (out0, oa1, kinds, scored, v1, head, wwo, wwx),
        [e_wide, e_thin, id_spec, id_spec, vspec, whole(width, LANES), ANY, ANY],
        [wide, o_vec(2, LANES)],
        [
            pltpu.VMEM((inner, width), BF16),
            pltpu.VMEM((rows, width), F32),
            pltpu.VMEM((rows, LANES), F32),
            pltpu.VMEM((2, 8, LANES), F32),
            dma((1,)),
        ],
        1.2 * mm, 8_000_000,
    )

    def mid_scratch(ext):
        return [
            pltpu.VMEM((inner, TAPS * inner), BF16),
            *ext,
            pltpu.VMEM((rows, TAPS * inner), BF16),
            pltpu.VMEM((rows, inner), F32),
            pltpu.VMEM((3, 8, inner), F32),
            dma((TAPS,)),
        ]

    def first(c, block, ng, v, grad, grad_spec, slx, src, src_spec, mux, rsx):
        return call(
            functools.partial(first_kernel, block=block),
            c,
            (ng, v, grad, slx, src, mux, rsx, nwo, nwx),
            [e_thin, vspec, grad_spec, e_wide, src_spec, e_one, e_one, ANY, ANY],
            [wide, o_vec(2, width)],
            [pltpu.VMEM((width, inner), BF16), pltpu.VMEM((rows, width), F32), pltpu.VMEM((2, 8, width), F32), dma((1,))],
            1.3 * mm, 10_000_000,
        )

    ng1, vecm1 = call(
        functools.partial(mid_kernel, far=True, block=1),
        tie(c_arr, tot, g1.ready()),
        (cg1, upg, dng, mk, v1, sln1, nn1, rsn1, cwo, cwx),
        [e_thin, each(RIM1, inner), each(RIM1, inner), e_masks, vspec, e_thin, e_thin, e_one, ANY, ANY],
        [thin, o_vec(3, inner)],
        mid_scratch([]),
        2.6 * mm, 10_000_000,
    )
    r1 = g1.go(upg, dng, tot)
    ig1, vecf1 = first(c_arr, 1, ng1, v1, output_cotangent, mine(rows, width), slx1, out0, e_wide, mux1, rsx1)
    cg0, vecl0 = call(
        last_kernel,
        tie(c_arr, g1.ready(ig1)),
        (ig1, v0, slc0, nc0, rsc0, wwo, wwx),
        [e_wide, vspec, e_thin, e_thin, e_one, ANY, ANY],
        [thin, o_vec(4, width)],
        [pltpu.VMEM((inner, width), BF16), pltpu.VMEM((rows, inner), F32), pltpu.VMEM((4, 8, width), F32), dma((1,))],
        1.3 * mm, 8_000_000,
    )
    g1.go()
    rim_up0, rim_dn0 = cg0[:, -RIM0:], cg0[:, :RIM0]
    rim0 = jnp.concatenate([lax.ppermute(rim_up0, "dp", ahead), lax.ppermute(rim_dn0, "dp", behind)], axis=1)
    g3 = Chain(*terms(tie(c_arr, g1.ready(rim_up0), rim_up0, rim_dn0), [(st0, cg0)]), steps)
    g1.go()
    g3.step()
    g2 = Chain(*terms(tie(c_arr, g1.ready(g3.keep), g3.keep), [(act1, ng1), (oa0, ig1)]), steps)
    g1.go()
    g3.ready(g2.keep)
    g2.step()
    ng0, vecm0 = call(
        functools.partial(mid_kernel, far=False, block=0),
        tie(c_arr, g1.ready(g2.keep), g3.send, g2.keep),
        (cg0, rim0, mk, v0, sln0, nn0, rsn0, cwo, cwx),
        [e_thin, each(2 * RIM0, inner), e_masks, vspec, e_thin, e_thin, e_one, ANY, ANY],
        [thin, o_vec(3, inner)],
        mid_scratch([pltpu.VMEM((rows + 2 * RIM0, inner), F32)]),
        2.6 * mm, 10_000_000,
    )
    g1.go()
    g3.go()
    g4 = Chain(*terms(tie(c_arr, g1.ready(ng0), g3.ready(ng0), g2.ready(ng0)), [(act0, ng0)]), steps)
    g1.go()
    g3.go()
    g2.go()
    g4.step()
    ig0, vecf0 = first(
        tie(c_arr, g4.keep, g1.ready(g4.keep), g3.ready(g4.keep), g2.ready(g4.keep)),
        0, ng0, v0, ig1, e_wide, slx0, block_input, mine(rows, width), mux0, rsx0,
    )
    g1.go()
    g3.go()
    g2.go()
    while not all(g.done() for g in (g1, g3, g2, g4)):
        for g in (g1, g3, g2, g4):
            if not g.done():
                g.step()

    parts, groups, base = [], [], 0
    for core, chain in ((1, g1), (0, g3), (None, g2), (0, g4)):
        pieces = chain.finish()
        height = sum(p.shape[0] for p in pieces) // 2
        if chain is g3:
            base = 0
        groups.append((core, base, list(range(len(parts), len(parts) + len(pieces)))))
        base += height
        if chain is g3:
            base = max(base, groups[0][1] + sum(p.shape[0] for p in parts[:4]) // 2)
        parts += pieces
    half = inner // 2
    cols = width // inner
    at2, at4 = groups[2][1], groups[3][1]
    conv_rows = [k * half for k in range(TAPS)]
    row0 = conv_rows + [at2 + (cols + k) * half for k in range(cols)] + [at4 + k * half for k in range(cols)]
    row1 = [r + cols * half for r in conv_rows] + [k * half for k in range(cols)] + [at2 + k * half for k in range(cols)]
    row_arr = jnp.where(low, jnp.array(row0, jnp.int32), jnp.array(row1, jnp.int32))
    sig_arr = jnp.where(low, jnp.stack(signs), jnp.stack(signs[::-1])).astype(jnp.int32)
    conv_grad, widen_grad, narrow_grad = pl.pallas_call(
        functools.partial(unpack_kernel, groups=groups, count=count, cols=cols),
        grid_spec=pltpu.PrefetchScalarGridSpec(
            num_scalar_prefetch=3,
            grid=(TAPS + 2 * cols,),
            in_specs=[ANY] * len(parts),
            out_specs=[
                pl.BlockSpec((1, inner, inner), lambda s, *_: (jnp.minimum(s, TAPS - 1), 0, 0)),
                pl.BlockSpec((inner, inner), lambda s, *_: (0, jnp.clip(s - TAPS, 0, cols - 1))),
                pl.BlockSpec((inner, inner), lambda s, *_: (jnp.clip(s - TAPS - cols, 0, cols - 1), 0)),
            ],
            scratch_shapes=[pltpu.VMEM((2, base, inner), BF16), dma((len(groups),))],
        ),
        out_shape=[
            jax.ShapeDtypeStruct((TAPS, inner, inner), F32),
            jax.ShapeDtypeStruct((inner, width), F32),
            jax.ShapeDtypeStruct((width, inner), F32),
        ],
        compiler_params=pltpu.CompilerParams(vmem_limit_bytes=VMEM_LIMIT),
        cost_estimate=pl.CostEstimate(flops=0, bytes_accessed=25_000_000, transcendentals=0),
    )(c_arr, row_arr, sig_arr, *parts)

    def padded(v):
        return jnp.pad(v, ((0, 0), (0, width - v.shape[1])))

    terms_small = [vec1, padded(vecm1), vecf1, vecl0, padded(vecm0), vecf0, padded(tot)]
    small = jnp.concatenate(terms_small, axis=0)
    small = jnp.pad(small, ((0, -small.shape[0] % 8), (0, 0)))
    small = small + swapped(small)
    for pairs, _ in steps:
        small = small + hop(small, pairs)
    s1, sm1, sf1, sl0, sm0, sf0, st = jnp.split(small, [4, 7, 9, 13, 16, 18], axis=0)
    type_total, loss_total = st[0, :vocab], st[1, :vocab]

    def sel(in0, in1, n=width):
        return jnp.where(low, in0, in1)[None, :n]

    def gathered(in0, in1):
        keep = jnp.where(low, in0, in1)
        come = swapped(jnp.where(low, in1, in0))
        return jnp.concatenate([jnp.where(low, keep, come), jnp.where(low, come, keep)], axis=0)[None]

    return (
        gathered(out0, out1),
        gathered(ig0, ig1),
        sel(sf0[0], sf1[0]),
        sel(sf0[1], sf1[1]),
        narrow_grad[None],
        sel(sm0[2], sm1[2], inner),
        sel(sm0[0], sm1[0], inner),
        sel(sm0[1], sm1[1], inner),
        conv_grad[None],
        sel(sl0[2], s1[2], inner),
        sel(sl0[0], s1[0], inner),
        sel(sl0[1], s1[1], inner),
        widen_grad[None],
        sel(sl0[3], s1[3]),
        type_total.astype(jnp.int32),
        loss_total / jnp.maximum(type_total, 1.0),
    )


def solution(mesh):
    rows = P(None, "dp", None)
    ids = P(None, "dp")
    vec = P("section", None)
    mat = P("section", None, None)
    conv = P("section", None, None, None)
    weights = (vec, vec, mat, vec, vec, vec, conv, vec, vec, vec, mat, vec)
    grads = P("section", None, "dp", None)
    return jax.shard_map(
        body,
        mesh=mesh,
        in_specs=(rows, rows, ids, ids, ids, ids, *weights, P()),
        out_specs=(grads, grads, *weights, P(), P()),
        check_vma=False,
    )
```

```python
import functools

import jax
import jax.numpy as jnp
from jax import lax
from jax.experimental import pallas as pl
from jax.experimental.pallas import tpu as pltpu
from jax.sharding import PartitionSpec as P

TAPS = 5
MID = TAPS // 2
DIL0 = 2
DIL1 = 64
EPS = 1e-05
SCALE = 100

RIM0 = 8
RIM1 = MID * DIL1
F32 = jnp.float32
BF16 = jnp.bfloat16
LANES = 128
LIVE1 = 8
VMEM_LIMIT = 56 * 1024 * 1024
ANY = pl.BlockSpec(memory_space=pl.ANY)


def dot_nn(a, b):
    return lax.dot_general(a, b, (((1,), (0,)), ((), ())), preferred_element_type=F32)


def dot_nt(a, b):
    return lax.dot_general(a, b, (((1,), (1,)), ((), ())), preferred_element_type=F32)


def dot_tn(a, b):
    return lax.dot_general(a, b, (((0,), (0,)), ((), ())), preferred_element_type=F32)


def gelu_parts(y):
    phi_big = lax.erf(y * 0.7071067811865476) * 0.5 + 0.5
    e = jnp.exp(y * y * -0.5)
    return y * phi_big, phi_big + y * e * 0.3989422804014327


def normed_of(u):
    mean = jnp.mean(u, axis=-1, keepdims=True)
    center = u - mean
    scale = lax.rsqrt(jnp.mean(center * center, axis=-1, keepdims=True) + EPS)
    return center * scale, mean, scale


def norm_back(err, slope, normed, scale, gain):
    q = err * slope
    p = q * gain
    m1 = jnp.mean(p, axis=-1, keepdims=True)
    m2 = jnp.mean(p * normed, axis=-1, keepdims=True)
    return (p - m1 - normed * m2) * scale, q * normed, q


def fold8(v):
    return sum(v[k : k + 8] for k in range(0, v.shape[0], 8))


def chunks(rows, size, body):
    steps = rows // size
    lax.fori_loop(0, steps, lambda i, c: (body(pl.multiple_of(i * size, size)), c)[1], 0, unroll=min(8, steps))


def summed_chunks(rows, size, width, terms, body):
    steps = rows // size

    def one(i, held):
        return tuple(h + fold8(v) for h, v in zip(held, body(pl.multiple_of(i * size, size))))

    return lax.fori_loop(0, steps, one, (jnp.zeros((8, width), F32),) * terms, unroll=min(8, steps))


def pick_copy(cond, one, other, dst, sem):
    @pl.when(cond)
    def _():
        pltpu.make_async_copy(one, dst, sem).start()

    @pl.when(jnp.logical_not(cond))
    def _():
        pltpu.make_async_copy(other, dst, sem).start()


def pick_wait(one, dst, sem):
    pltpu.make_async_copy(one, dst, sem).wait()


def conv_parts(one, dst):
    inner = one.shape[1]
    return [(j, dst.at[:, (TAPS - 1 - j) * inner : (TAPS - j) * inner]) for j in range(TAPS)]


def columns(row):
    return jnp.broadcast_to(row, (LANES, row.shape[1])).T


class Vectors:
    def __init__(self, ref, width, inner):
        at = 0
        for name in ("fg", "fs", "wb"):
            setattr(self, name, ref[:, at : at + width])
            at += width
        for name in ("nb", "mg", "ms", "cb", "lg", "ls"):
            setattr(self, name, ref[:, at : at + inner])
            at += inner


def pack_kernel(*refs):
    at = 0
    for ref in refs[:-1]:
        refs[-1][:, at : at + ref.shape[1]] = ref[...]
        at += ref.shape[1]


def first_norm(u, v):
    normed, mean, scale = normed_of(u)
    act, slope = gelu_parts(normed * v.fg + v.fs)
    return act.astype(BF16), slope.astype(BF16), mean, scale


def mid_norm(u, v):
    normed, _, scale = normed_of(u + v.nb)
    act, slope = gelu_parts(normed * v.mg + v.ms)
    return act.astype(BF16), slope.astype(BF16), normed.astype(BF16), scale


def my_row(c_ref, ref):
    return ref[pl.ds(c_ref[0] * pl.num_programs(0) + pl.program_id(0), 1), :].astype(F32)


def f0_kernel(c_ref, x_ref, xh_ref, rb_ref, ra_ref, v0_ref, v1_ref, nwo, nwx, cwo, cwx, wwo, wwx,
              mk, act0, slx0, mux0, rsx0, nn0, sln0, rsn0, st0, nc0, slc0, rsc0, oa0, out0,
              act1, slx1, mux1, rsx1, nn1, sln1, rsn1, mid1, head1, tail1,
              nw0, cw0, ww0, nw1, act_s, n32, mid32, c32, r32, sems):
    low = c_ref[0] == 0
    first = pl.program_id(0) == 0
    rows, width = x_ref.shape[1:]
    inner = n32.shape[1]
    v0, v1 = Vectors(v0_ref, width, inner), Vectors(v1_ref, width, inner)

    @pl.when(first)
    def _():
        pick_copy(low, nwo, nwx, nw0, sems.at[0])
        pick_copy(low, cwo, cwx, cw0, sems.at[1])
        pick_copy(low, wwo, wwx, ww0, sems.at[2])
        pick_copy(low, nwx, nwo, nw1, sems.at[3])

    lane = lax.broadcasted_iota(jnp.int32, (rows, LANES), 1)
    offset = jnp.where(lane < LIVE1, (lane - MID) * DIL0, (lane - LIVE1 - MID) * DIL1).astype(F32)
    before, after = columns(my_row(c_ref, rb_ref)), columns(my_row(c_ref, ra_ref))
    mk[0] = jnp.where((offset >= -before) & (offset <= after), 1.0, 0.0)

    def stage1(r):
        s = pl.ds(r, 16)
        act, slope, mean, scale = first_norm(x_ref[0, s, :].astype(F32), v0)
        act_s[s, :] = act
        act0[0, s, :] = act
        slx0[0, s, :] = slope
        mux0[0, s, :] = mean
        rsx0[0, s, :] = scale

    chunks(rows, 16, stage1)
    act, _, _, _ = first_norm(xh_ref[0].astype(F32), v0)
    act_s[rows : rows + 2 * RIM0, :] = act

    @pl.when(first)
    def _():
        pick_wait(nwo, nw0, sems.at[0])

    n32[...] = dot_nn(act_s[...], nw0[...])

    def stage2(r):
        s = pl.ds(r, 32)
        mid, slope, normed, scale = mid_norm(n32[s, :], v0)
        mid32[pl.ds(r + RIM0, 32), :] = mid.astype(F32)
        nn0[0, s, :] = normed
        sln0[0, s, :] = slope
        rsn0[0, s, :] = scale

    chunks(rows, 32, stage2)
    rim = mid_norm(n32[rows : rows + 2 * RIM0, :], v0)[0].astype(F32)
    mid32[0:RIM0, :] = rim[:RIM0]
    mid32[rows + RIM0 : rows + 2 * RIM0, :] = rim[RIM0:]
    near_taps(rows, inner, mid32, mk, st0.at[0])

    @pl.when(first)
    def _():
        pick_wait(cwo, cw0, sems.at[1])

    c32[...] = dot_nn(st0[0], cw0[...].reshape(TAPS * inner, inner))

    def stage4(r):
        s = pl.ds(r, 32)
        normed, _, scale = normed_of(c32[s, :] + v0.cb)
        act, slope = gelu_parts(normed * v0.lg + v0.ls)
        oa0[0, s, :] = act.astype(BF16)
        nc0[0, s, :] = normed.astype(BF16)
        slc0[0, s, :] = slope.astype(BF16)
        rsc0[0, s, :] = scale

    chunks(rows, 32, stage4)

    @pl.when(first)
    def _():
        pick_wait(wwo, ww0, sems.at[2])
        pick_wait(nwx, nw1, sems.at[3])

    r32[...] = dot_nn(oa0[0], ww0[...])

    def stage5(r):
        s = pl.ds(r, 16)
        res = (x_ref[0, s, :].astype(F32) + (r32[s, :] + v0.wb)).astype(BF16)
        out0[0, s, :] = res
        act, slope, mean, scale = first_norm(res.astype(F32), v1)
        act1[0, s, :] = act
        slx1[0, s, :] = slope
        mux1[0, s, :] = mean
        rsx1[0, s, :] = scale

    chunks(rows, 16, stage5)
    n32[0:rows, :] = dot_nn(act1[0], nw1[...])

    def stage6(r):
        s = pl.ds(r, 32)
        mid, slope, normed, scale = mid_norm(n32[s, :], v1)
        mid1[0, s, :] = mid
        nn1[0, s, :] = normed
        sln1[0, s, :] = slope
        rsn1[0, s, :] = scale

    chunks(rows, 32, stage6)
    head1[...] = mid1[:, :RIM1]
    tail1[...] = mid1[:, rows - RIM1 :]


def near_taps(rows, inner, ext32, mk, dst):
    def stack(r):
        s = pl.ds(r, 16)
        window = ext32[pl.ds(r, 32), :]
        for j in range(TAPS):
            at = RIM0 + (j - MID) * DIL0
            live = mk[0, s, j : j + 1]
            dst[s, j * inner : (j + 1) * inner] = (window[at : at + 16] * live).astype(BF16)

    chunks(rows, 16, stack)


def far_taps(rows, inner, own_ref, up_ref, dn_ref, mk, dst):
    pieces = rows // DIL1
    for k in range(pieces):
        for j in range(TAPS):
            at = k + j - MID
            live = mk[0, k * DIL1 : (k + 1) * DIL1, LIVE1 + j : LIVE1 + j + 1]
            if at < 0:
                part = up_ref[0, (at + MID) * DIL1 : (at + MID + 1) * DIL1, :]
            elif at >= pieces:
                part = dn_ref[0, (at - pieces) * DIL1 : (at - pieces + 1) * DIL1, :]
            else:
                part = own_ref[0, at * DIL1 : (at + 1) * DIL1, :]
            dst[k * DIL1 : (k + 1) * DIL1, j * inner : (j + 1) * inner] = (part.astype(F32) * live).astype(BF16)


def f1_kernel(c_ref, mid_ref, up_ref, dn_ref, mk, v1_ref, cot_ref, cwo, cwx, wwo, wwx,
              st1, oa1, cg1, head, tail, vec, cw1, ww1, c32, e32, acc, sems):
    low = c_ref[0] == 0
    step = pl.program_id(0)
    rows, width = cot_ref.shape[1:]
    inner = c32.shape[1]
    v1 = Vectors(v1_ref, width, inner)

    @pl.when(step == 0)
    def _():
        pick_copy(low, wwx, wwo, ww1, sems.at[1])
        pick_copy(low, cwx, cwo, cw1, sems.at[0])
        acc[...] = jnp.zeros_like(acc)

    far_taps(rows, inner, mid_ref, up_ref, dn_ref, mk, st1.at[0])
    (cot_sum,) = summed_chunks(rows, 16, width, 1, lambda r: (cot_ref[0, pl.ds(r, 16), :].astype(F32),))
    acc[3] += cot_sum

    @pl.when(step == 0)
    def _():
        pick_wait(wwx, ww1, sems.at[1])

    e32[...] = dot_nt(cot_ref[0], ww1[...])

    @pl.when(step == 0)
    def _():
        pick_wait(cwx, cw1, sems.at[0])

    c32[...] = dot_nn(st1[0], cw1[...].reshape(TAPS * inner, inner))

    def stage(r):
        s = pl.ds(r, 16)
        normed, _, scale = normed_of(c32[s, :] + v1.cb)
        act, slope = gelu_parts(normed * v1.lg + v1.ls)
        oa1[0, s, :] = act.astype(BF16)
        du, dgain, dshift = norm_back(e32[s, :], slope, normed, scale, v1.lg)
        du = du.astype(BF16)
        cg1[0, s, :] = du
        return dgain, dshift, du.astype(F32)

    sums = summed_chunks(rows, 16, inner, 3, stage)
    for k in range(3):
        acc[k, :, :inner] += sums[k]
    head[...] = cg1[:, :RIM1]
    tail[...] = cg1[:, rows - RIM1 :]

    @pl.when(step == pl.num_programs(0) - 1)
    def _():
        vec[...] = jnp.sum(acc[...], axis=1)


def o1_kernel(c_ref, out0_ref, oa_ref, rt_ref, lm_ref, v1_ref, head_ref, wwo, wwx,
              out1, tot, ww1, r32, lg, acc, sems, *, vocab):
    low = c_ref[0] == 0
    step = pl.program_id(0)
    rows, width = out0_ref.shape[1:]
    v1 = Vectors(v1_ref, width, oa_ref.shape[2])

    @pl.when(step == 0)
    def _():
        pick_copy(low, wwx, wwo, ww1, sems.at[0])
        acc[...] = jnp.zeros_like(acc)
        pick_wait(wwx, ww1, sems.at[0])

    r32[...] = dot_nn(oa_ref[0], ww1[...])

    def stage(r):
        s = pl.ds(r, 16)
        out1[0, s, :] = (out0_ref[0, s, :].astype(F32) + (r32[s, :] + v1.wb)).astype(BF16)

    chunks(rows, 16, stage)
    lg[...] = dot_nn(out1[0], head_ref[...])
    lane = lax.broadcasted_iota(jnp.int32, (rows, LANES), 1)
    logits = jnp.where(lane < vocab, lg[...], -1e30)
    top = jnp.max(logits, axis=-1, keepdims=True)
    log_total = top + jnp.log(jnp.sum(jnp.exp(logits - top), axis=-1, keepdims=True))
    kind, weight = columns(my_row(c_ref, rt_ref)), columns(my_row(c_ref, lm_ref))
    onehot = jnp.where(lane == kind.astype(jnp.int32), weight, 0.0)
    acc[0] += fold8(onehot)
    acc[1] += fold8(onehot * (log_total - logits))

    @pl.when(step == pl.num_programs(0) - 1)
    def _():
        tot[...] = jnp.sum(acc[...], axis=1)


def middle_back(rows, inner, m32, sln, nn, rsn, gain, ng, acc):
    def stage(r):
        s = pl.ds(r, 16)
        du, dgain, dshift = norm_back(m32[s, :], sln[0, s, :].astype(F32), nn[0, s, :].astype(F32), rsn[0, s, :], gain)
        du = du.astype(BF16)
        ng[0, s, :] = du
        return dgain, dshift, du.astype(F32)

    sums = summed_chunks(rows, 16, inner, 3, stage)
    for k in range(3):
        acc[k] += sums[k]


def mid_kernel(c_ref, cg_ref, *refs, far, block):
    if far:
        up_ref, dn_ref, mk, v_ref, sln, nn, rsn, cwo, cwx, ng, vec, cw2, stg, m32, acc, sems = refs
    else:
        rim_ref, mk, v_ref, sln, nn, rsn, cwo, cwx, ng, vec, cw2, ext, stg, m32, acc, sems = refs
    low = c_ref[0] == block
    step = pl.program_id(0)
    rows, inner = cg_ref.shape[1:]
    parts = conv_parts(cwo, cw2)

    @pl.when(step == 0)
    def _():
        for j, dst in parts:
            pick_copy(low, cwo.at[j], cwx.at[j], dst, sems.at[j])
        acc[...] = jnp.zeros_like(acc)

    if far:
        far_taps(rows, inner, cg_ref, up_ref, dn_ref, mk, stg)
    else:
        rim = rim_ref[0].astype(F32)
        ext[0:RIM0, :] = rim[:RIM0]
        ext[rows + RIM0 : rows + 2 * RIM0, :] = rim[RIM0:]

        def widen(r):
            ext[pl.ds(r + RIM0, 16), :] = cg_ref[0, pl.ds(r, 16), :].astype(F32)

        chunks(rows, 16, widen)
        near_taps(rows, inner, ext, mk, stg)

    @pl.when(step == 0)
    def _():
        for j, dst in parts:
            pick_wait(cwo.at[j], dst, sems.at[j])

    m32[...] = dot_nt(stg[...], cw2[...])
    at = v_ref.shape[1] - 5 * inner
    middle_back(rows, inner, m32, sln, nn, rsn, v_ref[:, at : at + inner], ng, acc)

    @pl.when(step == pl.num_programs(0) - 1)
    def _():
        vec[...] = jnp.sum(acc[...], axis=1)


def first_kernel(c_ref, ng_ref, v_ref, grad, slx, src, mux, rsx, nwo, nwx, ig, vec, nw, a32, acc, sems, *, block):
    low = c_ref[0] == block
    step = pl.program_id(0)
    rows, width = grad.shape[1:]
    gain = v_ref[:, :width]

    @pl.when(step == 0)
    def _():
        pick_copy(low, nwo, nwx, nw, sems.at[0])
        acc[...] = jnp.zeros_like(acc)
        pick_wait(nwo, nw, sems.at[0])

    a32[...] = dot_nt(ng_ref[0], nw[...])

    def stage(r):
        s = pl.ds(r, 16)
        scale = rsx[0, s, :]
        normed = (src[0, s, :].astype(F32) - mux[0, s, :]) * scale
        du, dgain, dshift = norm_back(a32[s, :], slx[0, s, :].astype(F32), normed, scale, gain)
        ig[0, s, :] = (grad[0, s, :].astype(F32) + du).astype(BF16)
        return dgain, dshift

    sums = summed_chunks(rows, 16, width, 2, stage)
    for k in range(2):
        acc[k] += sums[k]

    @pl.when(step == pl.num_programs(0) - 1)
    def _():
        vec[...] = jnp.sum(acc[...], axis=1)


def last_kernel(c_ref, ig_ref, v_ref, slc, nc, rsc, wwo, wwx, cg, head, tail, vec, ww, e32, acc, sems):
    low = c_ref[0] == 0
    step = pl.program_id(0)
    rows, width = ig_ref.shape[1:]
    inner = e32.shape[1]
    gain = Vectors(v_ref, width, inner).lg

    @pl.when(step == 0)
    def _():
        pick_copy(low, wwo, wwx, ww, sems.at[0])
        acc[...] = jnp.zeros_like(acc)

    (ig_sum,) = summed_chunks(rows, 16, width, 1, lambda r: (ig_ref[0, pl.ds(r, 16), :].astype(F32),))
    acc[3] += ig_sum

    @pl.when(step == 0)
    def _():
        pick_wait(wwo, ww, sems.at[0])

    e32[...] = dot_nt(ig_ref[0], ww[...])

    def stage(r):
        s = pl.ds(r, 16)
        du, dgain, dshift = norm_back(e32[s, :], slc[0, s, :].astype(F32), nc[0, s, :].astype(F32), rsc[0, s, :], gain)
        du = du.astype(BF16)
        cg[0, s, :] = du
        return dgain, dshift, du.astype(F32)

    sums = summed_chunks(rows, 16, inner, 3, stage)
    for k in range(3):
        acc[k, :, :inner] += sums[k]
    head[0] = cg[0, : 2 * RIM0, :].astype(F32)[:RIM0].astype(BF16)
    tail[0] = cg[0, rows - 2 * RIM0 :, :].astype(F32)[RIM0:].astype(BF16)

    @pl.when(step == pl.num_programs(0) - 1)
    def _():
        vec[...] = jnp.sum(acc[...], axis=1)


def weight_terms(c_arr, pairs, own, tile, unit):
    specs, args, spans = [], [], []
    at = 0

    def index(v, pick):
        if v.shape[0] == own:
            return lambda s, c: (0, 0, pick(s))
        return lambda s, c: (c[0], 0, pick(s))

    for a, g in pairs:
        na, ng = a.shape[2] // tile, g.shape[2] // tile
        local = functools.partial(lambda s, lo, n: jnp.clip(s - lo, 0, n - 1), lo=at, n=na * ng)
        block = (own, a.shape[1], tile)
        specs.append(pl.BlockSpec(block, index(a, lambda s, local=local, na=na: local(s) % na)))
        specs.append(pl.BlockSpec(block, index(g, lambda s, local=local, na=na: local(s) // na)))
        args += [a, g]
        spans.append((at, at + na * ng))
        at += na * ng
    half = tile // 2
    depth = own * args[0].shape[1]
    out_rows = -(-at * half // unit) * unit

    def kernel(c_ref, *refs):
        keep, send, whole = refs[-3:]
        s = pl.program_id(0)
        for k, (lo, hi) in enumerate(spans):

            @pl.when((s >= lo) & (s < hi))
            def _(k=k):
                a, g = (refs[2 * k + i][...].reshape(depth, tile) for i in range(2))
                whole[...] = dot_tn(a, g).astype(BF16)

        stay = pl.multiple_of(c_ref[0] * half, half)
        keep[...] = whole[pl.ds(stay, half), :]
        send[...] = whole[pl.ds(half - stay, half), :]

    return pl.pallas_call(
        kernel,
        grid_spec=pltpu.PrefetchScalarGridSpec(
            num_scalar_prefetch=1,
            grid=(at,),
            in_specs=specs,
            out_specs=[pl.BlockSpec((half, tile), lambda s, c: (s, 0))] * 2,
            scratch_shapes=[pltpu.VMEM((tile, tile), BF16)],
        ),
        out_shape=[jax.ShapeDtypeStruct((out_rows, tile), BF16)] * 2,
        compiler_params=pltpu.CompilerParams(vmem_limit_bytes=VMEM_LIMIT),
        cost_estimate=pl.CostEstimate(
            flops=at * 2 * tile * tile * depth // SCALE, bytes_accessed=4 * out_rows * tile // SCALE, transcendentals=0
        ),
    )(c_arr, *args)


def unpack_kernel(c_ref, row_ref, sig_ref, *refs, sets, count, outs):
    n = sum(len(g[1]) for g in sets)
    ins, grads, (held, sem) = refs[:n], refs[n:-2], refs[-2:]
    s = pl.program_id(0)
    half = held.shape[2] // 2

    def fetch(numbers):
        arrays = [ins[i] for i in numbers]
        shard = held.shape[1] // count
        first = 0
        for a in arrays:
            mine = 0 if first < count else 1
            for p in range(a.shape[0] // shard):
                h = c_ref[0] if mine == 0 else 1 - c_ref[0]
                to = pl.multiple_of(((first + p) % count ^ sig_ref[mine]) * shard, 16)
                pltpu.make_async_copy(a.at[pl.ds(p * shard, shard)], held.at[h, pl.ds(to, shard)], sem).start()
            first += a.shape[0] // shard

    @pl.when(s == 0)
    def _():
        for core, numbers in sets:
            if core is None:
                fetch(numbers)
            else:
                pl.when(c_ref[0] == core)(functools.partial(fetch, numbers))
        pltpu.make_async_copy(held, held, sem).wait()

    at = pl.multiple_of(row_ref[s], half)
    for k, grad in enumerate(grads):
        last = outs[k + 1] if k + 1 < len(outs) else None

        @pl.when((s >= outs[k]) if last is None else (s >= outs[k]) & (s < last))
        def _(grad=grad):
            lead = (0,) if len(grad.shape) == 3 else ()
            for h in range(2):
                grad[(*lead, pl.ds(h * half, half), slice(None))] = held[h, pl.ds(at, half), :].astype(F32)


def add_low(one, other):
    return (one.astype(F32) + other.astype(F32)).astype(BF16)


def part(v, at, rows):
    return lax.dynamic_slice_in_dim(v, at * rows, rows, 0)


def tie(value, *after):
    return lax.optimization_barrier((value, *after))[0]


class Route:
    def __init__(self, orders, whole, sec, at, count):
        self.split = len(orders[0]) - whole
        self.steps, signs = [], [0, 0]
        for k in range(len(orders[0])):
            pairs = [(s * count + d, s * count + (d ^ (1 << orders[s][k]))) for s in range(2) for d in range(count)]
            place = [(at >> orders[s][k]) & 1 for s in range(2)]
            self.steps.append((pairs, jnp.where(sec == 0, place[0], place[1])))
            if k < self.split:
                signs = [g + (p << (self.split - 1 - k)) for g, p in zip(signs, place)]
        signs = jnp.where(sec == 0, jnp.stack(signs), jnp.stack(signs[::-1]))
        self.signs = signs.astype(jnp.int32)
        self.shards = 1 << self.split


class Chain:
    def __init__(self, keep, send, route):
        self.keep, self.send, self.route = keep, [send], route
        self.at = -1
        self.fly, self.pieces = [], []
        self.last = len(route.steps) + route.split

    def ready(self):
        bits, split = len(self.route.steps), self.route.split
        if 0 <= self.at < split:
            (come,) = self.fly
            bit = self.route.steps[self.at][1]
            rows = self.keep.shape[0] // 2
            self.send = [add_low(part(self.keep, 1 - bit, rows), part(come, 1 - bit, rows))]
            self.keep = add_low(part(self.keep, bit, rows), part(come, bit, rows))
        elif split <= self.at <= bits:
            self.keep = add_low(self.keep, self.fly[0])
            self.pieces = self.send = [self.keep]
        elif self.at > bits:
            self.pieces = self.send = [jnp.concatenate(self.pieces + self.fly, axis=0)]
        return tuple(self.send)

    def go(self):
        bits = len(self.route.steps)
        if self.at < 0:
            self.fly = [swapped(v) for v in self.send]
        else:
            step = self.at if self.at < bits else self.route.split - 1 - (self.at - bits)
            self.fly = [hop(v, self.route.steps[step][0]) for v in self.send]
        self.at += 1

    def done(self):
        return self.at == self.last

    def finish(self):
        while not self.done():
            self.ready()
            self.go()
        pieces = self.pieces + self.fly
        return pieces + [swapped(p) for p in pieces]


def meet(chains, *values):
    fly = [v for g in chains for v in g.fly]
    out = list(lax.optimization_barrier((*fly, *values)))
    for g in chains:
        g.fly, out = out[: len(g.fly)], out[len(g.fly) :]
    return out[0] if len(out) == 1 else out


def swapped(v):
    return lax.ppermute(v, "section", [(0, 1), (1, 0)])


def hop(v, pairs):
    return lax.ppermute(v, ("section", "dp"), pairs)


def body(block_input, output_cotangent, residues_before, residues_after, residue_types, loss_mask,
         first_gain, first_shift, narrow_weight, narrow_bias, middle_gain, middle_shift,
         conv_weight, conv_bias, last_gain, last_shift, widen_weight, widen_bias, head_weight):
    sec = lax.axis_index("section")
    at = lax.axis_index("dp")
    count = lax.axis_size("dp")
    low = sec == 0
    micro, rows, width = block_input.shape
    own = micro // 2
    inner = narrow_weight.shape[2]
    vocab = head_weight.shape[1]
    ahead = [(i, (i + 1) % count) for i in range(count)]
    behind = [((i + 1) % count, i) for i in range(count)]
    c_arr = sec.astype(jnp.int32).reshape(1)

    nwo, cwo, wwo = narrow_weight[0], conv_weight[0], widen_weight[0]
    nwx, cwx, wwx = swapped(nwo), swapped(cwo), swapped(wwo)
    vectors = (first_gain, first_shift, widen_bias, narrow_bias, middle_gain, middle_shift, conv_bias, last_gain, last_shift)
    packed = pl.pallas_call(
        pack_kernel, out_shape=jax.ShapeDtypeStruct((1, sum(v.shape[1] for v in vectors)), F32)
    )(*vectors)
    packed_x = swapped(packed)
    v0 = jnp.where(low, packed, packed_x)
    v1 = jnp.where(low, packed_x, packed)

    x_own = lax.dynamic_slice_in_dim(block_input, sec * own, own, 0)
    xh = jnp.concatenate(
        [lax.ppermute(x_own[:, -RIM0:], "dp", ahead), lax.ppermute(x_own[:, :RIM0], "dp", behind)], axis=1
    )

    def mine(n, w):
        return pl.BlockSpec((1, n, w), lambda i, c: (c[0] * own + i, 0, 0))

    def each(n, w):
        return pl.BlockSpec((1, n, w), lambda i, c: (i, 0, 0))

    def whole(*shape):
        return pl.BlockSpec(shape, lambda i, c: (0,) * len(shape))

    def call(kernel, c, ins, in_specs, outs, scratch, flops, nbytes, trans=0):
        return pl.pallas_call(
            kernel,
            grid_spec=pltpu.PrefetchScalarGridSpec(
                num_scalar_prefetch=1,
                grid=(own,),
                in_specs=in_specs,
                out_specs=[o[1] for o in outs],
                scratch_shapes=scratch,
            ),
            out_shape=[o[0] for o in outs],
            compiler_params=pltpu.CompilerParams(vmem_limit_bytes=VMEM_LIMIT),
            cost_estimate=pl.CostEstimate(flops=int(flops / SCALE), bytes_accessed=int(nbytes / SCALE), transcendentals=0),
        )(c, *ins)

    def o_each(w, dtype=BF16):
        return (jax.ShapeDtypeStruct((own, rows, w), dtype), each(rows, w))

    def o_vec(n, w):
        return (jax.ShapeDtypeStruct((n, w), F32), whole(n, w))

    dma = pltpu.SemaphoreType.DMA
    vspec = whole(1, packed.shape[1])
    mm = 2 * own * rows * width * inner
    wide, thin, one, masks, taps = o_each(width), o_each(inner), o_each(1, F32), o_each(LANES, F32), o_each(TAPS * inner)
    e_wide, e_thin, e_one, e_masks = wide[1], thin[1], one[1], masks[1]
    id_spec = whole(micro, rows)
    def o_rim(n):
        return (jax.ShapeDtypeStruct((own, n, inner), BF16), each(n, inner))

    (mk, act0, slx0, mux0, rsx0, nn0, sln0, rsn0, st0, nc0, slc0, rsc0, oa0, out0,
     act1, slx1, mux1, rsx1, nn1, sln1, rsn1, mid1, head1, tail1) = call(
        f0_kernel,
        c_arr,
        (block_input, xh, residues_before, residues_after, v0, v1, nwo, nwx, cwo, cwx, wwo, wwx),
        [mine(rows, width), each(2 * RIM0, width), id_spec, id_spec, vspec, vspec] + [ANY] * 6,
        [masks, wide, wide, one, one, thin, thin, one, taps, thin, thin, one, thin, wide,
         wide, wide, one, one, thin, thin, one, thin, o_rim(RIM1), o_rim(RIM1)],
        [
            pltpu.VMEM((width, inner), BF16),
            pltpu.VMEM((TAPS, inner, inner), BF16),
            pltpu.VMEM((inner, width), BF16),
            pltpu.VMEM((width, inner), BF16),
            pltpu.VMEM((rows + 2 * RIM0, width), BF16),
            pltpu.VMEM((rows + 2 * RIM0, inner), F32),
            pltpu.VMEM((rows + 2 * RIM0, inner), F32),
            pltpu.VMEM((rows, inner), F32),
            pltpu.VMEM((rows, width), F32),
            dma((4,)),
        ],
        5.5 * mm, 40_000_000,
    )

    up1 = lax.ppermute(tail1, "dp", ahead)
    dn1 = lax.ppermute(head1, "dp", behind)
    st1, oa1, cg1, rim_dn, rim_up, vec1 = call(
        f1_kernel,
        c_arr,
        (mid1, up1, dn1, mk, v1, output_cotangent, cwo, cwx, wwo, wwx),
        [e_thin, each(RIM1, inner), each(RIM1, inner), e_masks, vspec, mine(rows, width)] + [ANY] * 4,
        [taps, thin, thin, o_rim(RIM1), o_rim(RIM1), o_vec(4, width)],
        [
            pltpu.VMEM((TAPS, inner, inner), BF16),
            pltpu.VMEM((inner, width), BF16),
            pltpu.VMEM((rows, inner), F32),
            pltpu.VMEM((rows, inner), F32),
            pltpu.VMEM((4, 8, width), F32),
            dma((2,)),
        ],
        3.5 * mm, 20_000_000,
    )

    upg = lax.ppermute(rim_up, "dp", ahead)
    dng = lax.ppermute(rim_dn, "dp", behind)

    rest = list(range(2, count.bit_length() - 1))
    big = Route([[0, *rest[:1], 1, *rest[1:]], [1, 0, *rest]], 1, sec, at, count)
    unit = 16 * count
    terms = functools.partial(weight_terms, own=own, tile=inner, unit=unit)

    g1_terms = terms(tie(c_arr, rim_up, rim_dn), [(oa1, output_cotangent), (st1, cg1)])
    upg, dng, *g1_terms = meet([], upg, dng, *g1_terms)
    g1 = Chain(*g1_terms, big)
    g1.go()
    def mid_scratch(ext):
        return [
            pltpu.VMEM((inner, TAPS * inner), BF16),
            *ext,
            pltpu.VMEM((rows, TAPS * inner), BF16),
            pltpu.VMEM((rows, inner), F32),
            pltpu.VMEM((3, 8, inner), F32),
            dma((TAPS,)),
        ]

    def first(c, block, ng, v, grad, grad_spec, slx, src, src_spec, mux, rsx):
        return call(
            functools.partial(first_kernel, block=block),
            c,
            (ng, v, grad, slx, src, mux, rsx, nwo, nwx),
            [e_thin, vspec, grad_spec, e_wide, src_spec, e_one, e_one, ANY, ANY],
            [wide, o_vec(2, width)],
            [pltpu.VMEM((width, inner), BF16), pltpu.VMEM((rows, width), F32), pltpu.VMEM((2, 8, width), F32), dma((1,))],
            1.3 * mm, 10_000_000,
        )

    ng1, vecm1 = call(
        functools.partial(mid_kernel, far=True, block=1),
        c_arr,
        (cg1, upg, dng, mk, v1, sln1, nn1, rsn1, cwo, cwx),
        [e_thin, each(RIM1, inner), each(RIM1, inner), e_masks, vspec, e_thin, e_thin, e_one, ANY, ANY],
        [thin, o_vec(3, inner)],
        mid_scratch([]),
        2.6 * mm, 10_000_000,
    )
    ng1 = meet([g1], ng1)
    c_n1 = tie(c_arr, *g1.ready())
    g1.go()
    ig1, vecf1 = first(c_n1, 1, ng1, v1, output_cotangent, mine(rows, width), slx1, out0, e_wide, mux1, rsx1)
    cg0, rim_dn0, rim_up0, vecl0 = call(
        last_kernel,
        c_arr,
        (ig1, v0, slc0, nc0, rsc0, wwo, wwx),
        [e_wide, vspec, e_thin, e_thin, e_one, ANY, ANY],
        [thin, o_rim(RIM0), o_rim(RIM0), o_vec(4, width)],
        [pltpu.VMEM((inner, width), BF16), pltpu.VMEM((rows, inner), F32), pltpu.VMEM((4, 8, width), F32), dma((1,))],
        1.3 * mm, 8_000_000,
    )
    cg0, rim_dn0, rim_up0 = meet([g1], cg0, rim_dn0, rim_up0)
    up0, dn0 = lax.ppermute(rim_up0, "dp", ahead), lax.ppermute(rim_dn0, "dp", behind)
    g3_terms = terms(tie(c_arr, *g1.ready(), rim_up0, rim_dn0), [(oa0, ig1), (st0, cg0)])
    g1.go()
    up0, dn0, *g3_terms = meet([g1], up0, dn0, *g3_terms)
    rim0 = jnp.concatenate([up0, dn0], axis=1)
    g3 = Chain(*g3_terms, big)
    g3.go()
    g1.ready()
    g1.go()

    head = jnp.pad(head_weight, ((0, 0), (0, LANES - vocab)))
    out1, tot = call(
        functools.partial(o1_kernel, vocab=vocab),
        tie(c_arr, g3.keep, *g1.send),
        (out0, oa1, residue_types, loss_mask, v1, head, wwo, wwx),
        [e_wide, e_thin, id_spec, id_spec, vspec, whole(width, LANES), ANY, ANY],
        [wide, o_vec(2, LANES)],
        [
            pltpu.VMEM((inner, width), BF16),
            pltpu.VMEM((rows, width), F32),
            pltpu.VMEM((rows, LANES), F32),
            pltpu.VMEM((2, 8, LANES), F32),
            dma((1,)),
        ],
        1.2 * mm, 8_000_000,
    )

    def handed(in0, in1):
        return jnp.where(low, in0, in1), swapped(jnp.where(low, in1, in0))

    def gathered(keep, come):
        return jnp.concatenate([jnp.where(low, keep, come), jnp.where(low, come, keep)], axis=0)[None]

    held_out = handed(out0, out1)
    tot = meet([g1, g3], tot)
    g1.ready()
    ng0, vecm0 = call(
        functools.partial(mid_kernel, far=False, block=0),
        tie(c_arr, *g3.ready(), *g1.send),
        (cg0, rim0, mk, v0, sln0, nn0, rsn0, cwo, cwx),
        [e_thin, each(2 * RIM0, inner), e_masks, vspec, e_thin, e_thin, e_one, ANY, ANY],
        [thin, o_vec(3, inner)],
        mid_scratch([pltpu.VMEM((rows + 2 * RIM0, inner), F32)]),
        2.6 * mm, 10_000_000,
    )
    g1.go()
    g3.go()
    ng0 = meet([g1], ng0)
    g4_terms = terms(tie(c_arr, *g1.ready()), [(act1, ng1), (act0, ng0)])
    g1.go()
    g4_terms = meet([g1, g3], *g4_terms)
    g4 = Chain(*g4_terms, big)
    g4.go()
    ig0, vecf0 = first(
        tie(c_arr, *g1.ready(), *g3.ready()), 0, ng0, v0, ig1, e_wide, slx0, block_input, mine(rows, width), mux0, rsx0
    )
    g1.go()
    g3.go()
    ig0, vecf0 = meet([g1, g3, g4], ig0, vecf0)

    def padded(v):
        return jnp.pad(v, ((0, 0), (0, width - v.shape[1])))

    terms_small = [vec1, padded(vecm1), vecf1, vecl0, padded(vecm0), vecf0, padded(tot)]
    small = jnp.concatenate(terms_small, axis=0)
    small = jnp.pad(small, ((0, -small.shape[0] % 8), (0, 0)))
    small = small + swapped(small)
    for pairs, _ in big.steps:
        small = small + hop(small, pairs)
    s1, sm1, sf1, sl0, sm0, sf0, st = jnp.split(small, [4, 7, 9, 13, 16, 18], axis=0)
    type_total, loss_total = st[0, :vocab], st[1, :vocab]

    half = inner // 2
    cols = width // inner

    block_outputs, input_grads = gathered(*held_out), gathered(*handed(ig0, ig1))

    def unpacked(c, chains, row_arr, out_specs, out_shape, firsts):
        parts, sets = [], []
        for core, chain in chains:
            pieces = chain.finish()
            sets.append((core, list(range(len(parts), len(parts) + len(pieces)))))
            parts += pieces
        return pl.pallas_call(
            functools.partial(unpack_kernel, sets=sets, count=chain.route.shards, outs=firsts),
            grid_spec=pltpu.PrefetchScalarGridSpec(
                num_scalar_prefetch=3,
                grid=(row_arr.shape[0],),
                in_specs=[ANY] * len(parts),
                out_specs=out_specs,
                scratch_shapes=[pltpu.VMEM((2, sum(p.shape[0] for p in pieces) // 2, inner), BF16), dma(())],
            ),
            out_shape=out_shape,
            compiler_params=pltpu.CompilerParams(vmem_limit_bytes=VMEM_LIMIT),
            cost_estimate=pl.CostEstimate(flops=0, bytes_accessed=5_000_000, transcendentals=0),
        )(c, row_arr, chain.route.signs, *parts)

    widen_grad, conv_grad = unpacked(
        tie(c_arr, block_outputs, input_grads),
        [(1, g1), (0, g3)],
        jnp.arange(cols + TAPS, dtype=jnp.int32) * half,
        [
            pl.BlockSpec((inner, inner), lambda s, *_: (0, jnp.minimum(s, cols - 1))),
            pl.BlockSpec((1, inner, inner), lambda s, *_: (jnp.maximum(s - cols, 0), 0, 0)),
        ],
        [jax.ShapeDtypeStruct((inner, width), F32), jax.ShapeDtypeStruct((TAPS, inner, inner), F32)],
        [0, cols],
    )
    (narrow_grad,) = unpacked(
        tie(c_arr, conv_grad),
        [(None, g4)],
        (jnp.arange(cols, dtype=jnp.int32) + jnp.where(low, cols, 0).astype(jnp.int32)) * half,
        [pl.BlockSpec((inner, inner), lambda s, *_: (s, 0))],
        [jax.ShapeDtypeStruct((width, inner), F32)],
        [0],
    )

    def sel(in0, in1, n=width):
        return jnp.where(low, in0, in1)[None, :n]

    return (
        block_outputs,
        input_grads,
        sel(sf0[0], sf1[0]),
        sel(sf0[1], sf1[1]),
        narrow_grad[None],
        sel(sm0[2], sm1[2], inner),
        sel(sm0[0], sm1[0], inner),
        sel(sm0[1], sm1[1], inner),
        conv_grad[None],
        sel(sl0[2], s1[2], inner),
        sel(sl0[0], s1[0], inner),
        sel(sl0[1], s1[1], inner),
        widen_grad[None],
        sel(sl0[3], s1[3]),
        type_total.astype(jnp.int32),
        loss_total / jnp.maximum(type_total, 1.0),
    )


def solution(mesh):
    rows = P(None, "dp", None)
    ids = P(None, "dp")
    vec = P("section", None)
    mat = P("section", None, None)
    conv = P("section", None, None, None)
    weights = (vec, vec, mat, vec, vec, vec, conv, vec, vec, vec, mat, vec)
    grads = P("section", None, "dp", None)
    return jax.shard_map(
        body,
        mesh=mesh,
        in_specs=(rows, rows, ids, ids, ids, ids, *weights, P()),
        out_specs=(grads, grads, *weights, P(), P()),
        check_vma=False,
    )
```

```python
import functools

import jax
import jax.numpy as jnp
from jax import lax
from jax.experimental import pallas as pl
from jax.experimental.pallas import tpu as pltpu
from jax.sharding import PartitionSpec as P

TAPS = 5
MID = TAPS // 2
DIL0 = 2
DIL1 = 64
EPS = 1e-05
SCALE = 100

RIM0 = 8
RIM1 = MID * DIL1
F32 = jnp.float32
BF16 = jnp.bfloat16
LANES = 128
LIVE1 = 8
VMEM_LIMIT = 56 * 1024 * 1024
ANY = pl.BlockSpec(memory_space=pl.ANY)


def dot_nn(a, b):
    return lax.dot_general(a, b, (((1,), (0,)), ((), ())), preferred_element_type=F32)


def dot_nt(a, b):
    return lax.dot_general(a, b, (((1,), (1,)), ((), ())), preferred_element_type=F32)


def dot_tn(a, b):
    return lax.dot_general(a, b, (((0,), (0,)), ((), ())), preferred_element_type=F32)


def gelu_parts(y):
    phi_big = lax.erf(y * 0.7071067811865476) * 0.5 + 0.5
    e = jnp.exp(y * y * -0.5)
    return y * phi_big, phi_big + y * e * 0.3989422804014327


def normed_of(u):
    mean = jnp.mean(u, axis=-1, keepdims=True)
    center = u - mean
    scale = lax.rsqrt(jnp.mean(center * center, axis=-1, keepdims=True) + EPS)
    return center * scale, mean, scale


def norm_back(err, slope, normed, scale, gain):
    q = err * slope
    p = q * gain
    m1 = jnp.mean(p, axis=-1, keepdims=True)
    m2 = jnp.mean(p * normed, axis=-1, keepdims=True)
    return (p - m1 - normed * m2) * scale, q * normed, q


def fold8(v):
    return sum(v[k : k + 8] for k in range(0, v.shape[0], 8))


def chunks(rows, size, body):
    steps = rows // size
    lax.fori_loop(0, steps, lambda i, c: (body(pl.multiple_of(i * size, size)), c)[1], 0, unroll=min(8, steps))


def summed_chunks(rows, size, width, terms, body):
    steps = rows // size

    def one(i, held):
        return tuple(h + fold8(v) for h, v in zip(held, body(pl.multiple_of(i * size, size))))

    return lax.fori_loop(0, steps, one, (jnp.zeros((8, width), F32),) * terms, unroll=min(8, steps))


def pick_copy(cond, one, other, dst, sem):
    @pl.when(cond)
    def _():
        pltpu.make_async_copy(one, dst, sem).start()

    @pl.when(jnp.logical_not(cond))
    def _():
        pltpu.make_async_copy(other, dst, sem).start()


def pick_wait(one, dst, sem):
    pltpu.make_async_copy(one, dst, sem).wait()


def conv_parts(one, dst):
    inner = one.shape[1]
    return [(j, dst.at[:, (TAPS - 1 - j) * inner : (TAPS - j) * inner]) for j in range(TAPS)]


def columns(row):
    return jnp.broadcast_to(row, (LANES, row.shape[1])).T


class Vectors:
    def __init__(self, ref, width, inner):
        at = 0
        for name in ("fg", "fs", "wb"):
            setattr(self, name, ref[:, at : at + width])
            at += width
        for name in ("nb", "mg", "ms", "cb", "lg", "ls"):
            setattr(self, name, ref[:, at : at + inner])
            at += inner


def stack_kernel(*refs):
    at = 0
    refs[-1][...] = jnp.zeros_like(refs[-1])
    for ref in refs[:-1]:
        refs[-1][at : at + ref.shape[0], : ref.shape[1]] = ref[...]
        at += ref.shape[0]


def pack_kernel(*refs):
    at = 0
    for ref in refs[:-1]:
        refs[-1][:, at : at + ref.shape[1]] = ref[...]
        at += ref.shape[1]


def first_norm(u, v):
    normed, mean, scale = normed_of(u)
    act, slope = gelu_parts(normed * v.fg + v.fs)
    return act.astype(BF16), slope.astype(BF16), mean, scale


def mid_norm(u, v):
    normed, _, scale = normed_of(u + v.nb)
    act, slope = gelu_parts(normed * v.mg + v.ms)
    return act.astype(BF16), slope.astype(BF16), normed.astype(BF16), scale


def my_row(c_ref, ref):
    return ref[pl.ds(c_ref[0] * pl.num_programs(0) + pl.program_id(0), 1), :].astype(F32)


def f0_kernel(c_ref, x_ref, xh_ref, rb_ref, ra_ref, v0_ref, v1_ref, nwo, nwx, cwo, cwx, wwo, wwx,
              mk, act0, slx0, mux0, rsx0, nn0, sln0, rsn0, st0, nc0, slc0, rsc0, oa0, out0,
              act1, slx1, mux1, rsx1, nn1, sln1, rsn1, mid1, head1, tail1,
              nw0, cw0, ww0, nw1, act_s, n32, mid32, c32, r32, sems):
    low = c_ref[0] == 0
    first = pl.program_id(0) == 0
    rows, width = x_ref.shape[1:]
    inner = n32.shape[1]
    v0, v1 = Vectors(v0_ref, width, inner), Vectors(v1_ref, width, inner)

    @pl.when(first)
    def _():
        pick_copy(low, nwo, nwx, nw0, sems.at[0])
        pick_copy(low, cwo, cwx, cw0, sems.at[1])
        pick_copy(low, wwo, wwx, ww0, sems.at[2])
        pick_copy(low, nwx, nwo, nw1, sems.at[3])

    lane = lax.broadcasted_iota(jnp.int32, (rows, LANES), 1)
    offset = jnp.where(lane < LIVE1, (lane - MID) * DIL0, (lane - LIVE1 - MID) * DIL1).astype(F32)
    before, after = columns(my_row(c_ref, rb_ref)), columns(my_row(c_ref, ra_ref))
    mk[0] = jnp.where((offset >= -before) & (offset <= after), 1.0, 0.0)

    def stage1(r):
        s = pl.ds(r, 16)
        act, slope, mean, scale = first_norm(x_ref[0, s, :].astype(F32), v0)
        act_s[s, :] = act
        act0[0, s, :] = act
        slx0[0, s, :] = slope
        mux0[0, s, :] = mean
        rsx0[0, s, :] = scale

    chunks(rows, 16, stage1)
    act, _, _, _ = first_norm(xh_ref[0].astype(F32), v0)
    act_s[rows : rows + 2 * RIM0, :] = act

    @pl.when(first)
    def _():
        pick_wait(nwo, nw0, sems.at[0])

    n32[...] = dot_nn(act_s[...], nw0[...])

    def stage2(r):
        s = pl.ds(r, 32)
        mid, slope, normed, scale = mid_norm(n32[s, :], v0)
        mid32[pl.ds(r + RIM0, 32), :] = mid.astype(F32)
        nn0[0, s, :] = normed
        sln0[0, s, :] = slope
        rsn0[0, s, :] = scale

    chunks(rows, 32, stage2)
    rim = mid_norm(n32[rows : rows + 2 * RIM0, :], v0)[0].astype(F32)
    mid32[0:RIM0, :] = rim[:RIM0]
    mid32[rows + RIM0 : rows + 2 * RIM0, :] = rim[RIM0:]
    near_taps(rows, inner, mid32, mk, st0.at[0])

    @pl.when(first)
    def _():
        pick_wait(cwo, cw0, sems.at[1])

    c32[...] = dot_nn(st0[0], cw0[...].reshape(TAPS * inner, inner))

    def stage4(r):
        s = pl.ds(r, 32)
        normed, _, scale = normed_of(c32[s, :] + v0.cb)
        act, slope = gelu_parts(normed * v0.lg + v0.ls)
        oa0[0, s, :] = act.astype(BF16)
        nc0[0, s, :] = normed.astype(BF16)
        slc0[0, s, :] = slope.astype(BF16)
        rsc0[0, s, :] = scale

    chunks(rows, 32, stage4)

    @pl.when(first)
    def _():
        pick_wait(wwo, ww0, sems.at[2])
        pick_wait(nwx, nw1, sems.at[3])

    r32[...] = dot_nn(oa0[0], ww0[...])

    def stage5(r):
        s = pl.ds(r, 16)
        res = (x_ref[0, s, :].astype(F32) + (r32[s, :] + v0.wb)).astype(BF16)
        out0[0, s, :] = res
        act, slope, mean, scale = first_norm(res.astype(F32), v1)
        act1[0, s, :] = act
        slx1[0, s, :] = slope
        mux1[0, s, :] = mean
        rsx1[0, s, :] = scale

    chunks(rows, 16, stage5)
    n32[0:rows, :] = dot_nn(act1[0], nw1[...])

    def stage6(r):
        s = pl.ds(r, 32)
        mid, slope, normed, scale = mid_norm(n32[s, :], v1)
        mid1[0, s, :] = mid
        nn1[0, s, :] = normed
        sln1[0, s, :] = slope
        rsn1[0, s, :] = scale

    chunks(rows, 32, stage6)
    head1[...] = mid1[:, :RIM1]
    tail1[...] = mid1[:, rows - RIM1 :]


def near_taps(rows, inner, ext32, mk, dst):
    def stack(r):
        s = pl.ds(r, 16)
        window = ext32[pl.ds(r, 32), :]
        for j in range(TAPS):
            at = RIM0 + (j - MID) * DIL0
            live = mk[0, s, j : j + 1]
            dst[s, j * inner : (j + 1) * inner] = (window[at : at + 16] * live).astype(BF16)

    chunks(rows, 16, stack)


def far_taps(rows, inner, own_ref, up_ref, dn_ref, mk, dst):
    pieces = rows // DIL1
    for k in range(pieces):
        for j in range(TAPS):
            at = k + j - MID
            if up_ref is None and (k < MID and j < MID or k >= pieces - MID and j > MID):
                dst[k * DIL1 : (k + 1) * DIL1, j * inner : (j + 1) * inner] = jnp.zeros((DIL1, inner), BF16)
                continue
            live = mk[0, k * DIL1 : (k + 1) * DIL1, LIVE1 + j : LIVE1 + j + 1]
            if at < 0:
                part = up_ref[0, (at + MID) * DIL1 : (at + MID + 1) * DIL1, :]
            elif at >= pieces:
                part = dn_ref[0, (at - pieces) * DIL1 : (at - pieces + 1) * DIL1, :]
            else:
                part = own_ref[0, at * DIL1 : (at + 1) * DIL1, :]
            dst[k * DIL1 : (k + 1) * DIL1, j * inner : (j + 1) * inner] = (part.astype(F32) * live).astype(BF16)


def e1_kernel(c_ref, mid_ref, mk, cot_ref, cwo, cwx, wwo, wwx, cpart, epart, vec, cw1, ww1, st, acc, sems):
    low = c_ref[0] == 0
    step = pl.program_id(0)
    rows, width = cot_ref.shape[1:]
    inner = mid_ref.shape[2]

    @pl.when(step == 0)
    def _():
        pick_copy(low, wwx, wwo, ww1, sems.at[1])
        pick_copy(low, cwx, cwo, cw1, sems.at[0])
        acc[...] = jnp.zeros_like(acc)

    far_taps(rows, inner, mid_ref, None, None, mk, st)
    (cot_sum,) = summed_chunks(rows, 16, width, 1, lambda r: (cot_ref[0, pl.ds(r, 16), :].astype(F32),))
    acc[...] += cot_sum

    @pl.when(step == 0)
    def _():
        pick_wait(wwx, ww1, sems.at[1])

    epart[0] = dot_nt(cot_ref[0], ww1[...])

    @pl.when(step == 0)
    def _():
        pick_wait(cwx, cw1, sems.at[0])

    cpart[0] = dot_nn(st[...], cw1[...].reshape(TAPS * inner, inner))

    @pl.when(step == pl.num_programs(0) - 1)
    def _():
        vec[...] = jnp.sum(acc[...], axis=0, keepdims=True)


def f1_kernel(c_ref, mid_ref, up_ref, dn_ref, mk, v1_ref, cpart, epart, cwo, cwx,
              st1, oa1, cg1, head, tail, vec, cw1, c32, acc, sems):
    low = c_ref[0] == 0
    step = pl.program_id(0)
    rows, inner = mid_ref.shape[1:]
    width = (v1_ref.shape[1] - 6 * inner) // 3
    v1 = Vectors(v1_ref, width, inner)

    @pl.when(step == 0)
    def _():
        pick_copy(low, cwx, cwo, cw1, sems.at[0])
        acc[...] = jnp.zeros_like(acc)

    far_taps(rows, inner, mid_ref, up_ref, dn_ref, mk, st1.at[0])

    @pl.when(step == 0)
    def _():
        pick_wait(cwx, cw1, sems.at[0])

    side = MID * inner
    first, last = cw1[:MID].reshape(side, inner), cw1[MID + 1 :].reshape(side, inner)
    c32[...] = cpart[0]
    c32[:RIM1, :] += dot_nn(st1[0, :RIM1, :side], first)
    c32[rows - RIM1 :, :] += dot_nn(st1[0, rows - RIM1 :, side + inner :], last)

    def stage(r):
        s = pl.ds(r, 16)
        normed, _, scale = normed_of(c32[s, :] + v1.cb)
        act, slope = gelu_parts(normed * v1.lg + v1.ls)
        oa1[0, s, :] = act.astype(BF16)
        du, dgain, dshift = norm_back(epart[0, s, :], slope, normed, scale, v1.lg)
        du = du.astype(BF16)
        cg1[0, s, :] = du
        return dgain, dshift, du.astype(F32)

    sums = summed_chunks(rows, 16, inner, 3, stage)
    for k in range(3):
        acc[k] += sums[k]
    head[...] = cg1[:, :RIM1]
    tail[...] = cg1[:, rows - RIM1 :]

    @pl.when(step == pl.num_programs(0) - 1)
    def _():
        vec[...] = jnp.sum(acc[...], axis=1)


def o1_kernel(c_ref, out0_ref, oa_ref, rt_ref, lm_ref, v1_ref, head_ref, wwo, wwx,
              out1, tot, ww1, r32, lg, acc, sems, *, vocab):
    low = c_ref[0] == 0
    step = pl.program_id(0)
    rows, width = out0_ref.shape[1:]
    v1 = Vectors(v1_ref, width, oa_ref.shape[2])

    @pl.when(step == 0)
    def _():
        pick_copy(low, wwx, wwo, ww1, sems.at[0])
        acc[...] = jnp.zeros_like(acc)
        pick_wait(wwx, ww1, sems.at[0])

    r32[...] = dot_nn(oa_ref[0], ww1[...])

    def stage(r):
        s = pl.ds(r, 16)
        out1[0, s, :] = (out0_ref[0, s, :].astype(F32) + (r32[s, :] + v1.wb)).astype(BF16)

    chunks(rows, 16, stage)
    lg[...] = dot_nn(out1[0], head_ref[...])
    lane = lax.broadcasted_iota(jnp.int32, (rows, LANES), 1)
    logits = jnp.where(lane < vocab, lg[...], -1e30)
    top = jnp.max(logits, axis=-1, keepdims=True)
    log_total = top + jnp.log(jnp.sum(jnp.exp(logits - top), axis=-1, keepdims=True))
    kind, weight = columns(my_row(c_ref, rt_ref)), columns(my_row(c_ref, lm_ref))
    onehot = jnp.where(lane == kind.astype(jnp.int32), weight, 0.0)
    acc[0] += fold8(onehot)
    acc[1] += fold8(onehot * (log_total - logits))

    @pl.when(step == pl.num_programs(0) - 1)
    def _():
        tot[...] = jnp.sum(acc[...], axis=1)


def middle_back(rows, inner, m32, sln, nn, rsn, gain, ng, acc):
    def stage(r):
        s = pl.ds(r, 16)
        du, dgain, dshift = norm_back(m32[s, :], sln[0, s, :].astype(F32), nn[0, s, :].astype(F32), rsn[0, s, :], gain)
        du = du.astype(BF16)
        ng[0, s, :] = du
        return dgain, dshift, du.astype(F32)

    sums = summed_chunks(rows, 16, inner, 3, stage)
    for k in range(3):
        acc[k] += sums[k]


def mid_kernel(c_ref, cg_ref, *refs, far, block):
    if far:
        up_ref, dn_ref, mk, v_ref, sln, nn, rsn, cwo, cwx, ng, vec, cw2, stg, m32, acc, sems = refs
    else:
        rim_ref, mk, v_ref, sln, nn, rsn, cwo, cwx, ng, vec, cw2, ext, stg, m32, acc, sems = refs
    low = c_ref[0] == block
    step = pl.program_id(0)
    rows, inner = cg_ref.shape[1:]
    parts = conv_parts(cwo, cw2)

    @pl.when(step == 0)
    def _():
        for j, dst in parts:
            pick_copy(low, cwo.at[j], cwx.at[j], dst, sems.at[j])
        acc[...] = jnp.zeros_like(acc)

    if far:
        far_taps(rows, inner, cg_ref, up_ref, dn_ref, mk, stg)
    else:
        rim = rim_ref[0].astype(F32)
        ext[0:RIM0, :] = rim[:RIM0]
        ext[rows + RIM0 : rows + 2 * RIM0, :] = rim[RIM0:]

        def widen(r):
            ext[pl.ds(r + RIM0, 16), :] = cg_ref[0, pl.ds(r, 16), :].astype(F32)

        chunks(rows, 16, widen)
        near_taps(rows, inner, ext, mk, stg)

    @pl.when(step == 0)
    def _():
        for j, dst in parts:
            pick_wait(cwo.at[j], dst, sems.at[j])

    m32[...] = dot_nt(stg[...], cw2[...])
    at = v_ref.shape[1] - 5 * inner
    middle_back(rows, inner, m32, sln, nn, rsn, v_ref[:, at : at + inner], ng, acc)

    @pl.when(step == pl.num_programs(0) - 1)
    def _():
        vec[...] = jnp.sum(acc[...], axis=1)


def first_kernel(c_ref, ng_ref, v_ref, grad, slx, src, mux, rsx, nwo, nwx, ig, vec, nw, a32, acc, sems, *, block):
    low = c_ref[0] == block
    step = pl.program_id(0)
    rows, width = grad.shape[1:]
    gain = v_ref[:, :width]

    @pl.when(step == 0)
    def _():
        pick_copy(low, nwo, nwx, nw, sems.at[0])
        acc[...] = jnp.zeros_like(acc)
        pick_wait(nwo, nw, sems.at[0])

    a32[...] = dot_nt(ng_ref[0], nw[...])

    def stage(r):
        s = pl.ds(r, 16)
        scale = rsx[0, s, :]
        normed = (src[0, s, :].astype(F32) - mux[0, s, :]) * scale
        du, dgain, dshift = norm_back(a32[s, :], slx[0, s, :].astype(F32), normed, scale, gain)
        ig[0, s, :] = (grad[0, s, :].astype(F32) + du).astype(BF16)
        return dgain, dshift

    sums = summed_chunks(rows, 16, width, 2, stage)
    for k in range(2):
        acc[k] += sums[k]

    @pl.when(step == pl.num_programs(0) - 1)
    def _():
        vec[...] = jnp.sum(acc[...], axis=1)


def joint_kernel(c_ref, ng_ref, v1_ref, grad, slx, src, mux, rsx, v0_ref, slc, nc, rsc, nwo, nwx, wwo, wwx,
                 ig, cg, head, tail, vecf, vecl, nw, ww, a32, e32, accf, accl, sems):
    low = c_ref[0] == 0
    step = pl.program_id(0)
    rows, width = grad.shape[1:]
    inner = e32.shape[1]
    first_gain, last_gain = v1_ref[:, :width], Vectors(v0_ref, width, inner).lg

    @pl.when(step == 0)
    def _():
        pick_copy(low, nwx, nwo, nw, sems.at[0])
        pick_copy(low, wwo, wwx, ww, sems.at[1])
        accf[...] = jnp.zeros_like(accf)
        accl[...] = jnp.zeros_like(accl)
        pick_wait(nwx, nw, sems.at[0])

    a32[...] = dot_nt(ng_ref[0], nw[...])

    def stage(r):
        s = pl.ds(r, 16)
        scale = rsx[0, s, :]
        normed = (src[0, s, :].astype(F32) - mux[0, s, :]) * scale
        du, dgain, dshift = norm_back(a32[s, :], slx[0, s, :].astype(F32), normed, scale, first_gain)
        out = (grad[0, s, :].astype(F32) + du).astype(BF16)
        ig[0, s, :] = out
        return dgain, dshift, out.astype(F32)

    sums = summed_chunks(rows, 16, width, 3, stage)
    accf[0] += sums[0]
    accf[1] += sums[1]
    accl[3] += sums[2]

    @pl.when(step == 0)
    def _():
        pick_wait(wwo, ww, sems.at[1])

    e32[...] = dot_nt(ig[0], ww[...])

    def stage2(r):
        s = pl.ds(r, 16)
        du, dgain, dshift = norm_back(
            e32[s, :], slc[0, s, :].astype(F32), nc[0, s, :].astype(F32), rsc[0, s, :], last_gain
        )
        du = du.astype(BF16)
        cg[0, s, :] = du
        return dgain, dshift, du.astype(F32)

    sums = summed_chunks(rows, 16, inner, 3, stage2)
    for k in range(3):
        accl[k, :, :inner] += sums[k]
    head[0] = cg[0, : 2 * RIM0, :].astype(F32)[:RIM0].astype(BF16)
    tail[0] = cg[0, rows - 2 * RIM0 :, :].astype(F32)[RIM0:].astype(BF16)

    @pl.when(step == pl.num_programs(0) - 1)
    def _():
        vecf[...] = jnp.sum(accf[...], axis=1)
        vecl[...] = jnp.sum(accl[...], axis=1)


def weight_terms(c_arr, pairs, own, tile, unit):
    specs, args, spans = [], [], []
    at = 0

    def index(v, pick):
        if v.shape[0] == own:
            return lambda s, c: (0, 0, pick(s))
        return lambda s, c: (c[0], 0, pick(s))

    for a, g in pairs:
        na, ng = a.shape[2] // tile, g.shape[2] // tile
        local = functools.partial(lambda s, lo, n: jnp.clip(s - lo, 0, n - 1), lo=at, n=na * ng)
        block = (own, a.shape[1], tile)
        specs.append(pl.BlockSpec(block, index(a, lambda s, local=local, na=na: local(s) % na)))
        specs.append(pl.BlockSpec(block, index(g, lambda s, local=local, na=na: local(s) // na)))
        args += [a, g]
        spans.append((at, at + na * ng))
        at += na * ng
    half = tile // 2
    depth = own * args[0].shape[1]
    out_rows = -(-at * half // unit) * unit

    def kernel(c_ref, *refs):
        keep, send, whole = refs[-3:]
        s = pl.program_id(0)
        for k, (lo, hi) in enumerate(spans):

            @pl.when((s >= lo) & (s < hi))
            def _(k=k):
                a, g = (refs[2 * k + i][...].reshape(depth, tile) for i in range(2))
                whole[...] = dot_tn(a, g).astype(BF16)

        stay = pl.multiple_of(c_ref[0] * half, half)
        keep[...] = whole[pl.ds(stay, half), :]
        send[...] = whole[pl.ds(half - stay, half), :]

    return pl.pallas_call(
        kernel,
        grid_spec=pltpu.PrefetchScalarGridSpec(
            num_scalar_prefetch=1,
            grid=(at,),
            in_specs=specs,
            out_specs=[pl.BlockSpec((half, tile), lambda s, c: (s, 0))] * 2,
            scratch_shapes=[pltpu.VMEM((tile, tile), BF16)],
        ),
        out_shape=[jax.ShapeDtypeStruct((out_rows, tile), BF16)] * 2,
        compiler_params=pltpu.CompilerParams(vmem_limit_bytes=VMEM_LIMIT),
        cost_estimate=pl.CostEstimate(
            flops=at * 2 * tile * tile * depth // SCALE, bytes_accessed=4 * out_rows * tile // SCALE, transcendentals=0
        ),
    )(c_arr, *args)


def unpack_kernel(c_ref, row_ref, sig_ref, *refs, sets, shards, outs):
    n = sum(len(g[1]) for g in sets)
    ins, grads, (held, sems) = refs[:n], refs[n:-2], refs[-2:]
    s = pl.program_id(0)
    half = grads[0].shape[0] // 2

    def fetch(numbers, base, sem):
        sign = 2 * sem
        arrays = [ins[i] for i in numbers]
        shard = sum(a.shape[0] for a in arrays) // (2 * shards)
        first = 0
        for a in arrays:
            mine = 0 if first < shards else 1
            for p in range(a.shape[0] // shard):
                h = c_ref[0] if mine == 0 else 1 - c_ref[0]
                to = pl.multiple_of(((first + p) % shards ^ sig_ref[sign + mine]) * shard + base, 16)
                pltpu.make_async_copy(a.at[pl.ds(p * shard, shard)], held.at[h, pl.ds(to, shard)], sems.at[sem]).start()
            first += a.shape[0] // shard

    def landed(numbers, base, sem):
        part = held.at[:, base : base + sum(ins[i].shape[0] for i in numbers) // 2]
        pltpu.make_async_copy(part, part, sems.at[sem]).wait()

    @pl.when(s == 0)
    def _():
        for core, numbers, base, sem, _ in sets:
            if core is None:
                fetch(numbers, base, sem)
            else:
                pl.when(c_ref[0] == core)(functools.partial(fetch, numbers, base, sem))

    for core, numbers, base, sem, step in sets:
        if core != 0:
            pl.when(s == step)(functools.partial(landed, numbers, base, sem))

    at = pl.multiple_of(row_ref[s], half)
    for k, grad in enumerate(grads):
        last = outs[k + 1] if k + 1 < len(outs) else None

        @pl.when((s >= outs[k]) if last is None else (s >= outs[k]) & (s < last))
        def _(grad=grad):
            lead = (0,) if len(grad.shape) == 3 else ()
            for h in range(2):
                grad[(*lead, pl.ds(h * half, half), slice(None))] = held[h, pl.ds(at, half), :].astype(F32)


def add_low(one, other):
    return (one.astype(F32) + other.astype(F32)).astype(BF16)


def part(v, at, rows):
    return lax.dynamic_slice_in_dim(v, at * rows, rows, 0)


def tie(value, *after):
    return lax.optimization_barrier((value, *after))[0]


class Route:
    def __init__(self, orders, whole, sec, at, count):
        self.split = len(orders[0]) - whole
        self.steps, signs = [], [0, 0]
        for k in range(len(orders[0])):
            pairs = [(s * count + d, s * count + (d ^ (1 << orders[s][k]))) for s in range(2) for d in range(count)]
            place = [(at >> orders[s][k]) & 1 for s in range(2)]
            self.steps.append((pairs, jnp.where(sec == 0, place[0], place[1])))
            if k < self.split:
                signs = [g + (p << (self.split - 1 - k)) for g, p in zip(signs, place)]
        signs = jnp.where(sec == 0, jnp.stack(signs), jnp.stack(signs[::-1]))
        self.signs = signs.astype(jnp.int32)
        self.shards = 1 << self.split


class Chain:
    def __init__(self, keep, send, route):
        self.keep, self.send, self.route = keep, [send], route
        self.at = -1
        self.fly, self.pieces = [], []
        self.last = len(route.steps) + route.split

    def ready(self):
        bits, split = len(self.route.steps), self.route.split
        if 0 <= self.at < split:
            (come,) = self.fly
            bit = self.route.steps[self.at][1]
            rows = self.keep.shape[0] // 2
            self.send = [add_low(part(self.keep, 1 - bit, rows), part(come, 1 - bit, rows))]
            self.keep = add_low(part(self.keep, bit, rows), part(come, bit, rows))
        elif split <= self.at <= bits:
            self.keep = add_low(self.keep, self.fly[0])
            self.pieces = self.send = [self.keep]
        elif self.at > bits:
            self.pieces = self.send = [jnp.concatenate(self.pieces + self.fly, axis=0)]
        return tuple(self.send)

    def go(self):
        bits = len(self.route.steps)
        if self.at < 0:
            self.fly = [swapped(v) for v in self.send]
        else:
            step = self.at if self.at < bits else self.route.split - 1 - (self.at - bits)
            self.fly = [hop(v, self.route.steps[step][0]) for v in self.send]
        self.at += 1

    def done(self):
        return self.at == self.last

    def finish(self):
        while not self.done():
            self.ready()
            self.go()
        pieces = self.pieces + self.fly
        return pieces + [swapped(p) for p in pieces]


def meet(chains, *values):
    fly = [v for g in chains for v in g.fly]
    out = list(lax.optimization_barrier((*fly, *values)))
    for g in chains:
        g.fly, out = out[: len(g.fly)], out[len(g.fly) :]
    return out[0] if len(out) == 1 else out


def swapped(v):
    return lax.ppermute(v, "section", [(0, 1), (1, 0)])


def hop(v, pairs):
    return lax.ppermute(v, ("section", "dp"), pairs)


def body(block_input, output_cotangent, residues_before, residues_after, residue_types, loss_mask,
         first_gain, first_shift, narrow_weight, narrow_bias, middle_gain, middle_shift,
         conv_weight, conv_bias, last_gain, last_shift, widen_weight, widen_bias, head_weight):
    sec = lax.axis_index("section")
    at = lax.axis_index("dp")
    count = lax.axis_size("dp")
    low = sec == 0
    micro, rows, width = block_input.shape
    own = micro // 2
    inner = narrow_weight.shape[2]
    vocab = head_weight.shape[1]
    ahead = [(i, (i + 1) % count) for i in range(count)]
    behind = [((i + 1) % count, i) for i in range(count)]
    c_arr = sec.astype(jnp.int32).reshape(1)

    nwo, cwo, wwo = narrow_weight[0], conv_weight[0], widen_weight[0]
    nwx, cwx, wwx = swapped(nwo), swapped(cwo), swapped(wwo)
    vectors = (first_gain, first_shift, widen_bias, narrow_bias, middle_gain, middle_shift, conv_bias, last_gain, last_shift)
    packed = pl.pallas_call(
        pack_kernel, out_shape=jax.ShapeDtypeStruct((1, sum(v.shape[1] for v in vectors)), F32)
    )(*vectors)
    packed_x = swapped(packed)
    v0 = jnp.where(low, packed, packed_x)
    v1 = jnp.where(low, packed_x, packed)

    x_own = lax.dynamic_slice_in_dim(block_input, sec * own, own, 0)
    xh = jnp.concatenate(
        [lax.ppermute(x_own[:, -RIM0:], "dp", ahead), lax.ppermute(x_own[:, :RIM0], "dp", behind)], axis=1
    )

    def mine(n, w):
        return pl.BlockSpec((1, n, w), lambda i, c: (c[0] * own + i, 0, 0))

    def each(n, w):
        return pl.BlockSpec((1, n, w), lambda i, c: (i, 0, 0))

    def whole(*shape):
        return pl.BlockSpec(shape, lambda i, c: (0,) * len(shape))

    def call(kernel, c, ins, in_specs, outs, scratch, flops, nbytes, trans=0):
        return pl.pallas_call(
            kernel,
            grid_spec=pltpu.PrefetchScalarGridSpec(
                num_scalar_prefetch=1,
                grid=(own,),
                in_specs=in_specs,
                out_specs=[o[1] for o in outs],
                scratch_shapes=scratch,
            ),
            out_shape=[o[0] for o in outs],
            compiler_params=pltpu.CompilerParams(vmem_limit_bytes=VMEM_LIMIT),
            cost_estimate=pl.CostEstimate(flops=int(flops / SCALE), bytes_accessed=int(nbytes / SCALE), transcendentals=0),
        )(c, *ins)

    def o_each(w, dtype=BF16):
        return (jax.ShapeDtypeStruct((own, rows, w), dtype), each(rows, w))

    def o_vec(n, w):
        return (jax.ShapeDtypeStruct((n, w), F32), whole(n, w))

    dma = pltpu.SemaphoreType.DMA
    vspec = whole(1, packed.shape[1])
    mm = 2 * own * rows * width * inner
    wide, thin, one, masks, taps = o_each(width), o_each(inner), o_each(1, F32), o_each(LANES, F32), o_each(TAPS * inner)
    e_wide, e_thin, e_one, e_masks = wide[1], thin[1], one[1], masks[1]
    id_spec = whole(micro, rows)
    def o_rim(n):
        return (jax.ShapeDtypeStruct((own, n, inner), BF16), each(n, inner))

    (mk, act0, slx0, mux0, rsx0, nn0, sln0, rsn0, st0, nc0, slc0, rsc0, oa0, out0,
     act1, slx1, mux1, rsx1, nn1, sln1, rsn1, mid1, head1, tail1) = call(
        f0_kernel,
        c_arr,
        (block_input, xh, residues_before, residues_after, v0, v1, nwo, nwx, cwo, cwx, wwo, wwx),
        [mine(rows, width), each(2 * RIM0, width), id_spec, id_spec, vspec, vspec] + [ANY] * 6,
        [masks, wide, wide, one, one, thin, thin, one, taps, thin, thin, one, thin, wide,
         wide, wide, one, one, thin, thin, one, thin, o_rim(RIM1), o_rim(RIM1)],
        [
            pltpu.VMEM((width, inner), BF16),
            pltpu.VMEM((TAPS, inner, inner), BF16),
            pltpu.VMEM((inner, width), BF16),
            pltpu.VMEM((width, inner), BF16),
            pltpu.VMEM((rows + 2 * RIM0, width), BF16),
            pltpu.VMEM((rows + 2 * RIM0, inner), F32),
            pltpu.VMEM((rows + 2 * RIM0, inner), F32),
            pltpu.VMEM((rows, inner), F32),
            pltpu.VMEM((rows, width), F32),
            dma((4,)),
        ],
        5.5 * mm, 40_000_000,
    )

    up1 = lax.ppermute(tail1, "dp", ahead)
    dn1 = lax.ppermute(head1, "dp", behind)
    f_thin = o_each(inner, F32)
    cpart, epart, vece1 = call(
        e1_kernel,
        c_arr,
        (mid1, mk, output_cotangent, cwo, cwx, wwo, wwx),
        [e_thin, e_masks, mine(rows, width)] + [ANY] * 4,
        [f_thin, f_thin, o_vec(1, width)],
        [
            pltpu.VMEM((TAPS, inner, inner), BF16),
            pltpu.VMEM((inner, width), BF16),
            pltpu.VMEM((rows, TAPS * inner), BF16),
            pltpu.VMEM((8, width), F32),
            dma((2,)),
        ],
        3.5 * mm, 20_000_000,
    )
    up1, dn1, cpart, epart = meet([], up1, dn1, cpart, epart)
    st1, oa1, cg1, rim_dn, rim_up, vec1 = call(
        f1_kernel,
        c_arr,
        (mid1, up1, dn1, mk, v1, cpart, epart, cwo, cwx),
        [e_thin, each(RIM1, inner), each(RIM1, inner), e_masks, vspec, f_thin[1], f_thin[1], ANY, ANY],
        [taps, thin, thin, o_rim(RIM1), o_rim(RIM1), o_vec(3, inner)],
        [
            pltpu.VMEM((TAPS, inner, inner), BF16),
            pltpu.VMEM((rows, inner), F32),
            pltpu.VMEM((3, 8, inner), F32),
            dma((1,)),
        ],
        2 * mm, 20_000_000,
    )

    upg = lax.ppermute(rim_up, "dp", ahead)
    dng = lax.ppermute(rim_dn, "dp", behind)

    rest = list(range(2, count.bit_length() - 1))
    big = Route([[0, *rest[:1], 1, *rest[1:]], [1, 0, *rest]], 1, sec, at, count)
    small_way = Route([[0, 1, *rest], [1, *rest[:1], 0, *rest[1:]]], 1, sec, at, count)
    unit = 16 * count
    terms = functools.partial(weight_terms, own=own, tile=inner, unit=unit)

    g1_terms = terms(tie(c_arr, rim_up, rim_dn), [(oa1, output_cotangent), (st1, cg1)])
    upg, dng, *g1_terms = meet([], upg, dng, *g1_terms)
    g1 = Chain(*g1_terms, big)
    g1.go()
    def mid_scratch(ext):
        return [
            pltpu.VMEM((inner, TAPS * inner), BF16),
            *ext,
            pltpu.VMEM((rows, TAPS * inner), BF16),
            pltpu.VMEM((rows, inner), F32),
            pltpu.VMEM((3, 8, inner), F32),
            dma((TAPS,)),
        ]

    def first(c, block, ng, v, grad, grad_spec, slx, src, src_spec, mux, rsx):
        return call(
            functools.partial(first_kernel, block=block),
            c,
            (ng, v, grad, slx, src, mux, rsx, nwo, nwx),
            [e_thin, vspec, grad_spec, e_wide, src_spec, e_one, e_one, ANY, ANY],
            [wide, o_vec(2, width)],
            [pltpu.VMEM((width, inner), BF16), pltpu.VMEM((rows, width), F32), pltpu.VMEM((2, 8, width), F32), dma((1,))],
            1.3 * mm, 10_000_000,
        )

    ng1, vecm1 = call(
        functools.partial(mid_kernel, far=True, block=1),
        c_arr,
        (cg1, upg, dng, mk, v1, sln1, nn1, rsn1, cwo, cwx),
        [e_thin, each(RIM1, inner), each(RIM1, inner), e_masks, vspec, e_thin, e_thin, e_one, ANY, ANY],
        [thin, o_vec(3, inner)],
        mid_scratch([]),
        2.6 * mm, 10_000_000,
    )
    ng1 = meet([g1], ng1)
    c_n1 = tie(c_arr, *g1.ready())
    g1.go()
    ig1, cg0, rim_dn0, rim_up0, vecf1, vecl0 = call(
        joint_kernel,
        c_n1,
        (ng1, v1, output_cotangent, slx1, out0, mux1, rsx1, v0, slc0, nc0, rsc0, nwo, nwx, wwo, wwx),
        [e_thin, vspec, mine(rows, width), e_wide, e_wide, e_one, e_one, vspec, e_thin, e_thin, e_one] + [ANY] * 4,
        [wide, thin, o_rim(RIM0), o_rim(RIM0), o_vec(2, width), o_vec(4, width)],
        [
            pltpu.VMEM((width, inner), BF16),
            pltpu.VMEM((inner, width), BF16),
            pltpu.VMEM((rows, width), F32),
            pltpu.VMEM((rows, inner), F32),
            pltpu.VMEM((2, 8, width), F32),
            pltpu.VMEM((4, 8, width), F32),
            dma((2,)),
        ],
        2.6 * mm, 18_000_000,
    )
    cg0, rim_dn0, rim_up0 = meet([g1], cg0, rim_dn0, rim_up0)
    up0, dn0 = lax.ppermute(rim_up0, "dp", ahead), lax.ppermute(rim_dn0, "dp", behind)
    g3_terms = terms(tie(c_arr, *g1.ready(), rim_up0, rim_dn0), [(oa0, ig1), (st0, cg0)])
    g1.go()
    up0, dn0, *g3_terms = meet([g1], up0, dn0, *g3_terms)
    rim0 = jnp.concatenate([up0, dn0], axis=1)
    g3 = Chain(*g3_terms, big)
    g3.go()
    g1.ready()
    g1.go()

    head = jnp.pad(head_weight, ((0, 0), (0, LANES - vocab)))
    out1, tot = call(
        functools.partial(o1_kernel, vocab=vocab),
        tie(c_arr, g3.keep, *g1.send),
        (out0, oa1, residue_types, loss_mask, v1, head, wwo, wwx),
        [e_wide, e_thin, id_spec, id_spec, vspec, whole(width, LANES), ANY, ANY],
        [wide, o_vec(2, LANES)],
        [
            pltpu.VMEM((inner, width), BF16),
            pltpu.VMEM((rows, width), F32),
            pltpu.VMEM((rows, LANES), F32),
            pltpu.VMEM((2, 8, LANES), F32),
            dma((1,)),
        ],
        1.2 * mm, 8_000_000,
    )

    def handed(in0, in1):
        return jnp.where(low, in0, in1), swapped(jnp.where(low, in1, in0))

    def gathered(keep, come):
        return jnp.concatenate([jnp.where(low, keep, come), jnp.where(low, come, keep)], axis=0)[None]

    held_out = handed(out0, out1)
    tot = meet([g1, g3], tot)
    g1.ready()
    ng0, vecm0 = call(
        functools.partial(mid_kernel, far=False, block=0),
        tie(c_arr, *g3.ready(), *g1.send),
        (cg0, rim0, mk, v0, sln0, nn0, rsn0, cwo, cwx),
        [e_thin, each(2 * RIM0, inner), e_masks, vspec, e_thin, e_thin, e_one, ANY, ANY],
        [thin, o_vec(3, inner)],
        mid_scratch([pltpu.VMEM((rows + 2 * RIM0, inner), F32)]),
        2.6 * mm, 10_000_000,
    )
    g1.go()
    g3.go()
    ng0 = meet([g1], ng0)
    g4_terms = terms(tie(c_arr, *g1.ready()), [(act1, ng1), (act0, ng0)])
    g1.go()
    g4_terms = meet([g1, g3], *g4_terms)
    g4 = Chain(*g4_terms, small_way)
    g4.go()
    ig0, vecf0 = first(
        tie(c_arr, *g1.ready(), *g3.ready()), 0, ng0, v0, ig1, e_wide, slx0, block_input, mine(rows, width), mux0, rsx0
    )
    g1.go()
    g3.go()
    ig0, vecf0 = meet([g1, g3, g4], ig0, vecf0)

    smalls = (vec1, vece1, vecm1, vecf1, vecl0, vecm0, vecf0, tot)
    height = -(-sum(v.shape[0] for v in smalls) // 8) * 8
    small = pl.pallas_call(stack_kernel, out_shape=jax.ShapeDtypeStruct((height, width), F32))(*smalls)
    come = swapped(small)
    block_outputs, input_grads = gathered(*held_out), gathered(*handed(ig0, ig1))
    small = small + come
    for pairs, _ in big.steps:
        small = small + hop(small, pairs)
    s1, sm1, sf1, sl0, sm0, sf0, st = jnp.split(small, [4, 7, 9, 13, 16, 18], axis=0)
    type_total, loss_total = st[0, :vocab], st[1, :vocab]

    half = inner // 2
    cols = width // inner
    parts, sets, base = [], [], 0
    for core, chain, sem, step in ((1, g1, 0, 0), (0, g3, 0, 0), (None, g4, 1, TAPS + cols)):
        pieces = chain.finish()
        sets.append((core, list(range(len(parts), len(parts) + len(pieces))), sem * base, sem, step))
        base = (base if sem else 0) + sum(p.shape[0] for p in pieces) // 2
        parts += pieces
    top = sets[2][2]
    wide_rows = jnp.arange(cols + TAPS, dtype=jnp.int32) * half
    narrow_rows = (jnp.arange(cols, dtype=jnp.int32) + jnp.where(low, cols, 0).astype(jnp.int32)) * half + top
    widen_grad, conv_grad, narrow_grad = pl.pallas_call(
        functools.partial(unpack_kernel, sets=sets, shards=big.shards, outs=[0, cols, cols + TAPS]),
        grid_spec=pltpu.PrefetchScalarGridSpec(
            num_scalar_prefetch=3,
            grid=(2 * cols + TAPS,),
            in_specs=[ANY] * len(parts),
            out_specs=[
                pl.BlockSpec((inner, inner), lambda s, *_: (0, jnp.minimum(s, cols - 1))),
                pl.BlockSpec((1, inner, inner), lambda s, *_: (jnp.clip(s - cols, 0, TAPS - 1), 0, 0)),
                pl.BlockSpec((inner, inner), lambda s, *_: (jnp.maximum(s - cols - TAPS, 0), 0)),
            ],
            scratch_shapes=[pltpu.VMEM((2, base, inner), BF16), dma((2,))],
        ),
        out_shape=[
            jax.ShapeDtypeStruct((inner, width), F32),
            jax.ShapeDtypeStruct((TAPS, inner, inner), F32),
            jax.ShapeDtypeStruct((width, inner), F32),
        ],
        compiler_params=pltpu.CompilerParams(vmem_limit_bytes=VMEM_LIMIT),
        cost_estimate=pl.CostEstimate(flops=0, bytes_accessed=500_000, transcendentals=0),
    )(tie(c_arr, block_outputs, input_grads), jnp.concatenate([wide_rows, narrow_rows]), jnp.concatenate([big.signs, small_way.signs]), *parts)

    def sel(in0, in1, n=width):
        return jnp.where(low, in0, in1)[None, :n]

    return (
        block_outputs,
        input_grads,
        sel(sf0[0], sf1[0]),
        sel(sf0[1], sf1[1]),
        narrow_grad[None],
        sel(sm0[2], sm1[2], inner),
        sel(sm0[0], sm1[0], inner),
        sel(sm0[1], sm1[1], inner),
        conv_grad[None],
        sel(sl0[2], s1[2], inner),
        sel(sl0[0], s1[0], inner),
        sel(sl0[1], s1[1], inner),
        widen_grad[None],
        sel(sl0[3], s1[3]),
        type_total.astype(jnp.int32),
        loss_total / jnp.maximum(type_total, 1.0),
    )


def solution(mesh):
    rows = P(None, "dp", None)
    ids = P(None, "dp")
    vec = P("section", None)
    mat = P("section", None, None)
    conv = P("section", None, None, None)
    weights = (vec, vec, mat, vec, vec, vec, conv, vec, vec, vec, mat, vec)
    grads = P("section", None, "dp", None)
    return jax.shard_map(
        body,
        mesh=mesh,
        in_specs=(rows, rows, ids, ids, ids, ids, *weights, P()),
        out_specs=(grads, grads, *weights, P(), P()),
        check_vma=False,
    )
```

```python
import functools

import jax
import jax.numpy as jnp
from jax import lax
from jax.experimental import pallas as pl
from jax.experimental.pallas import tpu as pltpu
from jax.sharding import PartitionSpec as P

TAPS = 5
MID = TAPS // 2
DIL0 = 2
DIL1 = 64
EPS = 1e-05
SCALE = 100

RIM0 = 8
RIM1 = MID * DIL1
F32 = jnp.float32
BF16 = jnp.bfloat16
LANES = 128
LIVE1 = 8
VMEM_LIMIT = 56 * 1024 * 1024
ANY = pl.BlockSpec(memory_space=pl.ANY)


def dot_nn(a, b):
    return lax.dot_general(a, b, (((1,), (0,)), ((), ())), preferred_element_type=F32)


def dot_nt(a, b):
    return lax.dot_general(a, b, (((1,), (1,)), ((), ())), preferred_element_type=F32)


def dot_tn(a, b):
    return lax.dot_general(a, b, (((0,), (0,)), ((), ())), preferred_element_type=F32)


def gelu_parts(y):
    phi_big = lax.erf(y * 0.7071067811865476) * 0.5 + 0.5
    e = jnp.exp(y * y * -0.5)
    return y * phi_big, phi_big + y * e * 0.3989422804014327


def normed_of(u):
    mean = jnp.mean(u, axis=-1, keepdims=True)
    center = u - mean
    scale = lax.rsqrt(jnp.mean(center * center, axis=-1, keepdims=True) + EPS)
    return center * scale, mean, scale


def norm_back(err, slope, normed, scale, gain):
    q = err * slope
    p = q * gain
    m1 = jnp.mean(p, axis=-1, keepdims=True)
    m2 = jnp.mean(p * normed, axis=-1, keepdims=True)
    return (p - m1 - normed * m2) * scale, q * normed, q


def fold8(v):
    return sum(v[k : k + 8] for k in range(0, v.shape[0], 8))


def chunks(rows, size, body):
    steps = rows // size
    lax.fori_loop(0, steps, lambda i, c: (body(pl.multiple_of(i * size, size)), c)[1], 0, unroll=min(16, steps))


def summed_chunks(rows, size, width, terms, body):
    steps = rows // size

    def one(i, held):
        return tuple(h + fold8(v) for h, v in zip(held, body(pl.multiple_of(i * size, size))))

    return lax.fori_loop(0, steps, one, (jnp.zeros((8, width), F32),) * terms, unroll=min(16, steps))


def pick_copy(cond, one, other, dst, sem):
    @pl.when(cond)
    def _():
        pltpu.make_async_copy(one, dst, sem).start()

    @pl.when(jnp.logical_not(cond))
    def _():
        pltpu.make_async_copy(other, dst, sem).start()


def pick_wait(one, dst, sem):
    pltpu.make_async_copy(one, dst, sem).wait()


def conv_parts(one, dst):
    inner = one.shape[1]
    return [(j, dst.at[:, (TAPS - 1 - j) * inner : (TAPS - j) * inner]) for j in range(TAPS)]


def columns(row):
    return jnp.broadcast_to(row, (LANES, row.shape[1])).T


class Vectors:
    def __init__(self, ref, width, inner):
        at = 0
        for name in ("fg", "fs", "wb"):
            setattr(self, name, ref[:, at : at + width])
            at += width
        for name in ("nb", "mg", "ms", "cb", "lg", "ls"):
            setattr(self, name, ref[:, at : at + inner])
            at += inner


def stack_kernel(*refs):
    at = 0
    refs[-1][...] = jnp.zeros_like(refs[-1])
    for ref in refs[:-1]:
        refs[-1][at : at + ref.shape[0], : ref.shape[1]] = ref[...]
        at += ref.shape[0]


def pack_kernel(*refs):
    at = 0
    for ref in refs[:-1]:
        refs[-1][:, at : at + ref.shape[1]] = ref[...]
        at += ref.shape[1]


def first_norm(u, v):
    normed, mean, scale = normed_of(u)
    act, slope = gelu_parts(normed * v.fg + v.fs)
    return act.astype(BF16), slope.astype(BF16), mean, scale


def mid_norm(u, v):
    normed, _, scale = normed_of(u + v.nb)
    act, slope = gelu_parts(normed * v.mg + v.ms)
    return act.astype(BF16), slope.astype(BF16), normed.astype(BF16), scale


def my_row(c_ref, ref):
    return ref[pl.ds(c_ref[0] * pl.num_programs(0) + pl.program_id(0), 1), :].astype(F32)


def f0_kernel(c_ref, x_ref, xh_ref, rb_ref, ra_ref, v0_ref, v1_ref, nwo, nwx, cwo, cwx, wwo, wwx,
              mk, act0, slx0, mux0, rsx0, nn0, sln0, rsn0, st0, nc0, slc0, rsc0, oa0, out0,
              act1, slx1, mux1, rsx1, nn1, sln1, rsn1, mid1, head1, tail1,
              nw0, cw0, ww0, nw1, act_s, n32, mid32, c32, r32, sems):
    low = c_ref[0] == 0
    first = pl.program_id(0) == 0
    rows, width = x_ref.shape[1:]
    inner = n32.shape[1]
    v0, v1 = Vectors(v0_ref, width, inner), Vectors(v1_ref, width, inner)

    @pl.when(first)
    def _():
        pick_copy(low, nwo, nwx, nw0, sems.at[0])
        pick_copy(low, cwo, cwx, cw0, sems.at[1])
        pick_copy(low, wwo, wwx, ww0, sems.at[2])
        pick_copy(low, nwx, nwo, nw1, sems.at[3])

    lane = lax.broadcasted_iota(jnp.int32, (rows, LANES), 1)
    offset = jnp.where(lane < LIVE1, (lane - MID) * DIL0, (lane - LIVE1 - MID) * DIL1).astype(F32)
    before, after = columns(my_row(c_ref, rb_ref)), columns(my_row(c_ref, ra_ref))
    mk[0] = jnp.where((offset >= -before) & (offset <= after), 1.0, 0.0)

    def stage1(r):
        s = pl.ds(r, 16)
        act, slope, mean, scale = first_norm(x_ref[0, s, :].astype(F32), v0)
        act_s[s, :] = act
        act0[0, s, :] = act
        slx0[0, s, :] = slope
        mux0[0, s, :] = mean
        rsx0[0, s, :] = scale

    chunks(rows, 16, stage1)
    act, _, _, _ = first_norm(xh_ref[0].astype(F32), v0)
    act_s[rows : rows + 2 * RIM0, :] = act

    @pl.when(first)
    def _():
        pick_wait(nwo, nw0, sems.at[0])

    n32[...] = dot_nn(act_s[...], nw0[...])

    def stage2(r):
        s = pl.ds(r, 32)
        mid, slope, normed, scale = mid_norm(n32[s, :], v0)
        mid32[pl.ds(r + RIM0, 32), :] = mid.astype(F32)
        nn0[0, s, :] = normed
        sln0[0, s, :] = slope
        rsn0[0, s, :] = scale

    chunks(rows, 32, stage2)
    rim = mid_norm(n32[rows : rows + 2 * RIM0, :], v0)[0].astype(F32)
    mid32[0:RIM0, :] = rim[:RIM0]
    mid32[rows + RIM0 : rows + 2 * RIM0, :] = rim[RIM0:]
    near_taps(rows, inner, mid32, mk, st0.at[0])

    @pl.when(first)
    def _():
        pick_wait(cwo, cw0, sems.at[1])

    c32[...] = dot_nn(st0[0], cw0[...].reshape(TAPS * inner, inner))

    def stage4(r):
        s = pl.ds(r, 32)
        normed, _, scale = normed_of(c32[s, :] + v0.cb)
        act, slope = gelu_parts(normed * v0.lg + v0.ls)
        oa0[0, s, :] = act.astype(BF16)
        nc0[0, s, :] = normed.astype(BF16)
        slc0[0, s, :] = slope.astype(BF16)
        rsc0[0, s, :] = scale

    chunks(rows, 32, stage4)

    @pl.when(first)
    def _():
        pick_wait(wwo, ww0, sems.at[2])
        pick_wait(nwx, nw1, sems.at[3])

    r32[...] = dot_nn(oa0[0], ww0[...])

    def stage5(r):
        s = pl.ds(r, 16)
        res = (x_ref[0, s, :].astype(F32) + (r32[s, :] + v0.wb)).astype(BF16)
        out0[0, s, :] = res
        act, slope, mean, scale = first_norm(res.astype(F32), v1)
        act1[0, s, :] = act
        slx1[0, s, :] = slope
        mux1[0, s, :] = mean
        rsx1[0, s, :] = scale

    chunks(rows, 16, stage5)
    n32[0:rows, :] = dot_nn(act1[0], nw1[...])

    def stage6(r):
        s = pl.ds(r, 32)
        mid, slope, normed, scale = mid_norm(n32[s, :], v1)
        mid1[0, s, :] = mid
        nn1[0, s, :] = normed
        sln1[0, s, :] = slope
        rsn1[0, s, :] = scale

    chunks(rows, 32, stage6)
    head1[...] = mid1[:, :RIM1]
    tail1[...] = mid1[:, rows - RIM1 :]


def near_taps(rows, inner, ext32, mk, dst):
    def stack(r):
        s = pl.ds(r, 16)
        window = ext32[pl.ds(r, 32), :]
        for j in range(TAPS):
            at = RIM0 + (j - MID) * DIL0
            live = mk[0, s, j : j + 1]
            dst[s, j * inner : (j + 1) * inner] = (window[at : at + 16] * live).astype(BF16)

    chunks(rows, 16, stack)


def far_taps(rows, inner, own_ref, up_ref, dn_ref, mk, dst):
    pieces = rows // DIL1
    for k in range(pieces):
        for j in range(TAPS):
            at = k + j - MID
            if up_ref is None and (k < MID and j < MID or k >= pieces - MID and j > MID):
                dst[k * DIL1 : (k + 1) * DIL1, j * inner : (j + 1) * inner] = jnp.zeros((DIL1, inner), BF16)
                continue
            live = mk[0, k * DIL1 : (k + 1) * DIL1, LIVE1 + j : LIVE1 + j + 1]
            if at < 0:
                part = up_ref[0, (at + MID) * DIL1 : (at + MID + 1) * DIL1, :]
            elif at >= pieces:
                part = dn_ref[0, (at - pieces) * DIL1 : (at - pieces + 1) * DIL1, :]
            else:
                part = own_ref[0, at * DIL1 : (at + 1) * DIL1, :]
            dst[k * DIL1 : (k + 1) * DIL1, j * inner : (j + 1) * inner] = (part.astype(F32) * live).astype(BF16)


def e1_kernel(c_ref, mid_ref, mk, cot_ref, cwo, cwx, wwo, wwx, cpart, epart, vec, cw1, ww1, st, acc, sems):
    low = c_ref[0] == 0
    step = pl.program_id(0)
    rows, width = cot_ref.shape[1:]
    inner = mid_ref.shape[2]

    @pl.when(step == 0)
    def _():
        pick_copy(low, wwx, wwo, ww1, sems.at[1])
        pick_copy(low, cwx, cwo, cw1, sems.at[0])
        acc[...] = jnp.zeros_like(acc)

    far_taps(rows, inner, mid_ref, None, None, mk, st)
    (cot_sum,) = summed_chunks(rows, 16, width, 1, lambda r: (cot_ref[0, pl.ds(r, 16), :].astype(F32),))
    acc[...] += cot_sum

    @pl.when(step == 0)
    def _():
        pick_wait(wwx, ww1, sems.at[1])

    epart[0] = dot_nt(cot_ref[0], ww1[...])

    @pl.when(step == 0)
    def _():
        pick_wait(cwx, cw1, sems.at[0])

    cpart[0] = dot_nn(st[...], cw1[...].reshape(TAPS * inner, inner))

    @pl.when(step == pl.num_programs(0) - 1)
    def _():
        vec[...] = jnp.sum(acc[...], axis=0, keepdims=True)


def f1_kernel(c_ref, mid_ref, up_ref, dn_ref, mk, v1_ref, cpart, epart, cwo, cwx,
              st1, oa1, cg1, head, tail, vec, cw1, c32, acc, sems):
    low = c_ref[0] == 0
    step = pl.program_id(0)
    rows, inner = mid_ref.shape[1:]
    width = (v1_ref.shape[1] - 6 * inner) // 3
    v1 = Vectors(v1_ref, width, inner)

    @pl.when(step == 0)
    def _():
        pick_copy(low, cwx, cwo, cw1, sems.at[0])
        acc[...] = jnp.zeros_like(acc)

    far_taps(rows, inner, mid_ref, up_ref, dn_ref, mk, st1.at[0])

    @pl.when(step == 0)
    def _():
        pick_wait(cwx, cw1, sems.at[0])

    side = MID * inner
    first, last = cw1[:MID].reshape(side, inner), cw1[MID + 1 :].reshape(side, inner)
    c32[...] = cpart[0]
    c32[:RIM1, :] += dot_nn(st1[0, :RIM1, :side], first)
    c32[rows - RIM1 :, :] += dot_nn(st1[0, rows - RIM1 :, side + inner :], last)

    def stage(r):
        s = pl.ds(r, 16)
        normed, _, scale = normed_of(c32[s, :] + v1.cb)
        act, slope = gelu_parts(normed * v1.lg + v1.ls)
        oa1[0, s, :] = act.astype(BF16)
        du, dgain, dshift = norm_back(epart[0, s, :], slope, normed, scale, v1.lg)
        du = du.astype(BF16)
        cg1[0, s, :] = du
        return dgain, dshift, du.astype(F32)

    sums = summed_chunks(rows, 16, inner, 3, stage)
    for k in range(3):
        acc[k] += sums[k]
    head[...] = cg1[:, :RIM1]
    tail[...] = cg1[:, rows - RIM1 :]

    @pl.when(step == pl.num_programs(0) - 1)
    def _():
        vec[...] = jnp.sum(acc[...], axis=1)


def o1_kernel(c_ref, out0_ref, oa_ref, rt_ref, lm_ref, v1_ref, head_ref, wwo, wwx,
              out1, tot, ww1, r32, lg, acc, sems, *, vocab):
    low = c_ref[0] == 0
    step = pl.program_id(0)
    rows, width = out0_ref.shape[1:]
    v1 = Vectors(v1_ref, width, oa_ref.shape[2])

    @pl.when(step == 0)
    def _():
        pick_copy(low, wwx, wwo, ww1, sems.at[0])
        acc[...] = jnp.zeros_like(acc)
        pick_wait(wwx, ww1, sems.at[0])

    r32[...] = dot_nn(oa_ref[0], ww1[...])

    def stage(r):
        s = pl.ds(r, 16)
        out1[0, s, :] = (out0_ref[0, s, :].astype(F32) + (r32[s, :] + v1.wb)).astype(BF16)

    chunks(rows, 16, stage)
    lg[...] = dot_nn(out1[0], head_ref[...])
    lane = lax.broadcasted_iota(jnp.int32, (rows, LANES), 1)
    logits = jnp.where(lane < vocab, lg[...], -1e30)
    top = jnp.max(logits, axis=-1, keepdims=True)
    log_total = top + jnp.log(jnp.sum(jnp.exp(logits - top), axis=-1, keepdims=True))
    kind, weight = columns(my_row(c_ref, rt_ref)), columns(my_row(c_ref, lm_ref))
    onehot = jnp.where(lane == kind.astype(jnp.int32), weight, 0.0)
    acc[0] += fold8(onehot)
    acc[1] += fold8(onehot * (log_total - logits))

    @pl.when(step == pl.num_programs(0) - 1)
    def _():
        tot[...] = jnp.sum(acc[...], axis=1)


def middle_back(rows, inner, m32, sln, nn, rsn, gain, ng, acc):
    def stage(r):
        s = pl.ds(r, 16)
        du, dgain, dshift = norm_back(m32[s, :], sln[0, s, :].astype(F32), nn[0, s, :].astype(F32), rsn[0, s, :], gain)
        du = du.astype(BF16)
        ng[0, s, :] = du
        return dgain, dshift, du.astype(F32)

    sums = summed_chunks(rows, 16, inner, 3, stage)
    for k in range(3):
        acc[k] += sums[k]


def mid_kernel(c_ref, cg_ref, *refs, far, block):
    if far:
        up_ref, dn_ref, mk, v_ref, sln, nn, rsn, cwo, cwx, ng, vec, cw2, stg, m32, acc, sems = refs
    else:
        rim_ref, mk, v_ref, sln, nn, rsn, cwo, cwx, ng, vec, cw2, ext, stg, m32, acc, sems = refs
    low = c_ref[0] == block
    step = pl.program_id(0)
    rows, inner = cg_ref.shape[1:]
    parts = conv_parts(cwo, cw2)

    @pl.when(step == 0)
    def _():
        for j, dst in parts:
            pick_copy(low, cwo.at[j], cwx.at[j], dst, sems.at[j])
        acc[...] = jnp.zeros_like(acc)

    if far:
        far_taps(rows, inner, cg_ref, up_ref, dn_ref, mk, stg)
    else:
        rim = rim_ref[0].astype(F32)
        ext[0:RIM0, :] = rim[:RIM0]
        ext[rows + RIM0 : rows + 2 * RIM0, :] = rim[RIM0:]

        def widen(r):
            ext[pl.ds(r + RIM0, 16), :] = cg_ref[0, pl.ds(r, 16), :].astype(F32)

        chunks(rows, 16, widen)
        near_taps(rows, inner, ext, mk, stg)

    @pl.when(step == 0)
    def _():
        for j, dst in parts:
            pick_wait(cwo.at[j], dst, sems.at[j])

    m32[...] = dot_nt(stg[...], cw2[...])
    at = v_ref.shape[1] - 5 * inner
    middle_back(rows, inner, m32, sln, nn, rsn, v_ref[:, at : at + inner], ng, acc)

    @pl.when(step == pl.num_programs(0) - 1)
    def _():
        vec[...] = jnp.sum(acc[...], axis=1)


def first_kernel(c_ref, ng_ref, v_ref, grad, slx, src, mux, rsx, nwo, nwx, ig, vec, nw, a32, acc, sems, *, block):
    low = c_ref[0] == block
    step = pl.program_id(0)
    rows, width = grad.shape[1:]
    gain = v_ref[:, :width]

    @pl.when(step == 0)
    def _():
        pick_copy(low, nwo, nwx, nw, sems.at[0])
        acc[...] = jnp.zeros_like(acc)
        pick_wait(nwo, nw, sems.at[0])

    a32[...] = dot_nt(ng_ref[0], nw[...])

    def stage(r):
        s = pl.ds(r, 16)
        scale = rsx[0, s, :]
        normed = (src[0, s, :].astype(F32) - mux[0, s, :]) * scale
        du, dgain, dshift = norm_back(a32[s, :], slx[0, s, :].astype(F32), normed, scale, gain)
        ig[0, s, :] = (grad[0, s, :].astype(F32) + du).astype(BF16)
        return dgain, dshift

    sums = summed_chunks(rows, 16, width, 2, stage)
    for k in range(2):
        acc[k] += sums[k]

    @pl.when(step == pl.num_programs(0) - 1)
    def _():
        vec[...] = jnp.sum(acc[...], axis=1)


def joint_kernel(c_ref, ng_ref, v1_ref, grad, slx, src, mux, rsx, v0_ref, slc, nc, rsc, nwo, nwx, wwo, wwx,
                 ig, cg, head, tail, vecf, vecl, nw, ww, a32, e32, accf, accl, sems):
    low = c_ref[0] == 0
    step = pl.program_id(0)
    rows, width = grad.shape[1:]
    inner = e32.shape[1]
    first_gain, last_gain = v1_ref[:, :width], Vectors(v0_ref, width, inner).lg

    @pl.when(step == 0)
    def _():
        pick_copy(low, nwx, nwo, nw, sems.at[0])
        pick_copy(low, wwo, wwx, ww, sems.at[1])
        accf[...] = jnp.zeros_like(accf)
        accl[...] = jnp.zeros_like(accl)
        pick_wait(nwx, nw, sems.at[0])

    a32[...] = dot_nt(ng_ref[0], nw[...])

    def stage(r):
        s = pl.ds(r, 16)
        scale = rsx[0, s, :]
        normed = (src[0, s, :].astype(F32) - mux[0, s, :]) * scale
        du, dgain, dshift = norm_back(a32[s, :], slx[0, s, :].astype(F32), normed, scale, first_gain)
        out = (grad[0, s, :].astype(F32) + du).astype(BF16)
        ig[0, s, :] = out
        return dgain, dshift, out.astype(F32)

    sums = summed_chunks(rows, 16, width, 3, stage)
    accf[0] += sums[0]
    accf[1] += sums[1]
    accl[3] += sums[2]

    @pl.when(step == 0)
    def _():
        pick_wait(wwo, ww, sems.at[1])

    e32[...] = dot_nt(ig[0], ww[...])

    def stage2(r):
        s = pl.ds(r, 16)
        du, dgain, dshift = norm_back(
            e32[s, :], slc[0, s, :].astype(F32), nc[0, s, :].astype(F32), rsc[0, s, :], last_gain
        )
        du = du.astype(BF16)
        cg[0, s, :] = du
        return dgain, dshift, du.astype(F32)

    sums = summed_chunks(rows, 16, inner, 3, stage2)
    for k in range(3):
        accl[k, :, :inner] += sums[k]
    head[0] = cg[0, : 2 * RIM0, :].astype(F32)[:RIM0].astype(BF16)
    tail[0] = cg[0, rows - 2 * RIM0 :, :].astype(F32)[RIM0:].astype(BF16)

    @pl.when(step == pl.num_programs(0) - 1)
    def _():
        vecf[...] = jnp.sum(accf[...], axis=1)
        vecl[...] = jnp.sum(accl[...], axis=1)


def weight_terms(c_arr, pairs, own, tile, unit):
    specs, args, spans = [], [], []
    at = 0

    def index(v, pick):
        if v.shape[0] == own:
            return lambda s, c: (0, 0, pick(s))
        return lambda s, c: (c[0], 0, pick(s))

    for a, g in pairs:
        na, ng = a.shape[2] // tile, g.shape[2] // tile
        local = functools.partial(lambda s, lo, n: jnp.clip(s - lo, 0, n - 1), lo=at, n=na * ng)
        block = (own, a.shape[1], tile)
        specs.append(pl.BlockSpec(block, index(a, lambda s, local=local, na=na: local(s) % na)))
        specs.append(pl.BlockSpec(block, index(g, lambda s, local=local, na=na: local(s) // na)))
        args += [a, g]
        spans.append((at, at + na * ng))
        at += na * ng
    half = tile // 2
    depth = own * args[0].shape[1]
    out_rows = -(-at * half // unit) * unit

    def kernel(c_ref, *refs):
        keep, send, whole = refs[-3:]
        s = pl.program_id(0)
        for k, (lo, hi) in enumerate(spans):

            @pl.when((s >= lo) & (s < hi))
            def _(k=k):
                a, g = (refs[2 * k + i][...].reshape(depth, tile) for i in range(2))
                whole[...] = dot_tn(a, g).astype(BF16)

        stay = pl.multiple_of(c_ref[0] * half, half)
        keep[...] = whole[pl.ds(stay, half), :]
        send[...] = whole[pl.ds(half - stay, half), :]

    return pl.pallas_call(
        kernel,
        grid_spec=pltpu.PrefetchScalarGridSpec(
            num_scalar_prefetch=1,
            grid=(at,),
            in_specs=specs,
            out_specs=[pl.BlockSpec((half, tile), lambda s, c: (s, 0))] * 2,
            scratch_shapes=[pltpu.VMEM((tile, tile), BF16)],
        ),
        out_shape=[jax.ShapeDtypeStruct((out_rows, tile), BF16)] * 2,
        compiler_params=pltpu.CompilerParams(vmem_limit_bytes=VMEM_LIMIT),
        cost_estimate=pl.CostEstimate(
            flops=at * 2 * tile * tile * depth // SCALE, bytes_accessed=4 * out_rows * tile // SCALE, transcendentals=0
        ),
    )(c_arr, *args)


def unpack_kernel(c_ref, row_ref, sig_ref, *refs, sets, shards, outs):
    n = sum(len(g[1]) for g in sets)
    ins, grads, (held, sems) = refs[:n], refs[n:-2], refs[-2:]
    s = pl.program_id(0)
    half = grads[0].shape[0] // 2

    def fetch(numbers, base, sem):
        sign = 2 * sem
        arrays = [ins[i] for i in numbers]
        shard = sum(a.shape[0] for a in arrays) // (2 * shards)
        first = 0
        for a in arrays:
            mine = 0 if first < shards else 1
            for p in range(a.shape[0] // shard):
                h = c_ref[0] if mine == 0 else 1 - c_ref[0]
                to = pl.multiple_of(((first + p) % shards ^ sig_ref[sign + mine]) * shard + base, 16)
                pltpu.make_async_copy(a.at[pl.ds(p * shard, shard)], held.at[h, pl.ds(to, shard)], sems.at[sem]).start()
            first += a.shape[0] // shard

    def landed(numbers, base, sem):
        part = held.at[:, base : base + sum(ins[i].shape[0] for i in numbers) // 2]
        pltpu.make_async_copy(part, part, sems.at[sem]).wait()

    @pl.when(s == 0)
    def _():
        for core, numbers, base, sem, _ in sets:
            if core is None:
                fetch(numbers, base, sem)
            else:
                pl.when(c_ref[0] == core)(functools.partial(fetch, numbers, base, sem))

    for core, numbers, base, sem, step in sets:
        if core != 0:
            pl.when(s == step)(functools.partial(landed, numbers, base, sem))

    at = pl.multiple_of(row_ref[s], half)
    for k, grad in enumerate(grads):
        last = outs[k + 1] if k + 1 < len(outs) else None

        @pl.when((s >= outs[k]) if last is None else (s >= outs[k]) & (s < last))
        def _(grad=grad):
            lead = (0,) if len(grad.shape) == 3 else ()
            for h in range(2):
                grad[(*lead, pl.ds(h * half, half), slice(None))] = held[h, pl.ds(at, half), :].astype(F32)


def add_low(one, other):
    return (one.astype(F32) + other.astype(F32)).astype(BF16)


def part(v, at, rows):
    return lax.dynamic_slice_in_dim(v, at * rows, rows, 0)


def tie(value, *after):
    return lax.optimization_barrier((value, *after))[0]


class Route:
    def __init__(self, orders, whole, sec, at, count):
        self.split = len(orders[0]) - whole
        self.steps, signs = [], [0, 0]
        for k in range(len(orders[0])):
            pairs = [(s * count + d, s * count + (d ^ (1 << orders[s][k]))) for s in range(2) for d in range(count)]
            place = [(at >> orders[s][k]) & 1 for s in range(2)]
            self.steps.append((pairs, jnp.where(sec == 0, place[0], place[1])))
            if k < self.split:
                signs = [g + (p << (self.split - 1 - k)) for g, p in zip(signs, place)]
        signs = jnp.where(sec == 0, jnp.stack(signs), jnp.stack(signs[::-1]))
        self.signs = signs.astype(jnp.int32)
        self.shards = 1 << self.split


class Chain:
    def __init__(self, keep, send, route):
        self.keep, self.send, self.route = keep, [send], route
        self.at = -1
        self.fly, self.pieces = [], []
        self.last = len(route.steps) + route.split

    def ready(self):
        bits, split = len(self.route.steps), self.route.split
        if 0 <= self.at < split:
            (come,) = self.fly
            bit = self.route.steps[self.at][1]
            rows = self.keep.shape[0] // 2
            self.send = [add_low(part(self.keep, 1 - bit, rows), part(come, 1 - bit, rows))]
            self.keep = add_low(part(self.keep, bit, rows), part(come, bit, rows))
        elif split <= self.at <= bits:
            self.keep = add_low(self.keep, self.fly[0])
            self.pieces = self.send = [self.keep]
        elif self.at > bits:
            self.pieces = self.send = [jnp.concatenate(self.pieces + self.fly, axis=0)]
        return tuple(self.send)

    def go(self):
        bits = len(self.route.steps)
        if self.at < 0:
            self.fly = [swapped(v) for v in self.send]
        else:
            step = self.at if self.at < bits else self.route.split - 1 - (self.at - bits)
            self.fly = [hop(v, self.route.steps[step][0]) for v in self.send]
        self.at += 1

    def done(self):
        return self.at == self.last

    def finish(self):
        while not self.done():
            self.ready()
            self.go()
        pieces = self.pieces + self.fly
        return pieces + [swapped(p) for p in pieces]


def meet(chains, *values):
    fly = [v for g in chains for v in g.fly]
    out = list(lax.optimization_barrier((*fly, *values)))
    for g in chains:
        g.fly, out = out[: len(g.fly)], out[len(g.fly) :]
    return out[0] if len(out) == 1 else out


def swapped(v):
    return lax.ppermute(v, "section", [(0, 1), (1, 0)])


def hop(v, pairs):
    return lax.ppermute(v, ("section", "dp"), pairs)


def body(block_input, output_cotangent, residues_before, residues_after, residue_types, loss_mask,
         first_gain, first_shift, narrow_weight, narrow_bias, middle_gain, middle_shift,
         conv_weight, conv_bias, last_gain, last_shift, widen_weight, widen_bias, head_weight):
    sec = lax.axis_index("section")
    at = lax.axis_index("dp")
    count = lax.axis_size("dp")
    low = sec == 0
    micro, rows, width = block_input.shape
    own = micro // 2
    inner = narrow_weight.shape[2]
    vocab = head_weight.shape[1]
    ahead = [(i, (i + 1) % count) for i in range(count)]
    behind = [((i + 1) % count, i) for i in range(count)]
    c_arr = sec.astype(jnp.int32).reshape(1)

    nwo, cwo, wwo = narrow_weight[0], conv_weight[0], widen_weight[0]
    nwx, cwx, wwx = swapped(nwo), swapped(cwo), swapped(wwo)
    vectors = (first_gain, first_shift, widen_bias, narrow_bias, middle_gain, middle_shift, conv_bias, last_gain, last_shift)
    packed = pl.pallas_call(
        pack_kernel, out_shape=jax.ShapeDtypeStruct((1, sum(v.shape[1] for v in vectors)), F32)
    )(*vectors)
    packed_x = swapped(packed)
    v0 = jnp.where(low, packed, packed_x)
    v1 = jnp.where(low, packed_x, packed)

    x_own = lax.dynamic_slice_in_dim(block_input, sec * own, own, 0)
    xh = jnp.concatenate(
        [lax.ppermute(x_own[:, -RIM0:], "dp", ahead), lax.ppermute(x_own[:, :RIM0], "dp", behind)], axis=1
    )

    def mine(n, w):
        return pl.BlockSpec((1, n, w), lambda i, c: (c[0] * own + i, 0, 0))

    def each(n, w):
        return pl.BlockSpec((1, n, w), lambda i, c: (i, 0, 0))

    def whole(*shape):
        return pl.BlockSpec(shape, lambda i, c: (0,) * len(shape))

    def call(kernel, c, ins, in_specs, outs, scratch, flops, nbytes, trans=0):
        return pl.pallas_call(
            kernel,
            grid_spec=pltpu.PrefetchScalarGridSpec(
                num_scalar_prefetch=1,
                grid=(own,),
                in_specs=in_specs,
                out_specs=[o[1] for o in outs],
                scratch_shapes=scratch,
            ),
            out_shape=[o[0] for o in outs],
            compiler_params=pltpu.CompilerParams(vmem_limit_bytes=VMEM_LIMIT),
            cost_estimate=pl.CostEstimate(flops=int(flops / SCALE), bytes_accessed=int(nbytes / SCALE), transcendentals=0),
        )(c, *ins)

    def o_each(w, dtype=BF16):
        return (jax.ShapeDtypeStruct((own, rows, w), dtype), each(rows, w))

    def o_vec(n, w):
        return (jax.ShapeDtypeStruct((n, w), F32), whole(n, w))

    dma = pltpu.SemaphoreType.DMA
    vspec = whole(1, packed.shape[1])
    mm = 2 * own * rows * width * inner
    wide, thin, one, masks, taps = o_each(width), o_each(inner), o_each(1, F32), o_each(LANES, F32), o_each(TAPS * inner)
    e_wide, e_thin, e_one, e_masks = wide[1], thin[1], one[1], masks[1]
    id_spec = whole(micro, rows)
    def o_rim(n):
        return (jax.ShapeDtypeStruct((own, n, inner), BF16), each(n, inner))

    (mk, act0, slx0, mux0, rsx0, nn0, sln0, rsn0, st0, nc0, slc0, rsc0, oa0, out0,
     act1, slx1, mux1, rsx1, nn1, sln1, rsn1, mid1, head1, tail1) = call(
        f0_kernel,
        c_arr,
        (block_input, xh, residues_before, residues_after, v0, v1, nwo, nwx, cwo, cwx, wwo, wwx),
        [mine(rows, width), each(2 * RIM0, width), id_spec, id_spec, vspec, vspec] + [ANY] * 6,
        [masks, wide, wide, one, one, thin, thin, one, taps, thin, thin, one, thin, wide,
         wide, wide, one, one, thin, thin, one, thin, o_rim(RIM1), o_rim(RIM1)],
        [
            pltpu.VMEM((width, inner), BF16),
            pltpu.VMEM((TAPS, inner, inner), BF16),
            pltpu.VMEM((inner, width), BF16),
            pltpu.VMEM((width, inner), BF16),
            pltpu.VMEM((rows + 2 * RIM0, width), BF16),
            pltpu.VMEM((rows + 2 * RIM0, inner), F32),
            pltpu.VMEM((rows + 2 * RIM0, inner), F32),
            pltpu.VMEM((rows, inner), F32),
            pltpu.VMEM((rows, width), F32),
            dma((4,)),
        ],
        5.5 * mm, 40_000_000,
    )

    up1 = lax.ppermute(tail1, "dp", ahead)
    dn1 = lax.ppermute(head1, "dp", behind)
    f_thin = o_each(inner, F32)
    cpart, epart, vece1 = call(
        e1_kernel,
        c_arr,
        (mid1, mk, output_cotangent, cwo, cwx, wwo, wwx),
        [e_thin, e_masks, mine(rows, width)] + [ANY] * 4,
        [f_thin, f_thin, o_vec(1, width)],
        [
            pltpu.VMEM((TAPS, inner, inner), BF16),
            pltpu.VMEM((inner, width), BF16),
            pltpu.VMEM((rows, TAPS * inner), BF16),
            pltpu.VMEM((8, width), F32),
            dma((2,)),
        ],
        3.5 * mm, 20_000_000,
    )
    up1, dn1, cpart, epart = meet([], up1, dn1, cpart, epart)
    st1, oa1, cg1, rim_dn, rim_up, vec1 = call(
        f1_kernel,
        c_arr,
        (mid1, up1, dn1, mk, v1, cpart, epart, cwo, cwx),
        [e_thin, each(RIM1, inner), each(RIM1, inner), e_masks, vspec, f_thin[1], f_thin[1], ANY, ANY],
        [taps, thin, thin, o_rim(RIM1), o_rim(RIM1), o_vec(3, inner)],
        [
            pltpu.VMEM((TAPS, inner, inner), BF16),
            pltpu.VMEM((rows, inner), F32),
            pltpu.VMEM((3, 8, inner), F32),
            dma((1,)),
        ],
        2 * mm, 20_000_000,
    )

    upg = lax.ppermute(rim_up, "dp", ahead)
    dng = lax.ppermute(rim_dn, "dp", behind)

    rest = list(range(2, count.bit_length() - 1))
    big = Route([[0, *rest[:1], 1, *rest[1:]], [1, 0, *rest]], 1, sec, at, count)
    small_way = Route([[0, 1, *rest], [1, *rest[:1], 0, *rest[1:]]], 1, sec, at, count)
    unit = 16 * count
    terms = functools.partial(weight_terms, own=own, tile=inner, unit=unit)

    g1_terms = terms(tie(c_arr, rim_up, rim_dn), [(oa1, output_cotangent), (st1, cg1)])
    upg, dng, *g1_terms = meet([], upg, dng, *g1_terms)
    g1 = Chain(*g1_terms, big)
    g1.go()
    def mid_scratch(ext):
        return [
            pltpu.VMEM((inner, TAPS * inner), BF16),
            *ext,
            pltpu.VMEM((rows, TAPS * inner), BF16),
            pltpu.VMEM((rows, inner), F32),
            pltpu.VMEM((3, 8, inner), F32),
            dma((TAPS,)),
        ]

    def first(c, block, ng, v, grad, grad_spec, slx, src, src_spec, mux, rsx):
        return call(
            functools.partial(first_kernel, block=block),
            c,
            (ng, v, grad, slx, src, mux, rsx, nwo, nwx),
            [e_thin, vspec, grad_spec, e_wide, src_spec, e_one, e_one, ANY, ANY],
            [wide, o_vec(2, width)],
            [pltpu.VMEM((width, inner), BF16), pltpu.VMEM((rows, width), F32), pltpu.VMEM((2, 8, width), F32), dma((1,))],
            1.3 * mm, 10_000_000,
        )

    ng1, vecm1 = call(
        functools.partial(mid_kernel, far=True, block=1),
        c_arr,
        (cg1, upg, dng, mk, v1, sln1, nn1, rsn1, cwo, cwx),
        [e_thin, each(RIM1, inner), each(RIM1, inner), e_masks, vspec, e_thin, e_thin, e_one, ANY, ANY],
        [thin, o_vec(3, inner)],
        mid_scratch([]),
        2.6 * mm, 10_000_000,
    )
    ng1 = meet([g1], ng1)
    c_n1 = tie(c_arr, *g1.ready())
    g1.go()
    ig1, cg0, rim_dn0, rim_up0, vecf1, vecl0 = call(
        joint_kernel,
        c_n1,
        (ng1, v1, output_cotangent, slx1, out0, mux1, rsx1, v0, slc0, nc0, rsc0, nwo, nwx, wwo, wwx),
        [e_thin, vspec, mine(rows, width), e_wide, e_wide, e_one, e_one, vspec, e_thin, e_thin, e_one] + [ANY] * 4,
        [wide, thin, o_rim(RIM0), o_rim(RIM0), o_vec(2, width), o_vec(4, width)],
        [
            pltpu.VMEM((width, inner), BF16),
            pltpu.VMEM((inner, width), BF16),
            pltpu.VMEM((rows, width), F32),
            pltpu.VMEM((rows, inner), F32),
            pltpu.VMEM((2, 8, width), F32),
            pltpu.VMEM((4, 8, width), F32),
            dma((2,)),
        ],
        2.6 * mm, 18_000_000,
    )
    cg0, rim_dn0, rim_up0 = meet([g1], cg0, rim_dn0, rim_up0)
    up0, dn0 = lax.ppermute(rim_up0, "dp", ahead), lax.ppermute(rim_dn0, "dp", behind)
    g3_terms = terms(tie(c_arr, *g1.ready(), rim_up0, rim_dn0), [(oa0, ig1), (st0, cg0)])
    g1.go()
    up0, dn0, *g3_terms = meet([g1], up0, dn0, *g3_terms)
    rim0 = jnp.concatenate([up0, dn0], axis=1)
    g3 = Chain(*g3_terms, big)
    g3.go()
    g1.ready()
    g1.go()

    head = jnp.pad(head_weight, ((0, 0), (0, LANES - vocab)))
    out1, tot = call(
        functools.partial(o1_kernel, vocab=vocab),
        tie(c_arr, g3.keep, *g1.send),
        (out0, oa1, residue_types, loss_mask, v1, head, wwo, wwx),
        [e_wide, e_thin, id_spec, id_spec, vspec, whole(width, LANES), ANY, ANY],
        [wide, o_vec(2, LANES)],
        [
            pltpu.VMEM((inner, width), BF16),
            pltpu.VMEM((rows, width), F32),
            pltpu.VMEM((rows, LANES), F32),
            pltpu.VMEM((2, 8, LANES), F32),
            dma((1,)),
        ],
        1.2 * mm, 8_000_000,
    )

    def handed(in0, in1):
        return jnp.where(low, in0, in1), swapped(jnp.where(low, in1, in0))

    def gathered(keep, come):
        return jnp.concatenate([jnp.where(low, keep, come), jnp.where(low, come, keep)], axis=0)[None]

    held_out = handed(out0, out1)
    tot = meet([g1, g3], tot)
    g1.ready()
    ng0, vecm0 = call(
        functools.partial(mid_kernel, far=False, block=0),
        tie(c_arr, *g3.ready(), *g1.send),
        (cg0, rim0, mk, v0, sln0, nn0, rsn0, cwo, cwx),
        [e_thin, each(2 * RIM0, inner), e_masks, vspec, e_thin, e_thin, e_one, ANY, ANY],
        [thin, o_vec(3, inner)],
        mid_scratch([pltpu.VMEM((rows + 2 * RIM0, inner), F32)]),
        2.6 * mm, 10_000_000,
    )
    g1.go()
    g3.go()
    ng0 = meet([g1], ng0)
    g4_terms = terms(tie(c_arr, *g1.ready()), [(act1, ng1), (act0, ng0)])
    g1.go()
    g4_terms = meet([g1, g3], *g4_terms)
    g4 = Chain(*g4_terms, small_way)
    g4.go()
    ig0, vecf0 = first(
        tie(c_arr, *g1.ready(), *g3.ready()), 0, ng0, v0, ig1, e_wide, slx0, block_input, mine(rows, width), mux0, rsx0
    )
    g1.go()
    g3.go()
    ig0, vecf0 = meet([g1, g3, g4], ig0, vecf0)

    smalls = (vec1, vece1, vecm1, vecf1, vecl0, vecm0, vecf0, tot)
    height = -(-sum(v.shape[0] for v in smalls) // 8) * 8
    small = pl.pallas_call(stack_kernel, out_shape=jax.ShapeDtypeStruct((height, width), F32))(*smalls)
    come = swapped(small)
    block_outputs, input_grads = gathered(*held_out), gathered(*handed(ig0, ig1))
    small = small + come
    for pairs, _ in big.steps:
        small = small + hop(small, pairs)
    s1, sm1, sf1, sl0, sm0, sf0, st = jnp.split(small, [4, 7, 9, 13, 16, 18], axis=0)
    type_total, loss_total = st[0, :vocab], st[1, :vocab]

    half = inner // 2
    cols = width // inner
    parts, sets, base = [], [], 0
    for core, chain, sem, step in ((1, g1, 0, 0), (0, g3, 0, 0), (None, g4, 1, TAPS + cols)):
        pieces = chain.finish()
        sets.append((core, list(range(len(parts), len(parts) + len(pieces))), sem * base, sem, step))
        base = (base if sem else 0) + sum(p.shape[0] for p in pieces) // 2
        parts += pieces
    top = sets[2][2]
    wide_rows = jnp.arange(cols + TAPS, dtype=jnp.int32) * half
    narrow_rows = (jnp.arange(cols, dtype=jnp.int32) + jnp.where(low, cols, 0).astype(jnp.int32)) * half + top
    widen_grad, conv_grad, narrow_grad = pl.pallas_call(
        functools.partial(unpack_kernel, sets=sets, shards=big.shards, outs=[0, cols, cols + TAPS]),
        grid_spec=pltpu.PrefetchScalarGridSpec(
            num_scalar_prefetch=3,
            grid=(2 * cols + TAPS,),
            in_specs=[ANY] * len(parts),
            out_specs=[
                pl.BlockSpec((inner, inner), lambda s, *_: (0, jnp.minimum(s, cols - 1))),
                pl.BlockSpec((1, inner, inner), lambda s, *_: (jnp.clip(s - cols, 0, TAPS - 1), 0, 0)),
                pl.BlockSpec((inner, inner), lambda s, *_: (jnp.maximum(s - cols - TAPS, 0), 0)),
            ],
            scratch_shapes=[pltpu.VMEM((2, base, inner), BF16), dma((2,))],
        ),
        out_shape=[
            jax.ShapeDtypeStruct((inner, width), F32),
            jax.ShapeDtypeStruct((TAPS, inner, inner), F32),
            jax.ShapeDtypeStruct((width, inner), F32),
        ],
        compiler_params=pltpu.CompilerParams(vmem_limit_bytes=VMEM_LIMIT),
        cost_estimate=pl.CostEstimate(flops=0, bytes_accessed=500_000, transcendentals=0),
    )(tie(c_arr, block_outputs, input_grads), jnp.concatenate([wide_rows, narrow_rows]), jnp.concatenate([big.signs, small_way.signs]), *parts)

    def sel(in0, in1, n=width):
        return jnp.where(low, in0, in1)[None, :n]

    return (
        block_outputs,
        input_grads,
        sel(sf0[0], sf1[0]),
        sel(sf0[1], sf1[1]),
        narrow_grad[None],
        sel(sm0[2], sm1[2], inner),
        sel(sm0[0], sm1[0], inner),
        sel(sm0[1], sm1[1], inner),
        conv_grad[None],
        sel(sl0[2], s1[2], inner),
        sel(sl0[0], s1[0], inner),
        sel(sl0[1], s1[1], inner),
        widen_grad[None],
        sel(sl0[3], s1[3]),
        type_total.astype(jnp.int32),
        loss_total / jnp.maximum(type_total, 1.0),
    )


def solution(mesh):
    rows = P(None, "dp", None)
    ids = P(None, "dp")
    vec = P("section", None)
    mat = P("section", None, None)
    conv = P("section", None, None, None)
    weights = (vec, vec, mat, vec, vec, vec, conv, vec, vec, vec, mat, vec)
    grads = P("section", None, "dp", None)
    return jax.shard_map(
        body,
        mesh=mesh,
        in_specs=(rows, rows, ids, ids, ids, ids, *weights, P()),
        out_specs=(grads, grads, *weights, P(), P()),
        check_vma=False,
    )
```
